32 devices in a mesh: dp: 4 (over x, core), wide: 8 (over z, y).
Axes of the slice: x: 2, y: 2, z: 4, core: 2. Of those that a mesh axis runs over, the one named last changes fastest.
Arguments:
- inputs: bfloat16 [32, 256, 2048], P(('dp', 'wide')), may hold values from -6 to 6
- cotangent: bfloat16 [32, 256, 2048], P(('dp', 'wide')), may hold values from -6 to 6
- keep_mask: int32 [32], P(('dp', 'wide')), may hold values 0 or 1
- positions: int32 [32, 256], P(('dp', 'wide')), may hold values from 0 to 510, as said below
- master_weights: float32 [172, 262144], P(None, ('dp', 'wide'))
- gains: float32 [2, 2048], replicated, may hold values from 0.5 to 1.5
- gain_moments: float32 [2, 2048], replicated, may hold values from 40.96 to 163.84
- block_slot: int32 [172], replicated, may hold values from 0 to 191, as said below
- stat_left: float32 [192, 512, 512], P(('dp', 'wide')), as said below
- stat_right: float32 [192, 512, 512], P(('dp', 'wide')), as said below
- root_left: float32 [192, 512, 512], P(('dp', 'wide')), as said below
- root_right: float32 [192, 512, 512], P(('dp', 'wide')), as said below
Outputs:
- output: bfloat16 [32, 256, 2048], P(('dp', 'wide'))
- input_grad: bfloat16 [32, 256, 2048], P(('dp', 'wide'))
- weight_grads: float32 [172, 262144], P(None, ('dp', 'wide'))
- new_left: float32 [192, 512, 512], P(('dp', 'wide'))
- new_right: float32 [192, 512, 512], P(('dp', 'wide'))
- new_weights: float32 [172, 262144], P(None, ('dp', 'wide'))
- gain_grads: float32 [2, 2048], replicated
- new_gain_moments: float32 [2, 2048], replicated
- new_gains: float32 [2, 2048], replicated
The draws below stay inside these ranges and needn't reach their ends.
Inputs may be any that keep to these rules, and one draw needn't show every extreme that they name: `block_slot`: distinct slots, one for each block; slots 0 and 191 always own a block. Each sequence's positions start at 0, rise by at least 1 from one token to the next (mostly by 1 or 2), and its last token is at 510. `stat_left`: symmetric positive definite. `stat_right`: symmetric positive definite. `root_left`: symmetric. `root_right`: symmetric.
All inputs are finite; a program needn't handle non-finite values. No bound on the sum of `keep_mask` on one device may be relied on, other than what follows from the above.
Results may differ from the reference program's by a relative error of at most 0.017.
Values may be sent and summed in bfloat16 or wider, within the bound.
A program may use at most 512 MiB of HBM per device.

```python
import math
import jax
import jax.numpy as jnp
from jax import lax

D = 2048
HEADS = 16
HD = 128
KVH = 4
FF = 5632
B = 512
SEQ = 256
LAYER = 16
DEPTH = 24
STEP = 10
RAMP = 20
NSEQ = 32
TOKENS = 8192
NBLK = 172
SLOTS = 192


def init_scale(block_index):
    rows_model = D // B
    rows_kv = KVH * HD // B
    rows_ff = FF // B
    bound_value = rows_model * rows_model + 2 * rows_model * rows_kv
    bound_out = bound_value + rows_model * rows_model
    bound_up = bound_out + 2 * rows_model * rows_ff
    drawn_scale = D ** (-0.5)
    out_scale = (SEQ / 8.0) ** 0.5 * D ** (-0.5)
    return jnp.where(block_index < bound_value, drawn_scale, jnp.where(block_index < bound_out, out_scale, jnp.where(block_index < bound_up, drawn_scale, FF ** (-0.5))))


def symmetric_draw(key, low_end, high_end, spread):
    first_key, second_key = jax.random.split(key)
    diagonal_values = jax.random.uniform(first_key, (SLOTS, B), jnp.float32, low_end, high_end)
    noise = jax.random.truncated_normal(second_key, -3.0, 3.0, (SLOTS, B, B), jnp.float32) * spread
    paired = (noise + jnp.swapaxes(noise, 1, 2)) * 0.70710678
    diagonal_mask = jnp.arange(B)[:, None] == jnp.arange(B)[None, :]
    return jnp.where(diagonal_mask[None, :, :], diagonal_values[:, :, None], paired)


def draw_positions(key, part):
    key = jax.random.fold_in(key, 12)
    spacing = jax.random.randint(key, (NSEQ, SEQ - 1), 1, 3)
    rising = (jnp.cumsum(spacing, axis=1) - spacing[:, :1]).astype(jnp.int32)
    last_column = jnp.full((NSEQ, 1), 2 * SEQ - 2, jnp.int32)
    return jnp.concatenate([rising, last_column], 1).astype(jnp.int32)


def draw_master_weights(key, part):
    key = jax.random.fold_in(key, 11)
    noise = jax.random.truncated_normal(key, -4.0, 4.0, (NBLK, B * B), jnp.float32)
    return noise * init_scale(jnp.arange(NBLK))[:, None].astype(jnp.float32)


def draw_block_slot(key, part):
    key = jax.random.fold_in(key, 13)
    first_key, second_key = jax.random.split(key)
    middle_slots = jax.random.permutation(first_key, SLOTS - 2)[:NBLK - 2] + 1
    chosen = jnp.concatenate([jnp.array([0, SLOTS - 1], jnp.int32), middle_slots.astype(jnp.int32)])
    return jax.random.permutation(second_key, chosen).astype(jnp.int32)


def draw_stat_left(key, part):
    key = jax.random.fold_in(key, 21)
    return symmetric_draw(key, 0.005 * B * TOKENS, 0.02 * B * TOKENS, 0.002 * TOKENS)


def draw_stat_right(key, part):
    key = jax.random.fold_in(key, 22)
    return symmetric_draw(key, 0.005 * B * TOKENS, 0.02 * B * TOKENS, 0.002 * TOKENS)


def draw_root_left(key, part):
    key = jax.random.fold_in(key, 23)
    return symmetric_draw(key, 1.0, 2.0, 0.5 * B ** (-0.5))


def draw_root_right(key, part):
    key = jax.random.fold_in(key, 24)
    return symmetric_draw(key, 1.0, 2.0, 0.5 * B ** (-0.5))


def set_ends(drawn, own_key, low, largest):
    dims = drawn.shape
    place = [jax.random.randint(jax.random.fold_in(own_key, axis), (), 0, dims[axis]) for axis in range(len(dims))]
    drawn = drawn.at[tuple(place)].set(low)
    longest = dims.index(max(dims))
    place[longest] = (place[longest] + 1) % dims[longest]
    return drawn.at[tuple(place)].set(largest)


def steps_of(stream_key, shape, cuts, low, top_value):
    level = 1.0
    for dim, parts in cuts:
        draws = jax.random.uniform(jax.random.fold_in(jax.random.fold_in(stream_key, 6), dim), (parts,), jnp.float32, low / len(cuts), top_value / len(cuts))
        level = level * jnp.repeat(jnp.exp(draws), shape[dim] // parts).reshape((-1,) + (1,) * (len(shape) - 1 - dim))
    return level


def bell_draw(key, dims, deviation, reach, shards=(), kind=jnp.bfloat16):
    values = jax.random.normal(key, dims, jnp.float32) * deviation
    if len(shards) > 0:
        values = steps_of(key, dims, shards, -0.22, 0.18) * values
    return jnp.clip(values, min=-reach, max=reach).astype(kind)


def setup_inputs(seed: int = 0) -> dict:
    key_list = jax.random.split(jax.random.key(seed), 13)
    return {
        "inputs": bell_draw(key_list[0], (NSEQ, SEQ, D), 1.0, 6.0, ((0, 32),)),
        "cotangent": bell_draw(key_list[1], (NSEQ, SEQ, D), 1.0, 6.0, ((0, 32),)),
        "keep_mask": set_ends((jax.random.randint(key_list[2], (NSEQ,), 0, 4) < 3).astype(jnp.int32), jax.random.fold_in(key_list[2], 1), 0, 1),
        "positions": draw_positions(jax.random.fold_in(key_list[12], 71), 0),
        "master_weights": draw_master_weights(jax.random.fold_in(key_list[12], 71), 0),
        "gains": jnp.clip(1.0 + 0.1 * jax.random.normal(key_list[5], (2, D), jnp.float32), 0.5, 1.5),
        "gain_moments": jnp.clip(jnp.exp(jax.random.uniform(key_list[6], (2, D), jnp.float32, math.log(40.96), math.log(163.84))), 40.96, 163.84),
        "block_slot": draw_block_slot(jax.random.fold_in(key_list[12], 71), 0),
        "stat_left": draw_stat_left(jax.random.fold_in(key_list[12], 71), 0),
        "stat_right": draw_stat_right(jax.random.fold_in(key_list[12], 71), 0),
        "root_left": draw_root_left(jax.random.fold_in(key_list[12], 71), 0),
        "root_right": draw_root_right(jax.random.fold_in(key_list[12], 71), 0),
    }


norm_eps = 1e-05
stat_decay = 0.95
weight_rate = 0.5
weight_decay = 0.001
gain_rate = 0.05
adam_eps = 1e-08
rope_base = 10000.0
scale_eps = 1e-06
masked_value = -1e+30

@jax.custom_vjp
def low(v):
    return lax.optimization_barrier(v.astype(jnp.bfloat16)).astype(jnp.float32)

@jax.custom_vjp
def low_back(v):
    return v

def low_keep(v):
    return (low(v), None)

def low_pass(kept, grad):
    return (grad,)

def back_keep(v):
    return (v, None)

def back_low(kept, grad):
    return (low(grad),)
low.defvjp(low_keep, low_pass)
low_back.defvjp(back_keep, back_low)

def keep_rate():
    return 1.0 - 0.2 * (2.0 ** (LAYER / (DEPTH - 1)) - 1.0) * min(STEP / RAMP, 1.0)

def block_shapes():
    rows_model = D // B
    rows_kv = KVH * HD // B
    rows_ff = FF // B
    return [(rows_model, rows_model), (rows_model, rows_kv), (rows_model, rows_kv), (rows_model, rows_model), (rows_model, rows_ff), (rows_model, rows_ff), (rows_ff, rows_model)]

def block_scale(block_index):
    bounds = []
    running = 0
    for row_blocks, col_blocks in block_shapes():
        running = running + row_blocks * col_blocks
        bounds.append(running)
    plain_scale = D ** (-0.5)
    out_scale = (SEQ / 8.0) ** 0.5 * D ** (-0.5)
    return jnp.where(block_index < bounds[2], plain_scale, jnp.where(block_index < bounds[3], out_scale, jnp.where(block_index < bounds[5], plain_scale, FF ** (-0.5)))).astype(jnp.float32)

def unpack_blocks(blocks, row_blocks, col_blocks):
    return blocks.reshape(row_blocks, col_blocks, B, B).transpose(0, 2, 1, 3).reshape(row_blocks * B, col_blocks * B)

def rope_tables(position):
    half_dim = HD // 2
    freqs = rope_base ** (-(jnp.arange(half_dim).astype(jnp.float32) * 2.0 / HD))
    angles = position.astype(jnp.float32)[:, None] * freqs[None, :]
    cosine_table = jnp.concatenate([jnp.cos(angles), jnp.cos(angles)], -1)
    sine_table = jnp.concatenate([jnp.sin(angles), jnp.sin(angles)], -1)
    return (cosine_table, sine_table)

def rotate(values, cosine_table, sine_table):
    half_dim = HD // 2
    turned = jnp.concatenate([-values[..., half_dim:], values[..., :half_dim]], -1)
    return values * cosine_table[:, None, :] + turned * sine_table[:, None, :]

def highest(left, right):
    return jnp.dot(left, right, precision=lax.Precision.HIGHEST)

def rms_norm(values, gain):
    return values * lax.rsqrt(lax.optimization_barrier(jnp.mean(values * values, -1, keepdims=True)) + norm_eps) * gain

def sequence_forward(matrices, gain_pair, residual, position, branch_scale):
    w_query, w_key, w_value, w_out, w_gate, w_up, w_down = matrices
    seq_len = residual.shape[0]
    group_size = HEADS // KVH
    cosine_table, sine_table = rope_tables(position)
    normed_one = low(rms_norm(residual, gain_pair[0]))
    query_rows = low(rotate(low_back(highest(normed_one, w_query)).reshape(seq_len, HEADS, HD), cosine_table, sine_table))
    key_rows = low(rotate(low_back(highest(normed_one, w_key)).reshape(seq_len, KVH, HD), cosine_table, sine_table))
    value_rows = low(low_back(highest(normed_one, w_value))).reshape(seq_len, KVH, HD)
    grouped = query_rows.reshape(seq_len, KVH, group_size, HD)
    scores = jnp.einsum('skgd,tkd->kgst', grouped, key_rows, precision=lax.Precision.HIGHEST) * HD ** (-0.5)
    scores = low_back(scores)
    causal = jnp.arange(seq_len)[:, None] >= jnp.arange(seq_len)[None, :]
    scores = jnp.where(causal, scores, masked_value)
    row_top = lax.optimization_barrier(jnp.max(scores, -1, keepdims=True))
    exp_scores = jnp.exp(scores - row_top)
    attn_probs = low(exp_scores / lax.optimization_barrier(jnp.sum(exp_scores, -1, keepdims=True)))
    attn_out = jnp.einsum('kgst,tkd->skgd', attn_probs, value_rows, precision=lax.Precision.HIGHEST).reshape(seq_len, D)
    attn_proj = low_back(highest(low(low_back(attn_out)), w_out))
    middle = residual + branch_scale * attn_proj
    normed_two = low(rms_norm(middle, gain_pair[1]))
    gate_rows = low_back(highest(normed_two, w_gate))
    up_rows = low_back(highest(normed_two, w_up))
    hidden = low(gate_rows * jax.nn.sigmoid(gate_rows) * up_rows)
    mlp_proj = low_back(highest(hidden, w_down))
    return middle + branch_scale * mlp_proj

def reference(inputs, cotangent, keep_mask, positions, master_weights, gains, gain_moments, block_slot, stat_left, stat_right, root_left, root_right):
    shapes = block_shapes()
    scales = keep_mask.astype(jnp.float32) / keep_rate()

    def whole_forward(masters, gain_pair, residuals):
        matrices = []
        first_row = 0
        for row_blocks, col_blocks in shapes:
            row_count = row_blocks * col_blocks
            matrices.append(low(unpack_blocks(masters[first_row:first_row + row_count], row_blocks, col_blocks)))
            first_row = first_row + row_count

        def one_sequence(items):
            return sequence_forward(matrices, gain_pair, items[0], items[1], items[2])
        return lax.map(jax.checkpoint(one_sequence), (residuals, positions, scales))
    result, pullback = jax.vjp(whole_forward, master_weights, gains, inputs.astype(jnp.float32))
    master_grad, gain_grad, input_grad = pullback(cotangent.astype(jnp.float32))
    slot_grads = jnp.zeros((SLOTS, B * B), jnp.float32).at[block_slot].set(master_grad).reshape(SLOTS, B, B)
    slot_block = jnp.full((SLOTS,), -1, jnp.int32).at[block_slot].set(jnp.arange(NBLK).astype(jnp.int32))
    slot_scale = jnp.where(slot_block >= 0, block_scale(jnp.maximum(slot_block, 0)), 0.0)

    def refresh(items):
        grad_block, left, right, left_root, right_root, factor = items
        renewed_left = stat_decay * left + (1.0 - stat_decay) * highest(grad_block, grad_block.T)
        renewed_right = stat_decay * right + (1.0 - stat_decay) * highest(grad_block.T, grad_block)
        precond = highest(highest(left_root, grad_block), right_root)
        step = weight_rate * factor * precond * lax.rsqrt(jnp.mean(precond * precond) + scale_eps)
        return (renewed_left, renewed_right, step.reshape(B * B))
    new_left, new_right, slot_steps = lax.map(refresh, (slot_grads, stat_left, stat_right, root_left, root_right, slot_scale))
    new_weights = (1.0 - weight_decay) * master_weights - slot_steps[block_slot]
    new_moments = stat_decay * gain_moments + (1.0 - stat_decay) * gain_grad * gain_grad
    new_gains = gains - gain_rate * gain_grad / (jnp.sqrt(new_moments) + adam_eps)
    return (result.astype(jnp.bfloat16), input_grad.astype(jnp.bfloat16), master_grad, new_left, new_right, new_weights, gain_grad, new_moments, new_gains)
```

```python
import functools

import jax
import jax.numpy as jnp
from jax import lax
from jax.experimental import pallas as pl
from jax.experimental.pallas import tpu as pltpu
from jax.sharding import PartitionSpec as P

D = 2048
HEADS = 16
HD = 128
KVH = 4
FF = 5632
B = 512
SEQ = 256
LAYER = 16
DEPTH = 24
STEP = 10
RAMP = 20
NBLK = 172


norm_eps = 1e-05
stat_decay = 0.95
weight_rate = 0.5
weight_decay = 0.001
gain_rate = 0.05
adam_eps = 1e-08
rope_base = 10000.0
scale_eps = 1e-06
masked_value = -1e30


def keep_rate():
    return 1.0 - 0.2 * (2.0 ** (LAYER / (DEPTH - 1)) - 1.0) * min(STEP / RAMP, 1.0)


def block_shapes():
    rows_model = D // B
    rows_kv = KVH * HD // B
    rows_ff = FF // B
    return [
        (rows_model, rows_model),
        (rows_model, rows_kv),
        (rows_model, rows_kv),
        (rows_model, rows_model),
        (rows_model, rows_ff),
        (rows_model, rows_ff),
        (rows_ff, rows_model),
    ]


def block_scale(block_index):
    bounds = []
    running = 0
    for row_blocks, col_blocks in block_shapes():
        running = running + row_blocks * col_blocks
        bounds.append(running)
    plain_scale = D ** (-0.5)
    out_scale = (SEQ / 8.0) ** 0.5 * D ** (-0.5)
    return jnp.where(
        block_index < bounds[2],
        plain_scale,
        jnp.where(
            block_index < bounds[3],
            out_scale,
            jnp.where(block_index < bounds[5], plain_scale, FF ** (-0.5)),
        ),
    ).astype(jnp.float32)


def rope_tables(position):
    half_dim = HD // 2
    freqs = rope_base ** (-(jnp.arange(half_dim).astype(jnp.float32) * 2.0 / HD))
    angles = position.astype(jnp.float32)[:, None] * freqs[None, :]
    cosine_table = jnp.concatenate([jnp.cos(angles), jnp.cos(angles)], -1)
    sine_table = jnp.concatenate([jnp.sin(angles), jnp.sin(angles)], -1)
    return (cosine_table, sine_table)


def rotate(values, cosine_table, sine_table):
    half_dim = HD // 2
    turned = jnp.concatenate([-values[..., half_dim:], values[..., :half_dim]], -1)
    return values * cosine_table[:, None, :] + turned * sine_table[:, None, :]


def norm_rate(values):
    return lax.rsqrt(jnp.mean(values * values, -1, keepdims=True) + norm_eps)


def norm_backward(values, rate, gain, grads):
    scaled = grads * gain
    value_grad = rate * scaled - values * rate * rate * rate * jnp.mean(
        values * scaled, -1, keepdims=True
    )
    gain_grad = jnp.sum(grads * values * rate, 0)
    return (value_grad, gain_grad)


def dot(left, right):
    return jnp.dot(left, right, preferred_element_type=jnp.float32)


def dot_back(grads, matrix):
    return lax.dot_general(
        grads, matrix, (((1,), (1,)), ((), ())), preferred_element_type=jnp.float32
    )


def dot_grad(rows, grads):
    return lax.dot_general(
        rows, grads, (((0,), (0,)), ((), ())), preferred_element_type=jnp.float32
    )


def share(values):
    return lax.all_gather(values, "dp", axis=0, tiled=True)


def total(values):
    return lax.psum_scatter(
        values.astype(jnp.bfloat16), "dp", scatter_dimension=0, tiled=True
    ).astype(jnp.float32)


MESH = pl.DeviceIdType.MESH
ANY = pl.BlockSpec(memory_space=pl.ANY)


def flip(index, part):
    chip, core = index // 2, index % 2
    return (chip + part // 2) % 2 * 2 + (core + part % 2) % 2


def remote(source, target, sent, landed, **device):
    return pltpu.make_async_remote_copy(
        src_ref=source,
        dst_ref=target,
        send_sem=sent,
        recv_sem=landed,
        device_id=device,
        device_id_type=MESH,
    )


def greet(line, z, y, j, w):
    barrier = pltpu.get_barrier_semaphore()
    for part in range(1, 4):
        pl.semaphore_signal(barrier, device_id={"dp": flip(j, part)}, device_id_type=MESH)
    pl.semaphore_signal(barrier, device_id={"wide": w + 1 - 2 * y}, device_id_type=MESH)

    @pl.when(z > 0)
    def _():
        pl.semaphore_signal(barrier, device_id={"wide": w - 2}, device_id_type=MESH)

    @pl.when(z < line - 1)
    def _():
        pl.semaphore_signal(barrier, device_id={"wide": w + 2}, device_id_type=MESH)

    ends = jnp.where(z > 0, 1, 0) + jnp.where(z < line - 1, 1, 0)
    pl.semaphore_wait(barrier, 4 + ends)


def each(count, step):
    def body(index, carry):
        step(index)
        return carry

    lax.fori_loop(0, count, body, 0)


def gather_kernel(line, half, *refs):
    sent_in, (residual_ref, scale_ref, gain_ref) = refs[:6], refs[6:9]
    outs, (qkv_out, attn_out, middle_out, normed_out) = refs[9:13], refs[13:17]
    rows_out, tables_out = refs[17:19]
    rows_v, tables_v, wqkv_v, wout_v, qkv_v, attn_v, part_v, sum_v, normed_v = refs[19:28]
    loc, dp_send, dp_recv, up_sem, dn_sem, y_sem, recv, keep, sum_send, sum_recv, norm_send, norm_recv = refs[28:]
    qkv_s, out_s, ffn_s = sent_in[:3]
    qkv, out, ffn, low_out = outs
    row_to = (rows_v, low_out, tables_v)
    f32, low = jnp.float32, jnp.bfloat16
    j, w = lax.axis_index("dp"), lax.axis_index("wide")
    z, y = w // 2, w % 2
    other = w + 1 - 2 * y
    greet(line, z, y, j, w)

    def row_copy(part, place):
        there = row_to[place].at[flip(j, 2) if part == 3 else j]
        return remote(
            there if part == 3 else sent_in[3 + place],
            there,
            dp_send.at[3 + place, part],
            dp_recv.at[3 + place, part],
            dp=flip(j, 1 if part == 3 else part),
        )

    def hand_on(place):
        row_copy(2, place).wait_recv()
        row_copy(3, place).start()

    def weight_copy(part, place):
        peer = flip(j, part)
        target = (qkv.at[:, j, w], out.at[j, w], ffn.at[:, j, w])[place]
        return remote(
            sent_in[place].at[peer], target, dp_send.at[place, part], dp_recv.at[place, part], dp=peer
        )

    copies = [
        pltpu.make_async_copy(qkv_s.at[j], qkv.at[:, j, w], loc.at[0]),
        pltpu.make_async_copy(out_s.at[j], out.at[j, w], loc.at[1]),
        pltpu.make_async_copy(ffn_s.at[j], ffn.at[:, j, w], loc.at[2]),
    ] + [
        pltpu.make_async_copy(sent_in[3 + place], row_to[place].at[j], loc.at[3 + place])
        for place in range(3)
    ]
    for copy in copies:
        copy.start()
    for place in range(2):
        for part in range(1, 4):
            weight_copy(part, place).start()

    chunks = []
    for part in range(4):
        chunks += [("qkv", part, 0), ("out", part, 0)]
        if part == 0:
            chunks += [("ffn", 0, 0)]
    chunks += [("ffn", 0, 1)]
    for part in range(1, 4):
        chunks += [("ffn", part, 0), ("ffn", part, 1)]
    count = len(chunks)

    def crosses_first(at):
        name, part, _ = chunks[at]
        return name == "ffn" and part == 0

    def view(at, origin):
        name, part, side = chunks[at]
        if name == "qkv":
            return qkv.at[:, flip(j, part), origin]
        if name == "out":
            return out.at[flip(j, part), origin]
        return ffn.at[:, flip(j, part), origin, :, side * half : (side + 1) * half]

    def up(at, origin):
        there = view(at, origin)
        return remote(there, there, up_sem.at[at, origin], recv.at[at, origin], wide=w + 2)

    def dn(at, origin):
        there = view(at, origin)
        return remote(there, there, dn_sem.at[at, origin], recv.at[at, origin], wide=w - 2)

    def across(at, origin):
        there = view(at, origin)
        return remote(there, there, y_sem.at[at, origin], recv.at[at, origin], wide=other)

    def arrived(at, origin):
        across(at, origin).wait_recv()

    start = lambda copy: copy.start()
    finish = lambda copy: copy.wait_send()

    def both_ways(at, origin, act):
        @pl.when(z < line - 1)
        def _():
            act(up(at, origin))

        @pl.when(z > 0)
        def _():
            act(dn(at, origin))

    waited = []

    def own(at):
        name, part, side = chunks[at]
        place = ("qkv", "out", "ffn").index(name)
        if (place, part) not in waited:
            waited.append((place, part))
            if part == 0:
                copies[place].wait()
            else:
                weight_copy(part, place).wait_recv()
        across(at, w).start()
        both_ways(at, w, start)

    def turn(at):
        arrived(at, other)
        both_ways(at, other, start)

    def pass_on(at, far, act, waiting):
        first = crosses_first(at)
        for side in (0, 1) if first else (0,):
            column = y if side == 0 else 1 - y

            @pl.when(z >= far)
            def _():
                origin = (z - far) * 2 + column
                if waiting:
                    arrived(at, origin)

                @pl.when(z < line - 1)
                def _():
                    act(up(at, origin))

                if not first:
                    act(across(at, origin))

            @pl.when(z + far < line)
            def _():
                origin = (z + far) * 2 + column
                if waiting:
                    arrived(at, origin)

                @pl.when(z > 0)
                def _():
                    act(dn(at, origin))

                if not first:
                    act(across(at, origin))

    heads = attn_v.shape[2] // HD
    seq = rows_v.shape[1]
    turns = (3, 2, 1, 0)
    attn_chunks = [at for at in range(count) if chunks[at][0] in ("qkv", "out")]
    loads = [
        pltpu.make_async_copy(qkv, wqkv_v, keep.at[0]),
        pltpu.make_async_copy(out, wout_v, keep.at[1]),
    ]

    def weights_ready():
        for at in attn_chunks:
            for far in range(line):
                arrived(at, far * 2 + 1 - y)
        for load in loads:
            load.start()
        for part in (1, 3):
            row_copy(part, 0).wait_recv()
            row_copy(part, 2).wait_recv()
        copies[3].wait()
        copies[5].wait()
        for load in loads:
            load.wait()

    def project(part):
        n = flip(j, part)
        cosine, sine = tables_v[n, 0], tables_v[n, 1]
        weights = wqkv_v[...].reshape(D, wqkv_v.shape[4])
        value = jnp.dot(rows_v[n], weights, preferred_element_type=f32)
        for head in range(heads + 1):
            one = value[:, head * HD : (head + 1) * HD]
            turned = one * cosine + pltpu.roll(one, HD // 2, 1) * sine
            qkv_v[part, :, head * HD : (head + 1) * HD] = turned.astype(low)
        qkv_v[part, :, (heads + 1) * HD :] = value[:, (heads + 1) * HD :].astype(low)

    def attend(part, head):
        query = qkv_v[part, :, head * HD : (head + 1) * HD]
        key = qkv_v[part, :, heads * HD : (heads + 1) * HD]
        scores = lax.dot_general(
            query, key, (((1,), (1,)), ((), ())), preferred_element_type=f32
        ) * HD ** (-0.5)
        row = lax.broadcasted_iota(jnp.int32, (seq, seq), 0)
        column = lax.broadcasted_iota(jnp.int32, (seq, seq), 1)
        scores = jnp.where(row >= column, scores, masked_value)
        weight = jnp.exp(scores - jnp.max(scores, -1, keepdims=True))
        probs = (weight / jnp.sum(weight, -1, keepdims=True)).astype(low)
        value = jnp.dot(probs, qkv_v[part, :, (heads + 1) * HD :], preferred_element_type=f32)
        attn_v[part, :, head * HD : (head + 1) * HD] = value.astype(low)

    def send_sum(part):
        peer = flip(j, 1 if part == 3 else part)
        return remote(
            part_v.at[part], sum_v.at[part], sum_send.at[part], sum_recv.at[part], dp=peer
        )

    def finished(part):
        n = flip(j, part)
        return [
            pltpu.make_async_copy(qkv_v.at[part], qkv_out.at[n], keep.at[2 + part]),
            pltpu.make_async_copy(attn_v.at[part], attn_out.at[n], keep.at[6 + part]),
        ]

    def project_out(part):
        weights = wout_v[...].reshape(heads * HD, D)
        if part == 2:
            send_sum(3).wait_recv()
        for cut in range(4):
            columns = slice(cut * D // 4, (cut + 1) * D // 4)
            value = jnp.dot(attn_v[part], weights[:, columns], preferred_element_type=f32)
            if part == 2:
                value = value + sum_v[3, :, columns].astype(f32)
            part_v[part, :, columns] = value.astype(low)
        if part > 0:
            send_sum(part).start()
        for copy in finished(part):
            copy.start()

    def send_normed(part):
        there = normed_out.at[flip(j, 2) if part == 3 else j]
        return remote(
            there if part == 3 else normed_v,
            there,
            norm_send.at[part],
            norm_recv.at[part],
            dp=flip(j, 1 if part == 3 else part),
        )

    keep_normed = pltpu.make_async_copy(normed_v, normed_out.at[j], keep.at[10])
    keep_rows = pltpu.make_async_copy(rows_v, rows_out, keep.at[11])
    keep_tables = pltpu.make_async_copy(tables_v, tables_out, keep.at[12])

    def normalize():
        for part in (1, 2):
            send_sum(part).wait_recv()
        scale = scale_ref[0, 0]

        def rows(index):
            here = pl.ds(pl.multiple_of(index * 32, 32), 32)
            total_rows = part_v[0, here, :].astype(f32)
            for part in (1, 2):
                total_rows = total_rows + sum_v[part, here, :].astype(f32)
            middle = residual_ref[here, :].astype(f32) + scale * total_rows
            middle_out[here, :] = middle
            rate = lax.rsqrt(jnp.mean(middle * middle, -1, keepdims=True) + norm_eps)
            normed_v[here, :] = (middle * rate * gain_ref[...]).astype(low)

        each(seq // 32, rows)
        for part in (1, 2):
            send_normed(part).start()
        keep_normed.start()
        keep_rows.start()
        keep_tables.start()

    work = [weights_ready]
    for part in turns:
        work.append(functools.partial(project, part))
        for head in range(heads):
            work.append(functools.partial(attend, part, head))
        work.append(functools.partial(project_out, part))
    work.append(normalize)
    ready = attn_chunks[-1] + line + 1

    def compute(pieces):
        for _ in range(pieces):
            if work:
                work.pop(0)()

    for step in range(count + line):
        if step < count:
            own(step)
        for far in range(1, line):
            at = step - far - 1
            if 0 <= at < count:
                if far == 1 and crosses_first(at):
                    turn(at)
                pass_on(at, far, start, True)
                if step >= ready:
                    compute(2)
        if step == 2:
            for part in range(1, 4):
                weight_copy(part, 2).start()
        if step == attn_chunks[-1]:
            for part in (1, 2):
                row_copy(part, 0).start()
                row_copy(part, 2).start()
        if step == attn_chunks[-1] + 2:
            for part in (1, 2):
                row_copy(part, 1).start()
        if step == ready - 1:
            hand_on(0)
            hand_on(2)
        if step >= ready:
            compute(2)
        if step == count + 1:
            hand_on(1)
    compute(len(work))
    send_normed(2).wait_recv()
    send_normed(3).start()

    for at in range(count):
        if not crosses_first(at) and at not in attn_chunks:
            for far in range(line):
                arrived(at, far * 2 + 1 - y)
    copies[4].wait()
    for place in range(3):
        for part in range(1, 4):
            if place == 1 and part != 2:
                row_copy(part, place).wait()
            else:
                row_copy(part, place).wait_send()
            weight_copy(part, place).wait_send()
    for at in range(count):
        across(at, w).wait_send()
        both_ways(at, w, finish)
        if crosses_first(at):
            both_ways(at, other, finish)
        for far in range(1, line):
            pass_on(at, far, finish, False)
    for part in range(4):
        for copy in finished(part):
            copy.wait()
        if part > 0:
            send_sum(part).wait_send()
            send_normed(part).wait_send()
        if part in (1, 3):
            send_normed(part).wait_recv()
    keep_normed.wait()
    keep_rows.wait()
    keep_tables.wait()


def gather_call(line, qkv_s, out_s, ffn_s, rows, low_rows, tables, residual, scale, gain):
    low = jnp.bfloat16
    ndp, wide = qkv_s.shape[0], 2 * line
    rm, piece = qkv_s.shape[1], qkv_s.shape[2]
    seq, wq = rows.shape[0], D // ndp

    def shape(*dims, kind=low):
        return jax.ShapeDtypeStruct(dims, kind)

    outs = (
        shape(rm, ndp, wide, piece, qkv_s.shape[3]),
        shape(ndp, wide, piece, out_s.shape[2]),
        shape(rm, ndp, wide, piece, ffn_s.shape[3]),
        shape(ndp, seq, D),
        shape(ndp, seq, qkv_s.shape[3]),
        shape(ndp, seq, wq),
        shape(seq, D, kind=jnp.float32),
        shape(ndp, seq, D),
        shape(ndp, seq, D),
        shape(ndp, *tables.shape, kind=tables.dtype),
    )
    dma = pltpu.SemaphoreType.DMA
    whole = pl.BlockSpec(memory_space=pltpu.VMEM)
    args = (qkv_s, out_s, ffn_s, rows, low_rows, tables)
    count = 16
    return pl.pallas_call(
        functools.partial(gather_kernel, line, ffn_s.shape[3] // 2),
        out_shape=outs,
        in_specs=[ANY] * len(args) + [whole, pl.BlockSpec(memory_space=pltpu.SMEM), whole],
        out_specs=[ANY] * 6 + [whole] + [ANY] * 3,
        scratch_shapes=[
            pltpu.VMEM((ndp, seq, D), low),
            pltpu.VMEM((ndp, *tables.shape), tables.dtype),
            pltpu.VMEM(outs[0].shape, low),
            pltpu.VMEM(outs[1].shape, low),
            pltpu.VMEM((ndp, seq, qkv_s.shape[3]), low),
            pltpu.VMEM((ndp, seq, wq), low),
            pltpu.VMEM((ndp, seq, D), low),
            pltpu.VMEM((ndp, seq, D), low),
            pltpu.VMEM((seq, D), low),
            dma((7,)),
            dma((6, 4)),
            dma((6, 4)),
        ]
        + [dma((count, wide))] * 4
        + [dma((13,)), dma((4,)), dma((4,)), dma((4,)), dma((4,))],
        compiler_params=pltpu.CompilerParams(
            collective_id=0, has_side_effects=True, vmem_limit_bytes=56 * 1024 * 1024
        ),
        name="gather_weights",
    )(*args, residual, scale, gain)


def scatter_kernel(line, half, *refs):
    (grad_ffn, normed_part, middle_in, cotangent, residual, w_out, w_qkv) = refs[:7]
    packed_in, attn_in, rows_in, tables_in, scale_ref, gains_ref = refs[7:13]
    outs, (input_grad, gain_parts) = refs[13:16], refs[16:18]
    crossed, lined, mine_ffn = refs[18:21], refs[21:24], refs[24]
    early, early_line, early_cross = refs[25:28]
    middle_v, late_v, sum_v, part_v, proj_v, wout_v, wqkv_v, wgrad_v, packed_v, tables_v, out_v, kv_v = refs[28:40]
    y_send, y_recv, load, up_sem, dn_sem, recv, dp_send, dp_recv, loc = refs[40:49]
    keep, two_send, two_recv, proj_send, proj_recv, one_send, one_recv = refs[49:]
    j, w = lax.axis_index("dp"), lax.axis_index("wide")
    z, y = w // 2, w % 2
    other = w + 1 - 2 * y
    greet(line, z, y, j, w)
    f32, low = jnp.float32, jnp.bfloat16
    window = 2

    chunks = [("early", 0, 0), ("early", 0, 1)]
    for part in range(1, 4):
        chunks += [("ffn", part, 0), ("ffn", part, 1)]
    for part in range(4):
        chunks += [("qkv", part, 0)]
    for part in range(4):
        chunks += [("out", part, 0)]
    count = len(chunks)
    names = ("qkv", "out", "ffn")

    def source(at, side):
        name, part, cut = chunks[at]
        if name == "qkv":
            return wgrad_v.at[:, flip(j, part), :, side]
        if name == "out":
            return wout_v.at[pl.ds(flip(j, part), 1), :, side]
        return grad_ffn.at[:, flip(j, part), :, side, :, cut * half : (cut + 1) * half]

    def held(refs, at):
        name, part, cut = chunks[at]
        ref = refs[names.index(name)]
        if name == "ffn":
            return ref.at[part - 1, :, :, :, cut * half : (cut + 1) * half]
        return ref.at[part]

    def own_rows(at):
        name, part, cut = chunks[at]
        if name == "ffn":
            return mine_ffn.at[(2 * part + cut) % (window + 2)]
        return source(at, y)

    def cross(at):
        return remote(
            source(at, 1 - y), held(crossed, at), y_send.at[at], y_recv.at[at], wide=other
        )

    def fetch(at):
        cut = chunks[at][2]
        if chunks[at][0] == "early":
            there = grad_ffn.at[:, j, :, :, :, cut * half : (cut + 1) * half]
            return pltpu.make_async_copy(there, early.at[cut], load.at[at])
        return pltpu.make_async_copy(source(at, y), own_rows(at), load.at[at])

    def fetches(at):
        return chunks[at][0] in ("early", "ffn")

    def cross_early(at):
        cut = chunks[at][2]
        return remote(
            early.at[cut, :, z, 1 - y], early_cross.at[cut], y_send.at[at], y_recv.at[at], wide=other
        )

    def moving(at, dest):
        if chunks[at][0] == "early":
            return early.at[chunks[at][2], :, dest]
        return held(crossed, at).at[:, dest]

    def landing(at, put):
        if chunks[at][0] == "early":
            return early_line.at[chunks[at][2], :, put]
        return held(lined, at).at[:, put]

    def up(at, dest, last):
        put = line if last else dest
        return remote(
            moving(at, dest), landing(at, put), up_sem.at[at, dest], recv.at[at, put], wide=w + 2
        )

    def dn(at, dest):
        return remote(
            moving(at, dest), landing(at, dest), dn_sem.at[at, dest], recv.at[at, dest], wide=w - 2
        )

    def arrived(at, put):
        there = landing(at, put)
        remote(there, there, dn_sem.at[at, 0], recv.at[at, put], wide=other).wait_recv()

    def add(at, dest, puts):
        name, part, cut = chunks[at]
        if name == "early":
            if not puts:
                return

            def rows(index):
                for side in range(2):
                    value = early[cut, index, dest, side].astype(f32)
                    for put in puts:
                        value = value + early_line[cut, index, put, side].astype(f32)
                    early[cut, index, dest, side] = value.astype(low)

            each(early.shape[1], rows)
            return
        here, own, line_in = held(crossed, at), own_rows(at), held(lined, at)

        def rows(index):
            value = here[index, dest].astype(f32) + own[index, dest].astype(f32)
            for put in puts:
                value = value + line_in[index, put].astype(f32)
            here[index, dest] = value.astype(low)

        each(here.shape[0], rows)

    def along(at, act):
        for far in range(line - 1, 0, -1):

            @pl.when(z >= far)
            def _():
                dest = z - far
                if act:

                    @pl.when(z < line - 1)
                    def _():
                        arrived(at, dest)
                        add(at, dest, (dest,))

                    @pl.when(z == line - 1)
                    def _():
                        add(at, dest, ())

                    dn(at, dest).start()
                else:
                    dn(at, dest).wait_send()

            @pl.when(z + far < line)
            def _():
                dest = z + far
                if act:

                    @pl.when(z > 0)
                    def _():
                        arrived(at, dest)
                        add(at, dest, (dest,))

                    @pl.when(z == 0)
                    def _():
                        add(at, dest, ())

                    up(at, dest, far == 1).start()
                else:
                    up(at, dest, far == 1).wait_send()

    def collect(at):
        @pl.when(z == 0)
        def _():
            arrived(at, z)
            add(at, z, (z,))

        @pl.when(z == line - 1)
        def _():
            arrived(at, line)
            add(at, z, (line,))

        @pl.when((z > 0) & (z < line - 1))
        def _():
            arrived(at, z)
            arrived(at, line)
            add(at, z, (z, line))

    def give(at):
        name, part, cut = chunks[at]
        rows = held(crossed, at).at[:, z]
        ref = outs[names.index(name)]
        if name == "out":
            target = ref.at[pl.ds(j, 1)]
        elif name == "qkv":
            target = ref.at[j]
        else:
            target = ref.at[j, :, :, cut * half : (cut + 1) * half]
        if part == 0:
            return pltpu.make_async_copy(rows, target, loc.at[at])
        return remote(rows, target, dp_send.at[at], dp_recv.at[at], dp=flip(j, part))

    def give_early(at):
        cut = chunks[at][2]
        target = outs[2].at[j, :, :, cut * half : (cut + 1) * half]
        return pltpu.make_async_copy(early_cross.at[cut], target, loc.at[at])

    def collect_and_give(at):
        collect(at)
        if chunks[at][0] == "early":
            cross_early(at).start()
        else:
            give(at).start()

    def finish_early(at):
        cut = chunks[at][2]
        cross_early(at).wait_recv()

        def rows(index):
            value = early_cross[cut, index].astype(f32) + early[cut, index, z, y].astype(f32)
            early_cross[cut, index] = value.astype(low)

        each(early.shape[1], rows)
        give_early(at).start()

    heads = out_v.shape[1] // HD
    seq = middle_v.shape[0]
    wide_rows = heads * HD
    loads = [
        pltpu.make_async_copy(middle_in, middle_v, keep.at[0]),
        pltpu.make_async_copy(cotangent, late_v, keep.at[1]),
        pltpu.make_async_copy(normed_part.at[j], part_v.at[0], keep.at[2]),
        pltpu.make_async_copy(normed_part.at[flip(j, 2)], part_v.at[2], keep.at[3]),
        pltpu.make_async_copy(w_out, wout_v, keep.at[4]),
        pltpu.make_async_copy(w_qkv, wqkv_v, keep.at[5]),
        pltpu.make_async_copy(packed_in, packed_v, keep.at[6]),
        pltpu.make_async_copy(tables_in, tables_v, keep.at[7]),
    ]
    load_rows = pltpu.make_async_copy(rows_in, part_v, keep.at[8])
    load_attn = [
        pltpu.make_async_copy(
            attn_in.at[n], late_v.at[:, n * wide_rows : (n + 1) * wide_rows], keep.at[9 + n]
        )
        for n in range(4)
    ]
    load_residual = pltpu.make_async_copy(residual, late_v, keep.at[13])
    keep_input = pltpu.make_async_copy(late_v, input_grad, keep.at[14])

    def send_two(part):
        block = part_v.at[2] if part == 2 else normed_part.at[flip(j, part)]
        peer = flip(j, 1 if part == 3 else part)
        return remote(block, sum_v.at[part - 1], two_send.at[part], two_recv.at[part], dp=peer)

    def send_one(part):
        peer = flip(j, 1 if part == 3 else part)
        return remote(
            part_v.at[part], sum_v.at[part - 1], one_send.at[part], one_recv.at[part], dp=peer
        )

    def send_proj(part):
        there = proj_v.at[flip(j, 2) if part == 3 else j]
        peer = flip(j, 1 if part == 3 else part)
        return remote(there, there, proj_send.at[part], proj_recv.at[part], dp=peer)

    def over_rows(step):
        each(seq // 32, lambda index: step(pl.ds(pl.multiple_of(index * 32, 32), 32)))

    def add_two():
        loads[3].wait()
        send_two(3).wait_recv()

        def rows(here):
            value = part_v[2, here, :].astype(f32) + sum_v[2, here, :].astype(f32)
            part_v[2, here, :] = value.astype(low)

        over_rows(rows)
        send_two(2).start()

    def norm_back(values, grads, gain, gain_row):
        rate = lax.rsqrt(jnp.mean(values * values, -1, keepdims=True) + norm_eps)
        scaled = grads * gain
        mean = jnp.mean(values * scaled, -1, keepdims=True)
        gain_parts[gain_row : gain_row + 1, :] += jnp.sum(grads * values * rate, 0, keepdims=True)
        return rate * scaled - values * rate * rate * rate * mean

    def second_norm():
        for at in (0, 1, 2):
            loads[at].wait()
        send_two(1).wait_recv()
        send_two(2).wait_recv()
        gain_parts[...] = jnp.zeros_like(gain_parts)
        scale = scale_ref[0, 0]

        def rows(here):
            grads = part_v[0, here, :].astype(f32)
            for part in (1, 2):
                grads = grads + sum_v[part - 1, here, :].astype(f32)
            value_grad = norm_back(middle_v[here, :], grads, gains_ref[1:2, :], 1)
            middle_grad = late_v[here, :].astype(f32) + value_grad
            middle_v[here, :] = middle_grad
            proj_v[j, here, :] = (scale * middle_grad).astype(low)

        over_rows(rows)
        send_proj(1).start()
        send_proj(2).start()
        send_two(2).wait_send()
        load_rows.start()
        for copy in load_attn:
            copy.start()

    def hand_on():
        send_proj(2).wait_recv()
        send_proj(3).start()

    def out_back(part):
        if part == 0:
            for at in (4, 5, 6, 7):
                loads[at].wait()
        elif part != 2:
            send_proj(part).wait_recv()
        weights = wout_v[...].reshape(wide_rows, D)
        value = lax.dot_general(
            proj_v[flip(j, part)], weights, (((1,), (1,)), ((), ())), preferred_element_type=f32
        )
        out_v[...] = value.astype(low)

    def turn_back(values, n):
        return values * tables_v[n, 0] - pltpu.roll(values, HD // 2, 1) * tables_v[n, 1]

    def attend_back(part, head):
        n = flip(j, part)
        own = slice(head * HD, (head + 1) * HD)
        query = packed_v[n, :, own]
        key = packed_v[n, :, wide_rows : wide_rows + HD]
        value = packed_v[n, :, wide_rows + HD :]
        grad = out_v[:, own]
        scores = lax.dot_general(
            query, key, (((1,), (1,)), ((), ())), preferred_element_type=f32
        ) * HD ** (-0.5)
        row = lax.broadcasted_iota(jnp.int32, (seq, seq), 0)
        column = lax.broadcasted_iota(jnp.int32, (seq, seq), 1)
        scores = jnp.where(row >= column, scores, masked_value)
        weight = jnp.exp(scores - jnp.max(scores, -1, keepdims=True))
        probs = weight / jnp.sum(weight, -1, keepdims=True)
        prob_grads = lax.dot_general(
            grad, value, (((1,), (1,)), ((), ())), preferred_element_type=f32
        )
        row_dot = jnp.sum(prob_grads * probs, -1, keepdims=True)
        score_low = (probs * (prob_grads - row_dot)).astype(low)
        query_grad = jnp.dot(score_low, key, preferred_element_type=f32) * HD ** (-0.5)
        key_grad = lax.dot_general(
            score_low, query, (((0,), (0,)), ((), ())), preferred_element_type=f32
        ) * HD ** (-0.5)
        value_grad = lax.dot_general(
            probs.astype(low), grad, (((0,), (0,)), ((), ())), preferred_element_type=f32
        )
        if head == 0:
            kv_v[0] = key_grad
            kv_v[1] = value_grad
        else:
            kv_v[0] += key_grad
            kv_v[1] += value_grad
        packed_v[n, :, own] = turn_back(query_grad, n).astype(low)
        if head == heads - 1:
            packed_v[n, :, wide_rows : wide_rows + HD] = turn_back(kv_v[0], n).astype(low)
            packed_v[n, :, wide_rows + HD :] = kv_v[1].astype(low)

    def out_grad(cut):
        if cut == 0:
            for copy in load_attn:
                copy.wait()
        columns = slice(cut * D // 4, (cut + 1) * D // 4)
        rows = jnp.concatenate(
            [late_v[:, n * wide_rows : (n + 1) * wide_rows] for n in range(4)], 0
        )
        grads = proj_v[:, :, columns].reshape(4 * seq, D // 4)
        value = lax.dot_general(rows, grads, (((0,), (0,)), ((), ())), preferred_element_type=f32)
        shape = wout_v.shape[:-1] + (D // 4,)
        wout_v[:, :, :, :, columns] = value.astype(low).reshape(shape)

    def qkv_grad(cut):
        if cut == 0:
            load_rows.wait()
            load_residual.start()
        columns = slice(cut * D // 4, (cut + 1) * D // 4)
        rows = part_v[:, :, columns].reshape(4 * seq, D // 4)
        grads = packed_v[...].reshape(4 * seq, packed_v.shape[2])
        value = lax.dot_general(rows, grads, (((0,), (0,)), ((), ())), preferred_element_type=f32)
        wgrad_v[cut] = value.astype(low).reshape(wgrad_v.shape[1:])

    def rows_back(part):
        n = flip(j, part)
        if part == 2:
            send_one(3).wait_recv()
        for cut in range(4):
            columns = slice(cut * D // 4, (cut + 1) * D // 4)
            weights = wqkv_v[cut].reshape(D // 4, packed_v.shape[2])
            value = lax.dot_general(
                packed_v[n], weights, (((1,), (1,)), ((), ())), preferred_element_type=f32
            )
            if part == 2:
                value = value + sum_v[2, :, columns].astype(f32)
            part_v[part, :, columns] = value.astype(low)
        if part > 0:
            send_one(part).start()

    def first_norm():
        load_residual.wait()
        for part in (1, 2):
            send_one(part).wait_recv()

        def rows(here):
            grads = part_v[0, here, :].astype(f32)
            for part in (1, 2):
                grads = grads + sum_v[part - 1, here, :].astype(f32)
            value_grad = norm_back(late_v[here, :].astype(f32), grads, gains_ref[0:1, :], 0)
            late_v[here, :] = (middle_v[here, :] + value_grad).astype(low)

        over_rows(rows)
        keep_input.start()

    def sequence(part):
        return [functools.partial(out_back, part)] + [
            functools.partial(attend_back, part, head) for head in range(heads)
        ]

    work = {
        1: [second_norm] + sequence(0),
        2: sequence(1) + [hand_on],
        3: sequence(3) + sequence(2),
        4: [functools.partial(out_grad, cut) for cut in range(4)]
        + [functools.partial(qkv_grad, cut) for cut in range(4)],
        7: [functools.partial(rows_back, 3)],
        8: [functools.partial(rows_back, 2)],
        9: [functools.partial(rows_back, 1)],
        10: [functools.partial(rows_back, 0)],
        12: [first_norm],
    }

    late = list(range(2, count))
    send_two(3).start()
    send_two(1).start()
    for at in range(2):
        fetch(at).start()
    for copy in loads:
        copy.start()

    def begin(at):
        if fetches(at):
            fetch(at).start()
        cross(at).start()

    for at in late[:window]:
        begin(at)
    add_two()
    for at in range(2):
        fetch(at).wait()
        along(at, True)
    for step, at in enumerate(late):
        pieces = work.get(step, [])
        cut = (len(pieces) + 1) // 2
        cross(at).wait_send()
        following = late[step + window] if step + window < len(late) else None
        if following is not None and step != 4:
            begin(following)
        cross(at).wait_recv()
        if fetches(at):
            fetch(at).wait()
        along(at, True)
        for piece in pieces[:cut]:
            piece()
        if step < 2:
            collect_and_give(step)
        if step >= 1:
            collect_and_give(late[step - 1])
        for piece in pieces[cut:]:
            piece()
        if step == 4:
            begin(following)
        if step in (3, 4):
            finish_early(step - 3)
    collect_and_give(late[-1])
    for at in range(count):
        along(at, False)
        if chunks[at][0] == "early":
            cross_early(at).wait_send()
            give_early(at).wait()
        else:
            give(at).wait()
    for part in range(1, 4):
        if part != 2:
            send_two(part).wait_send()
        send_proj(part).wait_send()
        send_one(part).wait_send()
    keep_input.wait()


def scatter_call(line, ffn, normed_part, middle, cotangent, residual, w_out, w_qkv, packed, attn, rows, tables, scale, gains):
    low = jnp.bfloat16
    rm, ndp, _, piece, wq = w_qkv.shape
    wf, wo = ffn.shape[4], w_out.shape[3]
    seq = middle.shape[0]
    ffn = ffn.reshape(rm, ndp, line, 2, piece, wf)
    w_out = w_out.reshape(ndp, line, 2, piece, wo)
    w_qkv = w_qkv.reshape(rm, ndp, line, 2, piece, wq)

    def shape(*dims, kind=low):
        return jax.ShapeDtypeStruct(dims, kind)

    outs = (
        shape(ndp, rm, piece, wq),
        shape(ndp, piece, wo),
        shape(ndp, rm, piece, wf),
        shape(seq, D),
        shape(2, D, kind=jnp.float32),
    )

    def held(places):
        return [
            pltpu.VMEM((ndp, rm, places, piece, wq), low),
            pltpu.VMEM((ndp, 1, places, piece, wo), low),
            pltpu.VMEM((ndp - 1, rm, places, piece, wf), low),
        ]

    dma = pltpu.SemaphoreType.DMA
    whole = pl.BlockSpec(memory_space=pltpu.VMEM)
    count = 16
    return pl.pallas_call(
        functools.partial(scatter_kernel, line, wf // 2),
        out_shape=outs,
        in_specs=[ANY] * 11 + [pl.BlockSpec(memory_space=pltpu.SMEM), whole],
        out_specs=[ANY] * 4 + [whole],
        scratch_shapes=held(line)
        + held(line + 1)
        + [
            pltpu.VMEM((4, rm, line, piece, wf // 2), low),
            pltpu.VMEM((2, rm, line, 2, piece, wf // 2), low),
            pltpu.VMEM((2, rm, line + 1, 2, piece, wf // 2), low),
            pltpu.VMEM((2, rm, piece, wf // 2), low),
            pltpu.VMEM((seq, D), jnp.float32),
            pltpu.VMEM((seq, D), low),
            pltpu.VMEM((3, seq, D), low),
            pltpu.VMEM((ndp, seq, D), low),
            pltpu.VMEM((ndp, seq, D), low),
            pltpu.VMEM(w_out.shape, low),
            pltpu.VMEM(w_qkv.shape, low),
            pltpu.VMEM(w_qkv.shape, low),
            pltpu.VMEM(packed.shape, low),
            pltpu.VMEM(tables.shape, tables.dtype),
            pltpu.VMEM((seq, attn.shape[2]), low),
            pltpu.VMEM((2, seq, HD), jnp.float32),
        ]
        + [dma((count,))] * 3
        + [dma((count, line)), dma((count, line)), dma((count, line + 1))]
        + [dma((count,))] * 3
        + [dma((15,))]
        + [dma((4,))] * 6,
        compiler_params=pltpu.CompilerParams(
            collective_id=1, has_side_effects=True, vmem_limit_bytes=60 * 1024 * 1024
        ),
        name="scatter_grads",
    )(ffn, normed_part, middle, cotangent, residual, w_out, w_qkv, packed, attn, rows, tables, scale, gains)


def gains_kernel(line, part_ref, total_ref, dp_parts, wide_parts, dp_send, dp_recv, wide_send, wide_recv):
    j, w = lax.axis_index("dp"), lax.axis_index("wide")
    wide = 2 * line
    barrier = pltpu.get_barrier_semaphore()
    for part in range(1, 4):
        pl.semaphore_signal(barrier, device_id={"dp": flip(j, part)}, device_id_type=MESH)
    for far in range(1, wide):
        pl.semaphore_signal(barrier, device_id={"wide": (w + far) % wide}, device_id_type=MESH)
    pl.semaphore_wait(barrier, 3 + wide - 1)
    copies = [
        remote(part_ref, dp_parts.at[j], dp_send.at[part], dp_recv.at[part], dp=flip(j, part))
        for part in range(1, 4)
    ]
    for copy in copies:
        copy.start()
    dp_parts[j] = part_ref[...]
    for copy in copies:
        copy.wait()
    value = dp_parts[0]
    for rank in range(1, 4):
        value = value + dp_parts[rank]
    wide_parts[w] = value
    copies = [
        remote(
            wide_parts.at[w],
            wide_parts.at[w],
            wide_send.at[far],
            wide_recv.at[far],
            wide=(w + far) % wide,
        )
        for far in range(1, wide)
    ]
    for copy in copies:
        copy.start()
    for copy in copies:
        copy.wait()
    value = wide_parts[0]
    for rank in range(1, wide):
        value = value + wide_parts[rank]
    total_ref[...] = value


def gains_call(line, parts):
    dma = pltpu.SemaphoreType.DMA
    whole = pl.BlockSpec(memory_space=pltpu.VMEM)
    return pl.pallas_call(
        functools.partial(gains_kernel, line),
        out_shape=jax.ShapeDtypeStruct(parts.shape, jnp.float32),
        in_specs=[whole],
        out_specs=whole,
        scratch_shapes=[
            pltpu.VMEM((4, *parts.shape), jnp.float32),
            pltpu.VMEM((2 * line, *parts.shape), jnp.float32),
            dma((4,)),
            dma((4,)),
            dma((2 * line,)),
            dma((2 * line,)),
        ],
        compiler_params=pltpu.CompilerParams(collective_id=2, has_side_effects=True),
        name="sum_gains",
    )(parts)


def attention(tokens, ndp, heads, qkv_rows, tables):
    low = jnp.bfloat16
    seq_len = tokens // ndp
    cosine, sine = tables[:, 0].reshape(tokens, 1, HD), tables[:, 1].reshape(tokens, 1, HD)
    turned = qkv_rows[:, : (heads + 1) * HD].reshape(tokens, heads + 1, HD)
    turned = (turned * cosine + jnp.roll(turned, HD // 2, -1) * sine).astype(low)
    query_rows = turned[:, :heads].reshape(ndp, seq_len, heads, HD)
    key_rows = turned[:, heads].reshape(ndp, seq_len, HD)
    value_rows = qkv_rows[:, (heads + 1) * HD :].astype(low).reshape(ndp, seq_len, HD)
    probs_low = attention_probs(query_rows, key_rows).astype(low)
    out_low = jnp.einsum(
        "ngst,ntd->nsgd", probs_low, value_rows, preferred_element_type=jnp.float32
    ).astype(low)
    packed = jnp.concatenate(
        [turned.reshape(ndp, seq_len, (heads + 1) * HD), value_rows], -1
    )
    return packed, out_low.reshape(ndp, seq_len, heads * HD)


def attention_probs(query_rows, key_rows):
    seq_len = query_rows.shape[1]
    causal = jnp.arange(seq_len)[:, None] >= jnp.arange(seq_len)[None, :]
    scores = jnp.einsum(
        "nsgd,ntd->ngst", query_rows, key_rows, preferred_element_type=jnp.float32
    ) * HD ** (-0.5)
    scores = jnp.where(causal, scores, masked_value)
    row_top = jnp.max(scores, -1, keepdims=True)
    exp_scores = jnp.exp(scores - row_top)
    return exp_scores / jnp.sum(exp_scores, -1, keepdims=True)


def gather_weights(qkv_s, out_s, ffn_s, rows, low_rows, tables, residual, scale, gain):
    ndp, nwide = lax.axis_size("dp"), lax.axis_size("wide")
    if ndp == 4 and nwide == 8 and qkv_s.shape[2] % 16 == 0:
        return gather_call(
            nwide // 2, qkv_s, out_s, ffn_s, rows, low_rows, tables, residual, scale, gain
        )

    def spread(values):
        moved = lax.all_to_all(values, "dp", split_axis=0, concat_axis=0, tiled=True)
        return lax.all_gather(moved, "wide", axis=0)

    seq_len = rows.shape[0]
    tokens = ndp * seq_len
    heads = HEADS // ndp
    w_qkv = spread(qkv_s).transpose(2, 1, 0, 3, 4)
    w_out = spread(out_s).transpose(1, 0, 2, 3)
    w_ffn = spread(ffn_s).transpose(2, 1, 0, 3, 4)
    normed_one = lax.all_gather(rows, "dp", axis=0)
    all_tables = lax.all_gather(tables, "dp", axis=0)
    packed, out_low = attention(
        tokens,
        ndp,
        heads,
        dot(normed_one.reshape(tokens, D), w_qkv.reshape(D, -1)),
        all_tables,
    )
    part = dot(out_low.reshape(tokens, heads * HD), w_out.reshape(heads * HD, D))
    middle = residual.astype(jnp.float32) + scale * total(part)
    normed_two = (middle * norm_rate(middle) * gain).astype(jnp.bfloat16)
    return (
        w_qkv,
        w_out,
        w_ffn,
        lax.all_gather(low_rows, "dp", axis=0),
        packed,
        out_low,
        middle,
        lax.all_gather(normed_two, "dp", axis=0),
        normed_one,
        all_tables,
    )


def scatter_grads(
    ffn, normed_part, middle, cotangent, residual, w_out, w_qkv, packed, attn, rows, tables, scale, gains
):
    ndp, nwide = lax.axis_size("dp"), lax.axis_size("wide")
    if ndp == 4 and nwide == 8 and ffn.shape[3] % 16 == 0:
        return scatter_call(
            nwide // 2, ffn, normed_part, middle, cotangent, residual,
            w_out, w_qkv, packed, attn, rows, tables, scale, gains,
        )
    low = jnp.bfloat16
    _, seq_len, width = packed.shape
    tokens = ndp * seq_len
    heads = HEADS // ndp
    wq = heads * HD
    score_scale = HD ** (-0.5)
    query_rows = packed[..., :wq].reshape(ndp, seq_len, heads, HD)
    key_rows = packed[..., wq : wq + HD]
    value_rows = packed[..., wq + HD :]
    normed_grad = total(normed_part.reshape(tokens, D))
    middle_local, gain_two = norm_backward(middle, norm_rate(middle), gains[1], normed_grad)
    middle_grad = cotangent.astype(jnp.float32) + middle_local
    proj_low = share((scale * middle_grad).astype(low))
    probs_float = attention_probs(query_rows, key_rows)
    attn_grad = dot_back(proj_low, w_out.reshape(wq, D)).astype(low)
    attn_grad = attn_grad.reshape(ndp, seq_len, heads, HD)
    prob_grads = jnp.einsum(
        "nsgd,ntd->ngst", attn_grad, value_rows, preferred_element_type=jnp.float32
    )
    row_dot = jnp.sum(prob_grads * probs_float, -1, keepdims=True)
    score_low = (probs_float * (prob_grads - row_dot)).astype(low)
    query_grad = (
        jnp.einsum("ngst,ntd->nsgd", score_low, key_rows, preferred_element_type=jnp.float32)
        * score_scale
    )
    key_grad = (
        jnp.einsum("ngst,nsgd->ntd", score_low, query_rows, preferred_element_type=jnp.float32)
        * score_scale
    )
    value_grad = jnp.einsum(
        "ngst,nsgd->ntd",
        probs_float.astype(low),
        attn_grad,
        preferred_element_type=jnp.float32,
    )
    turned = jnp.concatenate([query_grad.reshape(ndp, seq_len, wq), key_grad], -1)
    turned = turned.reshape(tokens, heads + 1, HD)
    cosine = tables[:, 0].reshape(tokens, 1, HD)
    sine = tables[:, 1].reshape(tokens, 1, HD)
    turned = (turned * cosine - jnp.roll(turned, HD // 2, -1) * sine).astype(low)
    qkv_low = jnp.concatenate(
        [turned.reshape(tokens, wq + HD), value_grad.reshape(tokens, HD).astype(low)], 1
    )
    normed_grad = total(dot_back(qkv_low, w_qkv.reshape(D, width)))
    source = residual.astype(jnp.float32)
    input_local, gain_one = norm_backward(source, norm_rate(source), gains[0], normed_grad)

    def collect(values):
        moved = lax.psum_scatter(values, "wide", scatter_dimension=0, tiled=False)
        return lax.all_to_all(moved, "dp", split_axis=0, concat_axis=0, tiled=True)

    grad_qkv = dot_grad(rows.reshape(tokens, D), qkv_low).astype(low).reshape(w_qkv.shape)
    grad_out = dot_grad(attn.reshape(tokens, wq), proj_low).astype(low).reshape(w_out.shape)
    return (
        collect(grad_qkv.transpose(2, 1, 0, 3, 4)),
        collect(grad_out.transpose(1, 0, 2, 3)),
        collect(ffn.transpose(2, 1, 0, 3, 4)),
        (middle_grad + input_local).astype(low),
        jnp.stack([gain_one, gain_two]),
    )


def sum_gains(parts):
    ndp, nwide = lax.axis_size("dp"), lax.axis_size("wide")
    if ndp == 4 and nwide == 8:
        return gains_call(nwide // 2, parts)
    return lax.psum(parts, ("dp", "wide"))


def unfold_rows(rows_ref, flat_ref, piece):
    count = rows_ref.shape[0]
    for first in range(0, count, 8):
        size = min(8, count - first)
        for row in range(piece):
            for group in range(B // 128):
                start = row * B + group * 128
                flat_ref[group, pl.ds(first * piece + row, size, stride=piece), :] = rows_ref[
                    first : first + size, start : start + 128
                ]


def block_places(rm, ndp, rf, part):
    places = []
    for i in range(rm):
        for c in range(ndp):
            places.append((i * ndp + c, 0, 0, (c, i), 0, B))
    for i in range(rm):
        for c in range(ndp):
            places.append((rm * rm + i, c * part, 0, (c, i), B, part))
            places.append((rm * rm + rm + i, c * part, 0, (c, i), B + part, part))
    first = rm * rm + 2 * rm
    for c in range(ndp):
        for i in range(rm):
            places.append((first + c * rm + i, 0, 1, (c,), i * B, B))
    first = first + rm * rm
    for i in range(rm):
        for b in range(rf):
            for c in range(ndp):
                for side in range(2):
                    block = first + side * rm * rf + i * rf + b
                    places.append((block, c * part, 2, (c, i), (side * rf + b) * part, part))
    first = first + 2 * rm * rf
    for b in range(rf):
        for i in range(rm):
            places.append((first + b * rm + i, 0, 3, (b,), i * B, B))
    return places


def pack_kernel(places, piece, rows_ref, *refs):
    pieces, flat_ref = refs[:4], refs[4]
    unfold_rows(rows_ref, flat_ref, piece)
    for block, column, array, lead, start, width in places:
        for offset in range(0, width, 128):
            value = flat_ref[(column + offset) // 128, block * piece : (block + 1) * piece, :]
            there = slice(start + offset, start + offset + 128)
            pieces[array][(*lead, slice(None), there)] = value.astype(jnp.bfloat16)


def slots_kernel(places, piece, slot_ref, *refs):
    pieces, send_ref, blocks_ref = refs[:4], refs[4], refs[5]
    for block, column, array, lead, start, width in places:
        value = pieces[array][(*lead, slice(None), slice(start, start + width))]
        blocks_ref[block, :, column : column + width] = value
    each_slot = send_ref.shape[1]

    def device(index, carry):
        for slot in range(each_slot):
            block = slot_ref[index * each_slot + slot]
            value = blocks_ref[jnp.maximum(block, 0)]
            send_ref[index, slot] = jnp.where(block >= 0, value, jnp.zeros_like(value))
        return carry

    lax.fori_loop(0, send_ref.shape[0], device, 0)


def precondition_kernel(scale_ref, grad_ref, left_ref, right_ref, step_ref):
    low, f32 = jnp.bfloat16, jnp.float32
    scale = scale_ref[pl.program_id(0)]
    grad = grad_ref[:, 0].reshape(B, B)
    value = jnp.dot(left_ref[0].astype(low), grad, preferred_element_type=f32)
    value = jnp.dot(value.astype(low), right_ref[0].astype(low), preferred_element_type=f32)
    rate = lax.rsqrt(jnp.mean(value * value, keepdims=True) + scale_eps)
    value = value * (weight_rate * scale * rate)
    step_ref[:, 0] = value.astype(low).reshape(step_ref.shape[0], step_ref.shape[2], B)


def update_kernel(piece, slot_ref, steps_ref, master_ref, out_ref, flat_ref):
    each_slot = steps_ref.shape[1]
    count = master_ref.shape[0]

    def block(index, carry):
        slot = slot_ref[index]
        value = steps_ref[slot // each_slot, slot % each_slot].astype(jnp.float32)
        rows = pl.ds(pl.multiple_of(index * piece, piece), piece)
        for group in range(B // 128):
            flat_ref[group, rows, :] = value[:, group * 128 : (group + 1) * 128]
        return carry

    lax.fori_loop(0, count, block, 0)
    for first in range(0, count, 8):
        size = min(8, count - first)
        for row in range(piece):
            for group in range(B // 128):
                step = flat_ref[group, pl.ds(first * piece + row, size, stride=piece), :]
                start = row * B + group * 128
                columns = slice(start, start + 128)
                out_ref[first : first + size, columns] = (1.0 - weight_decay) * master_ref[
                    first : first + size, columns
                ] - step


def vmem_call(kernel, outs, args, scratch=(), prefetch=0, name=None):
    whole = pl.BlockSpec(memory_space=pltpu.VMEM)
    small = pl.BlockSpec(memory_space=pltpu.SMEM)
    return pl.pallas_call(
        kernel,
        out_shape=outs,
        in_specs=[small] * prefetch + [whole] * (len(args) - prefetch),
        out_specs=jax.tree.map(lambda _: whole, outs),
        scratch_shapes=list(scratch),
        compiler_params=pltpu.CompilerParams(vmem_limit_bytes=48 * 1024 * 1024),
        name=name,
    )(*args)


def pack_call(rows, ndp):
    rm, rf, part, piece = D // B, FF // B, B // ndp, rows.shape[1] // B
    low = jnp.bfloat16
    outs = (
        jax.ShapeDtypeStruct((ndp, rm, piece, B + 2 * part), low),
        jax.ShapeDtypeStruct((ndp, piece, D), low),
        jax.ShapeDtypeStruct((ndp, rm, piece, 2 * rf * part), low),
        jax.ShapeDtypeStruct((rf, piece, D), low),
    )
    return vmem_call(
        functools.partial(pack_kernel, block_places(rm, ndp, rf, part), piece),
        outs,
        (rows,),
        [pltpu.VMEM((B // 128, NBLK * piece, 128), jnp.float32)],
        name="pack",
    )


def slots_call(slot_block, pieces, devices):
    ndp, rm, piece, _ = pieces[0].shape
    rf = pieces[3].shape[0]
    low = jnp.bfloat16
    outs = (
        jax.ShapeDtypeStruct((devices, slot_block.shape[0] // devices, piece, B), low),
        jax.ShapeDtypeStruct((NBLK, piece, B), low),
    )
    return vmem_call(
        functools.partial(slots_kernel, block_places(rm, ndp, rf, B // ndp), piece),
        outs,
        (slot_block, *pieces),
        prefetch=1,
        name="to_slots",
    )


def precondition_call(scale, owned, left, right):
    devices, slots, piece, _ = owned.shape
    block = pl.BlockSpec((devices, 1, piece, B), lambda n: (0, n, 0, 0))
    square = pl.BlockSpec((1, B, B), lambda n: (n, 0, 0))
    return pl.pallas_call(
        precondition_kernel,
        out_shape=jax.ShapeDtypeStruct(owned.shape, jnp.bfloat16),
        grid=(slots,),
        in_specs=[pl.BlockSpec(memory_space=pltpu.SMEM), block, square, square],
        out_specs=block,
        compiler_params=pltpu.CompilerParams(vmem_limit_bytes=48 * 1024 * 1024),
        name="precondition",
    )(scale, owned, left, right)


def update_call(block_slot, returned, master):
    piece = master.shape[1] // B
    return vmem_call(
        functools.partial(update_kernel, piece),
        jax.ShapeDtypeStruct(master.shape, jnp.float32),
        (block_slot, returned, master),
        [pltpu.VMEM((B // 128, NBLK * piece, 128), jnp.float32)],
        prefetch=1,
        name="update",
    )


def pack(master_weights, ndp):
    low = jnp.bfloat16
    piece = master_weights.shape[1] // B
    if ndp == 4 and piece % 16 == 0:
        return pack_call(master_weights, ndp)
    rm, rf, part = D // B, FF // B, B // ndp
    first_key = rm * rm
    first_value = first_key + rm
    first_out = first_value + rm
    first_gate = first_out + rm * rm
    first_up = first_gate + rm * rf
    first_down = first_up + rm * rf
    mine = master_weights.astype(low).reshape(NBLK, piece, B)

    def cut_columns(first, blocks):
        own = mine[first : first + rm * blocks].reshape(rm, blocks, piece, ndp, part)
        return own.transpose(3, 0, 2, 1, 4).reshape(ndp, rm, piece, blocks * part)

    qkv_s = jnp.concatenate(
        [
            mine[:first_key].reshape(rm, ndp, piece, B).transpose(1, 0, 2, 3),
            cut_columns(first_key, 1),
            cut_columns(first_value, 1),
        ],
        -1,
    )
    out_s = (
        mine[first_out:first_gate].reshape(ndp, rm, piece, B).transpose(0, 2, 1, 3)
    ).reshape(ndp, piece, D)
    ffn_s = jnp.concatenate([cut_columns(first_gate, rf), cut_columns(first_up, rf)], -1)
    down_s = mine[first_down:].reshape(rf, rm, piece, B).transpose(0, 2, 1, 3)
    down_s = down_s.reshape(rf, piece, D)
    return qkv_s, out_s, ffn_s, down_s


def to_slots(slot_block, pieces, devices):
    ndp, rm, piece, _ = pieces[0].shape
    if ndp == 4 and piece % 16 == 0:
        return slots_call(slot_block, pieces, devices)
    grad_qkv, grad_out, grad_ffn, grad_down = pieces
    low = jnp.bfloat16
    rf = grad_down.shape[0]
    part = B // ndp
    wq = B

    def join_columns(cut, blocks):
        own = cut.reshape(ndp, rm, piece, blocks, part).transpose(1, 3, 2, 0, 4)
        return own.reshape(rm * blocks, piece, B)

    grad_rows = jnp.concatenate(
        [
            grad_qkv[..., :wq].transpose(1, 0, 2, 3).reshape(rm * ndp, piece, B),
            join_columns(grad_qkv[..., wq : wq + part], 1),
            join_columns(grad_qkv[..., wq + part :], 1),
            grad_out.reshape(ndp, piece, rm, B).transpose(0, 2, 1, 3).reshape(ndp * rm, piece, B),
            join_columns(grad_ffn[..., : rf * part], rf),
            join_columns(grad_ffn[..., rf * part :], rf),
            grad_down.reshape(rf, piece, rm, B).transpose(0, 2, 1, 3).reshape(rf * rm, piece, B),
        ],
        0,
    )
    send_rows = jnp.where(
        (slot_block >= 0)[:, None, None],
        grad_rows[jnp.maximum(slot_block, 0)],
        jnp.zeros((), low),
    )
    return send_rows.reshape(devices, -1, piece, B), grad_rows


def precondition(scale, owned, left, right):
    low = jnp.bfloat16
    devices, slots, piece, _ = owned.shape
    if piece % 16 == 0:
        return precondition_call(scale, owned, left, right)
    blocks = owned.transpose(1, 0, 2, 3).reshape(slots, B, B)
    value = jnp.einsum("nij,njk->nik", left.astype(low), blocks, preferred_element_type=jnp.float32)
    value = jnp.einsum(
        "nij,njk->nik", value.astype(low), right.astype(low), preferred_element_type=jnp.float32
    )
    rate = lax.rsqrt(jnp.mean(value * value, axis=(1, 2), keepdims=True) + scale_eps)
    steps = weight_rate * scale[:, None, None] * value * rate
    return steps.astype(low).reshape(slots, devices, piece, B).transpose(1, 0, 2, 3)


def update(block_slot, returned, master_weights):
    devices, slots, piece, _ = returned.shape
    if piece % 16 == 0:
        return update_call(block_slot, returned, master_weights)
    steps = returned.reshape(devices * slots, piece, B)[block_slot].astype(jnp.float32)
    return (1.0 - weight_decay) * master_weights - steps.reshape(NBLK, piece * B)


def local(
    inputs,
    cotangent,
    keep_mask,
    positions,
    master_weights,
    gains,
    gain_moments,
    block_slot,
    stat_left,
    stat_right,
    root_left,
    root_right,
):
    low = jnp.bfloat16
    ndp = lax.axis_size("dp")
    nwide = lax.axis_size("wide")
    rm = D // B
    rf = FF // B
    seq_len = inputs.shape[1]
    tokens = ndp * seq_len
    slot_dev = stat_left.shape[0]
    slots_all = slot_dev * ndp * nwide
    piece = master_weights.shape[1] // B
    part = B // ndp

    residual = inputs[0].astype(jnp.float32)
    branch_scale = keep_mask[0].astype(jnp.float32) / keep_rate()
    out_grad_f = cotangent[0].astype(jnp.float32)
    rate_one = norm_rate(residual)

    qkv_s, out_s, ffn_s, down_s = pack(master_weights, ndp)
    down_all = lax.all_gather(down_s, "wide", axis=0)
    cosine_table, sine_table = rope_tables(positions[0])
    signs = jnp.where(jnp.arange(HD) < HD // 2, -1.0, 1.0)
    (
        w_qkv,
        w_out,
        w_ffn,
        down_low,
        packed,
        out_low,
        middle,
        normed_two,
        normed_one,
        all_tables,
    ) = gather_weights(
        qkv_s,
        out_s,
        ffn_s,
        (residual * rate_one * gains[0]).astype(low),
        (branch_scale * out_grad_f).astype(low),
        jnp.stack([cosine_table, sine_table * signs]),
        inputs[0],
        branch_scale.reshape(1, 1),
        gains[1:],
    )
    w_ffn = w_ffn.reshape(D, 2 * rf * part)
    w_down = down_all.transpose(1, 0, 2, 3).reshape(rf * part, D)
    normed_two = normed_two.reshape(tokens, D)
    down_low = down_low.reshape(tokens, D)

    ffn_rows = dot(normed_two, w_ffn)
    gate_rows, up_rows = ffn_rows[:, : rf * part], ffn_rows[:, rf * part :]
    sigmoid_gate = jax.nn.sigmoid(gate_rows)
    hidden = (gate_rows * sigmoid_gate * up_rows).astype(low)
    hidden_grad = dot_back(down_low, w_down)
    gate_low = (
        hidden_grad * up_rows * sigmoid_gate * (1.0 + gate_rows * (1.0 - sigmoid_gate))
    ).astype(low)
    up_low = (hidden_grad * gate_rows * sigmoid_gate).astype(low)
    ffn_low = jnp.concatenate([gate_low, up_low], 1)
    down_part = dot_grad(hidden, down_low).astype(low).reshape(rf, nwide, piece, D)
    down_part, ffn_low = lax.optimization_barrier((down_part.transpose(1, 0, 2, 3), ffn_low))
    grad_down = lax.psum_scatter(down_part, "wide", scatter_dimension=0, tiled=False)
    result = middle + branch_scale * total(dot(hidden, w_down))
    output = result.astype(low)[None]
    grad_qkv, grad_out, grad_ffn, input_grad, gain_parts = scatter_grads(
        dot_grad(normed_two, ffn_low).astype(low).reshape(rm, ndp, nwide, piece, 2 * rf * part),
        dot_back(ffn_low, w_ffn).astype(low).reshape(ndp, seq_len, D),
        middle,
        cotangent[0],
        inputs[0],
        w_out,
        w_qkv,
        packed,
        out_low,
        normed_one,
        all_tables,
        branch_scale.reshape(1, 1),
        gains,
    )
    input_grad = input_grad[None]
    gain_grads = sum_gains(gain_parts)
    new_gain_moments = stat_decay * gain_moments + (1.0 - stat_decay) * gain_grads * gain_grads
    new_gains = gains - gain_rate * gain_grads / (jnp.sqrt(new_gain_moments) + adam_eps)

    slot_block = jnp.full((slots_all,), -1, jnp.int32).at[block_slot].set(jnp.arange(NBLK))
    send_rows, grad_rows = to_slots(
        slot_block, (grad_qkv, grad_out, grad_ffn, grad_down), ndp * nwide
    )
    grad_local = grad_rows.reshape(NBLK, piece * B).astype(jnp.float32)
    owned = lax.all_to_all(send_rows, ("dp", "wide"), split_axis=0, concat_axis=0, tiled=True)
    own_blocks = lax.dynamic_slice_in_dim(
        slot_block, lax.axis_index(("dp", "wide")) * slot_dev, slot_dev
    )
    own_scale = jnp.where(own_blocks >= 0, block_scale(jnp.maximum(own_blocks, 0)), 0.0)
    steps_local = precondition(own_scale, owned, root_left, root_right)
    steps_local, gain_grads = lax.optimization_barrier((steps_local, gain_grads))
    returned = lax.all_to_all(steps_local, ("dp", "wide"), split_axis=0, concat_axis=0, tiled=True)
    blocks = owned.transpose(1, 0, 2, 3).reshape(slot_dev, B, B)
    new_left = stat_decay * stat_left + (1.0 - stat_decay) * jnp.einsum(
        "nij,nkj->nik", blocks, blocks, preferred_element_type=jnp.float32
    )
    new_right = stat_decay * stat_right + (1.0 - stat_decay) * jnp.einsum(
        "nji,njk->nik", blocks, blocks, preferred_element_type=jnp.float32
    )
    new_weights = update(block_slot, returned, master_weights)
    return (
        output,
        input_grad,
        grad_local,
        new_left,
        new_right,
        new_weights,
        gain_grads,
        new_gain_moments,
        new_gains,
    )


def solution(mesh):
    placed = (
        P(("dp", "wide"), None, None),
        P(("dp", "wide"), None, None),
        P(("dp", "wide")),
        P(("dp", "wide"), None),
        P(None, ("dp", "wide")),
        P(),
        P(),
        P(),
        P(("dp", "wide"), None, None),
        P(("dp", "wide"), None, None),
        P(("dp", "wide"), None, None),
        P(("dp", "wide"), None, None),
    )
    return jax.shard_map(
        local,
        mesh=mesh,
        in_specs=placed,
        out_specs=(
            P(("dp", "wide"), None, None),
            P(("dp", "wide"), None, None),
            P(None, ("dp", "wide")),
            P(("dp", "wide"), None, None),
            P(("dp", "wide"), None, None),
            P(None, ("dp", "wide")),
            P(),
            P(),
            P(),
        ),
        check_vma=False,
    )
```

```python
import functools

import jax
import jax.numpy as jnp
from jax import lax
from jax.experimental import pallas as pl
from jax.experimental.pallas import tpu as pltpu
from jax.sharding import PartitionSpec as P

D = 2048
HEADS = 16
HD = 128
KVH = 4
FF = 5632
B = 512
SEQ = 256
LAYER = 16
DEPTH = 24
STEP = 10
RAMP = 20
NBLK = 172


norm_eps = 1e-05
stat_decay = 0.95
weight_rate = 0.5
weight_decay = 0.001
gain_rate = 0.05
adam_eps = 1e-08
rope_base = 10000.0
scale_eps = 1e-06
masked_value = -1e30


def keep_rate():
    return 1.0 - 0.2 * (2.0 ** (LAYER / (DEPTH - 1)) - 1.0) * min(STEP / RAMP, 1.0)


def block_shapes():
    rows_model = D // B
    rows_kv = KVH * HD // B
    rows_ff = FF // B
    return [
        (rows_model, rows_model),
        (rows_model, rows_kv),
        (rows_model, rows_kv),
        (rows_model, rows_model),
        (rows_model, rows_ff),
        (rows_model, rows_ff),
        (rows_ff, rows_model),
    ]


def block_scale(block_index):
    bounds = []
    running = 0
    for row_blocks, col_blocks in block_shapes():
        running = running + row_blocks * col_blocks
        bounds.append(running)
    plain_scale = D ** (-0.5)
    out_scale = (SEQ / 8.0) ** 0.5 * D ** (-0.5)
    return jnp.where(
        block_index < bounds[2],
        plain_scale,
        jnp.where(
            block_index < bounds[3],
            out_scale,
            jnp.where(block_index < bounds[5], plain_scale, FF ** (-0.5)),
        ),
    ).astype(jnp.float32)


def rope_tables(position):
    half_dim = HD // 2
    freqs = rope_base ** (-(jnp.arange(half_dim).astype(jnp.float32) * 2.0 / HD))
    angles = position.astype(jnp.float32)[:, None] * freqs[None, :]
    cosine_table = jnp.concatenate([jnp.cos(angles), jnp.cos(angles)], -1)
    sine_table = jnp.concatenate([jnp.sin(angles), jnp.sin(angles)], -1)
    return (cosine_table, sine_table)


def rotate(values, cosine_table, sine_table):
    half_dim = HD // 2
    turned = jnp.concatenate([-values[..., half_dim:], values[..., :half_dim]], -1)
    return values * cosine_table[:, None, :] + turned * sine_table[:, None, :]


def norm_rate(values):
    return lax.rsqrt(jnp.mean(values * values, -1, keepdims=True) + norm_eps)


def norm_backward(values, rate, gain, grads):
    scaled = grads * gain
    value_grad = rate * scaled - values * rate * rate * rate * jnp.mean(
        values * scaled, -1, keepdims=True
    )
    gain_grad = jnp.sum(grads * values * rate, 0)
    return (value_grad, gain_grad)


def dot(left, right):
    return jnp.dot(left, right, preferred_element_type=jnp.float32)


def dot_back(grads, matrix):
    return lax.dot_general(
        grads, matrix, (((1,), (1,)), ((), ())), preferred_element_type=jnp.float32
    )


def dot_grad(rows, grads):
    return lax.dot_general(
        rows, grads, (((0,), (0,)), ((), ())), preferred_element_type=jnp.float32
    )


def share(values):
    return lax.all_gather(values, "dp", axis=0, tiled=True)


def total(values):
    return lax.psum_scatter(
        values.astype(jnp.bfloat16), "dp", scatter_dimension=0, tiled=True
    ).astype(jnp.float32)


MESH = pl.DeviceIdType.MESH
ANY = pl.BlockSpec(memory_space=pl.ANY)


def flip(index, part):
    chip, core = index // 2, index % 2
    return (chip + part // 2) % 2 * 2 + (core + part % 2) % 2


def remote(source, target, sent, landed, **device):
    return pltpu.make_async_remote_copy(
        src_ref=source,
        dst_ref=target,
        send_sem=sent,
        recv_sem=landed,
        device_id=device,
        device_id_type=MESH,
    )


def greet(line, z, y, j, w):
    barrier = pltpu.get_barrier_semaphore()
    for part in range(1, 4):
        pl.semaphore_signal(barrier, device_id={"dp": flip(j, part)}, device_id_type=MESH)
    pl.semaphore_signal(barrier, device_id={"wide": w + 1 - 2 * y}, device_id_type=MESH)

    @pl.when(z > 0)
    def _():
        pl.semaphore_signal(barrier, device_id={"wide": w - 2}, device_id_type=MESH)

    @pl.when(z < line - 1)
    def _():
        pl.semaphore_signal(barrier, device_id={"wide": w + 2}, device_id_type=MESH)

    ends = jnp.where(z > 0, 1, 0) + jnp.where(z < line - 1, 1, 0)
    pl.semaphore_wait(barrier, 4 + ends)


def each(count, step):
    def body(index, carry):
        step(index)
        return carry

    lax.fori_loop(0, count, body, 0)


def gather_kernel(line, blocks, half, *refs):
    sent_in, down_s, (residual_ref, scale_ref, gain_ref) = refs[:6], refs[6], refs[7:10]
    outs, (qkv_out, attn_out, middle_out, normed_out) = refs[10:15], refs[15:19]
    rows_out, tables_out = refs[19:21]
    rows_v, tables_v, wqkv_v, wout_v, qkv_v, attn_v, part_v, sum_v, normed_v = refs[21:30]
    loc, dp_send, dp_recv, up_sem, dn_sem, y_sem, recv, keep, sum_send, sum_recv, norm_send, norm_recv = refs[30:]
    qkv_s, out_s, ffn_s = sent_in[:3]
    qkv, out, ffn, down, low_out = outs
    row_to = (rows_v, low_out, tables_v)
    f32, low = jnp.float32, jnp.bfloat16
    j, w = lax.axis_index("dp"), lax.axis_index("wide")
    z, y = w // 2, w % 2
    other = w + 1 - 2 * y
    greet(line, z, y, j, w)

    def row_copy(part, place):
        there = row_to[place].at[flip(j, 2) if part == 3 else j]
        return remote(
            there if part == 3 else sent_in[3 + place],
            there,
            dp_send.at[3 + place, part],
            dp_recv.at[3 + place, part],
            dp=flip(j, 1 if part == 3 else part),
        )

    def hand_on(place):
        row_copy(2, place).wait_recv()
        row_copy(3, place).start()

    def weight_copy(part, place):
        peer = flip(j, part)
        target = (qkv.at[:, j, w], out.at[j, w], ffn.at[:, j, w])[place]
        return remote(
            sent_in[place].at[peer], target, dp_send.at[place, part], dp_recv.at[place, part], dp=peer
        )

    copies = [
        pltpu.make_async_copy(qkv_s.at[j], qkv.at[:, j, w], loc.at[0]),
        pltpu.make_async_copy(out_s.at[j], out.at[j, w], loc.at[1]),
        pltpu.make_async_copy(ffn_s.at[j], ffn.at[:, j, w], loc.at[2]),
    ] + [
        pltpu.make_async_copy(sent_in[3 + place], row_to[place].at[j], loc.at[3 + place])
        for place in range(3)
    ] + [pltpu.make_async_copy(down_s, down.at[:, w], loc.at[6])]
    for copy in copies:
        copy.start()
    for place in range(2):
        for part in range(1, 4):
            weight_copy(part, place).start()

    chunks = []
    for part in range(4):
        chunks += [("qkv", part, 0), ("out", part, 0)]
    for part in range(4):
        chunks += [("ffn", part, 0), ("ffn", part, 1)]
    chunks += [("down", slice(0, blocks // 2), 0), ("down", slice(blocks // 2, blocks), 0)]
    count = len(chunks)

    def crosses_first(at):
        name, part, _ = chunks[at]
        return name == "ffn" and part == 0

    def view(at, origin):
        name, part, side = chunks[at]
        if name == "qkv":
            return qkv.at[:, flip(j, part), origin]
        if name == "out":
            return out.at[flip(j, part), origin]
        if name == "down":
            return down.at[part, origin]
        return ffn.at[:, flip(j, part), origin, :, side * half : (side + 1) * half]

    def up(at, origin):
        there = view(at, origin)
        return remote(there, there, up_sem.at[at, origin], recv.at[at, origin], wide=w + 2)

    def dn(at, origin):
        there = view(at, origin)
        return remote(there, there, dn_sem.at[at, origin], recv.at[at, origin], wide=w - 2)

    def across(at, origin):
        there = view(at, origin)
        return remote(there, there, y_sem.at[at, origin], recv.at[at, origin], wide=other)

    def arrived(at, origin):
        across(at, origin).wait_recv()

    start = lambda copy: copy.start()
    finish = lambda copy: copy.wait_send()

    def both_ways(at, origin, act):
        @pl.when(z < line - 1)
        def _():
            act(up(at, origin))

        @pl.when(z > 0)
        def _():
            act(dn(at, origin))

    waited = []

    def own(at):
        name, part, side = chunks[at]
        place = ("qkv", "out", "ffn", "down").index(name)
        if place == 3:
            if part.start == 0:
                copies[6].wait()
        elif (place, part) not in waited:
            waited.append((place, part))
            if part == 0:
                copies[place].wait()
            else:
                weight_copy(part, place).wait_recv()
        across(at, w).start()
        both_ways(at, w, start)

    def turn(at):
        arrived(at, other)
        both_ways(at, other, start)

    def pass_on(at, far, act, waiting):
        first = crosses_first(at)
        for side in (0, 1) if first else (0,):
            column = y if side == 0 else 1 - y

            @pl.when(z >= far)
            def _():
                origin = (z - far) * 2 + column
                if waiting:
                    arrived(at, origin)

                @pl.when(z < line - 1)
                def _():
                    act(up(at, origin))

                if not first:
                    act(across(at, origin))

            @pl.when(z + far < line)
            def _():
                origin = (z + far) * 2 + column
                if waiting:
                    arrived(at, origin)

                @pl.when(z > 0)
                def _():
                    act(dn(at, origin))

                if not first:
                    act(across(at, origin))

    heads = attn_v.shape[2] // HD
    seq = rows_v.shape[1]
    turns = (3, 2, 1, 0)
    attn_chunks = [at for at in range(count) if chunks[at][0] in ("qkv", "out")]
    loads = [
        pltpu.make_async_copy(qkv, wqkv_v, keep.at[0]),
        pltpu.make_async_copy(out, wout_v, keep.at[1]),
    ]

    def weights_ready():
        for at in attn_chunks:
            for far in range(line):
                arrived(at, far * 2 + 1 - y)
        for load in loads:
            load.start()
        for part in (1, 3):
            row_copy(part, 0).wait_recv()
            row_copy(part, 2).wait_recv()
        copies[3].wait()
        copies[5].wait()
        for load in loads:
            load.wait()

    def project(part):
        n = flip(j, part)
        cosine, sine = tables_v[n, 0], tables_v[n, 1]
        weights = wqkv_v[...].reshape(D, wqkv_v.shape[4])
        value = jnp.dot(rows_v[n], weights, preferred_element_type=f32)
        for head in range(heads + 1):
            one = value[:, head * HD : (head + 1) * HD]
            turned = one * cosine + pltpu.roll(one, HD // 2, 1) * sine
            qkv_v[part, :, head * HD : (head + 1) * HD] = turned.astype(low)
        qkv_v[part, :, (heads + 1) * HD :] = value[:, (heads + 1) * HD :].astype(low)

    def attend(part, head):
        query = qkv_v[part, :, head * HD : (head + 1) * HD]
        key = qkv_v[part, :, heads * HD : (heads + 1) * HD]
        scores = lax.dot_general(
            query, key, (((1,), (1,)), ((), ())), preferred_element_type=f32
        ) * HD ** (-0.5)
        row = lax.broadcasted_iota(jnp.int32, (seq, seq), 0)
        column = lax.broadcasted_iota(jnp.int32, (seq, seq), 1)
        scores = jnp.where(row >= column, scores, masked_value)
        weight = jnp.exp(scores - jnp.max(scores, -1, keepdims=True))
        probs = (weight / jnp.sum(weight, -1, keepdims=True)).astype(low)
        value = jnp.dot(probs, qkv_v[part, :, (heads + 1) * HD :], preferred_element_type=f32)
        attn_v[part, :, head * HD : (head + 1) * HD] = value.astype(low)

    def send_sum(part):
        peer = flip(j, 1 if part == 3 else part)
        return remote(
            part_v.at[part], sum_v.at[part], sum_send.at[part], sum_recv.at[part], dp=peer
        )

    def finished(part):
        n = flip(j, part)
        return [
            pltpu.make_async_copy(qkv_v.at[part], qkv_out.at[n], keep.at[2 + part]),
            pltpu.make_async_copy(attn_v.at[part], attn_out.at[n], keep.at[6 + part]),
        ]

    def project_out(part):
        weights = wout_v[...].reshape(heads * HD, D)
        if part == 2:
            send_sum(3).wait_recv()
        for cut in range(4):
            columns = slice(cut * D // 4, (cut + 1) * D // 4)
            value = jnp.dot(attn_v[part], weights[:, columns], preferred_element_type=f32)
            if part == 2:
                value = value + sum_v[3, :, columns].astype(f32)
            part_v[part, :, columns] = value.astype(low)
        if part > 0:
            send_sum(part).start()
        for copy in finished(part):
            copy.start()

    def send_normed(part):
        there = normed_out.at[flip(j, 2) if part == 3 else j]
        return remote(
            there if part == 3 else normed_v,
            there,
            norm_send.at[part],
            norm_recv.at[part],
            dp=flip(j, 1 if part == 3 else part),
        )

    keep_normed = pltpu.make_async_copy(normed_v, normed_out.at[j], keep.at[10])
    keep_rows = pltpu.make_async_copy(rows_v, rows_out, keep.at[11])
    keep_tables = pltpu.make_async_copy(tables_v, tables_out, keep.at[12])

    def normalize():
        for part in (1, 2):
            send_sum(part).wait_recv()
        scale = scale_ref[0, 0]

        def rows(index):
            here = pl.ds(pl.multiple_of(index * 32, 32), 32)
            total_rows = part_v[0, here, :].astype(f32)
            for part in (1, 2):
                total_rows = total_rows + sum_v[part, here, :].astype(f32)
            middle = residual_ref[here, :].astype(f32) + scale * total_rows
            middle_out[here, :] = middle
            rate = lax.rsqrt(jnp.mean(middle * middle, -1, keepdims=True) + norm_eps)
            normed_v[here, :] = (middle * rate * gain_ref[...]).astype(low)

        each(seq // 32, rows)
        for part in (1, 2):
            send_normed(part).start()
        keep_normed.start()
        keep_rows.start()
        keep_tables.start()

    work = [weights_ready]
    for part in turns:
        work.append(functools.partial(project, part))
        for head in range(heads):
            work.append(functools.partial(attend, part, head))
        work.append(functools.partial(project_out, part))
    work.append(normalize)
    ready = attn_chunks[-1] + line

    def compute(pieces):
        for _ in range(pieces):
            if work:
                work.pop(0)()

    for step in range(count + line - 1):
        if step < count:
            own(step)
        for far in range(1, line):
            at = step - far
            if 0 <= at < count:
                if far == 1 and crosses_first(at):
                    turn(at)
                pass_on(at, far, start, True)
                if step >= ready:
                    compute(1)
        if step == 2:
            for part in range(1, 4):
                weight_copy(part, 2).start()
        if step == attn_chunks[-1] - 1:
            for part in (1, 2):
                row_copy(part, 0).start()
                row_copy(part, 2).start()
        if step == ready - 1:
            hand_on(0)
            hand_on(2)
        if step == ready:
            for part in (1, 2):
                row_copy(part, 1).start()
        if step >= ready:
            compute(1)
        if step == count:
            hand_on(1)
    compute(len(work))
    send_normed(2).wait_recv()
    send_normed(3).start()

    for at in range(count):
        if not crosses_first(at) and at not in attn_chunks:
            for far in range(line):
                arrived(at, far * 2 + 1 - y)
    copies[4].wait()
    for place in range(3):
        for part in range(1, 4):
            if place == 1 and part != 2:
                row_copy(part, place).wait()
            else:
                row_copy(part, place).wait_send()
            weight_copy(part, place).wait_send()
    for at in range(count):
        across(at, w).wait_send()
        both_ways(at, w, finish)
        if crosses_first(at):
            both_ways(at, other, finish)
        for far in range(1, line):
            pass_on(at, far, finish, False)
    for part in range(4):
        for copy in finished(part):
            copy.wait()
        if part > 0:
            send_sum(part).wait_send()
            send_normed(part).wait_send()
        if part in (1, 3):
            send_normed(part).wait_recv()
    keep_normed.wait()
    keep_rows.wait()
    keep_tables.wait()


def gather_call(line, qkv_s, out_s, ffn_s, down_s, rows, low_rows, tables, residual, scale, gain):
    low = jnp.bfloat16
    ndp, wide = qkv_s.shape[0], 2 * line
    rm, piece = qkv_s.shape[1], qkv_s.shape[2]
    seq, wq = rows.shape[0], D // ndp

    def shape(*dims, kind=low):
        return jax.ShapeDtypeStruct(dims, kind)

    outs = (
        shape(rm, ndp, wide, piece, qkv_s.shape[3]),
        shape(ndp, wide, piece, out_s.shape[2]),
        shape(rm, ndp, wide, piece, ffn_s.shape[3]),
        shape(down_s.shape[0], wide, piece, down_s.shape[2]),
        shape(ndp, seq, D),
        shape(ndp, seq, qkv_s.shape[3]),
        shape(ndp, seq, wq),
        shape(seq, D, kind=jnp.float32),
        shape(ndp, seq, D),
        shape(ndp, seq, D),
        shape(ndp, *tables.shape, kind=tables.dtype),
    )
    dma = pltpu.SemaphoreType.DMA
    whole = pl.BlockSpec(memory_space=pltpu.VMEM)
    args = (qkv_s, out_s, ffn_s, rows, low_rows, tables, down_s)
    count = 18
    return pl.pallas_call(
        functools.partial(gather_kernel, line, down_s.shape[0], ffn_s.shape[3] // 2),
        out_shape=outs,
        in_specs=[ANY] * len(args) + [whole, pl.BlockSpec(memory_space=pltpu.SMEM), whole],
        out_specs=[ANY] * 7 + [whole] + [ANY] * 3,
        scratch_shapes=[
            pltpu.VMEM((ndp, seq, D), low),
            pltpu.VMEM((ndp, *tables.shape), tables.dtype),
            pltpu.VMEM(outs[0].shape, low),
            pltpu.VMEM(outs[1].shape, low),
            pltpu.VMEM((ndp, seq, qkv_s.shape[3]), low),
            pltpu.VMEM((ndp, seq, wq), low),
            pltpu.VMEM((ndp, seq, D), low),
            pltpu.VMEM((ndp, seq, D), low),
            pltpu.VMEM((seq, D), low),
            dma((7,)),
            dma((6, 4)),
            dma((6, 4)),
        ]
        + [dma((count, wide))] * 4
        + [dma((13,)), dma((4,)), dma((4,)), dma((4,)), dma((4,))],
        compiler_params=pltpu.CompilerParams(
            collective_id=0, has_side_effects=True, vmem_limit_bytes=56 * 1024 * 1024
        ),
        name="gather_weights",
    )(*args, residual, scale, gain)


def scatter_kernel(line, half, *refs):
    (grad_ffn, normed_part, middle_in, cotangent, residual, w_out, w_qkv) = refs[:7]
    packed_in, attn_in, rows_in, tables_in, scale_ref, gains_ref = refs[7:13]
    outs, (input_grad, gain_parts) = refs[13:16], refs[16:18]
    crossed, lined, mine_ffn = refs[18:21], refs[21:24], refs[24]
    early, early_line, early_cross = refs[25:28]
    middle_v, late_v, sum_v, part_v, proj_v, wout_v, wqkv_v, wgrad_v, packed_v, tables_v, out_v, kv_v = refs[28:40]
    y_send, y_recv, load, up_sem, dn_sem, recv, dp_send, dp_recv, loc = refs[40:49]
    keep, two_send, two_recv, proj_send, proj_recv, one_send, one_recv = refs[49:]
    j, w = lax.axis_index("dp"), lax.axis_index("wide")
    z, y = w // 2, w % 2
    other = w + 1 - 2 * y
    greet(line, z, y, j, w)
    f32, low = jnp.float32, jnp.bfloat16
    window = 2

    chunks = [("early", 0, 0), ("early", 0, 1)]
    for part in range(1, 4):
        chunks += [("ffn", part, 0), ("ffn", part, 1)]
    for part in range(4):
        chunks += [("qkv", part, 0)]
    for part in range(4):
        chunks += [("out", part, 0)]
    count = len(chunks)
    names = ("qkv", "out", "ffn")

    def source(at, side):
        name, part, cut = chunks[at]
        if name == "qkv":
            return wgrad_v.at[:, flip(j, part), :, side]
        if name == "out":
            return wout_v.at[pl.ds(flip(j, part), 1), :, side]
        return grad_ffn.at[:, flip(j, part), :, side, :, cut * half : (cut + 1) * half]

    def held(refs, at):
        name, part, cut = chunks[at]
        ref = refs[names.index(name)]
        if name == "ffn":
            return ref.at[part - 1, :, :, :, cut * half : (cut + 1) * half]
        return ref.at[part]

    def own_rows(at):
        name, part, cut = chunks[at]
        if name == "ffn":
            return mine_ffn.at[(2 * part + cut) % (window + 2)]
        return source(at, y)

    def cross(at):
        return remote(
            source(at, 1 - y), held(crossed, at), y_send.at[at], y_recv.at[at], wide=other
        )

    def fetch(at):
        cut = chunks[at][2]
        if chunks[at][0] == "early":
            there = grad_ffn.at[:, j, :, :, :, cut * half : (cut + 1) * half]
            return pltpu.make_async_copy(there, early.at[cut], load.at[at])
        return pltpu.make_async_copy(source(at, y), own_rows(at), load.at[at])

    def fetches(at):
        return chunks[at][0] in ("early", "ffn")

    def cross_early(at):
        cut = chunks[at][2]
        return remote(
            early.at[cut, :, z, 1 - y], early_cross.at[cut], y_send.at[at], y_recv.at[at], wide=other
        )

    def moving(at, dest):
        if chunks[at][0] == "early":
            return early.at[chunks[at][2], :, dest]
        return held(crossed, at).at[:, dest]

    def landing(at, put):
        if chunks[at][0] == "early":
            return early_line.at[chunks[at][2], :, put]
        return held(lined, at).at[:, put]

    def up(at, dest, last):
        put = line if last else dest
        return remote(
            moving(at, dest), landing(at, put), up_sem.at[at, dest], recv.at[at, put], wide=w + 2
        )

    def dn(at, dest):
        return remote(
            moving(at, dest), landing(at, dest), dn_sem.at[at, dest], recv.at[at, dest], wide=w - 2
        )

    def arrived(at, put):
        there = landing(at, put)
        remote(there, there, dn_sem.at[at, 0], recv.at[at, put], wide=other).wait_recv()

    def add(at, dest, puts):
        name, part, cut = chunks[at]
        if name == "early":
            if not puts:
                return

            def rows(index):
                for side in range(2):
                    value = early[cut, index, dest, side].astype(f32)
                    for put in puts:
                        value = value + early_line[cut, index, put, side].astype(f32)
                    early[cut, index, dest, side] = value.astype(low)

            each(early.shape[1], rows)
            return
        here, own, line_in = held(crossed, at), own_rows(at), held(lined, at)

        def rows(index):
            value = here[index, dest].astype(f32) + own[index, dest].astype(f32)
            for put in puts:
                value = value + line_in[index, put].astype(f32)
            here[index, dest] = value.astype(low)

        each(here.shape[0], rows)

    def along(at, act):
        for far in range(line - 1, 0, -1):

            @pl.when(z >= far)
            def _():
                dest = z - far
                if act:

                    @pl.when(z < line - 1)
                    def _():
                        arrived(at, dest)
                        add(at, dest, (dest,))

                    @pl.when(z == line - 1)
                    def _():
                        add(at, dest, ())

                    dn(at, dest).start()
                else:
                    dn(at, dest).wait_send()

            @pl.when(z + far < line)
            def _():
                dest = z + far
                if act:

                    @pl.when(z > 0)
                    def _():
                        arrived(at, dest)
                        add(at, dest, (dest,))

                    @pl.when(z == 0)
                    def _():
                        add(at, dest, ())

                    up(at, dest, far == 1).start()
                else:
                    up(at, dest, far == 1).wait_send()

    def collect(at):
        @pl.when(z == 0)
        def _():
            arrived(at, z)
            add(at, z, (z,))

        @pl.when(z == line - 1)
        def _():
            arrived(at, line)
            add(at, z, (line,))

        @pl.when((z > 0) & (z < line - 1))
        def _():
            arrived(at, z)
            arrived(at, line)
            add(at, z, (z, line))

    def give(at):
        name, part, cut = chunks[at]
        rows = held(crossed, at).at[:, z]
        ref = outs[names.index(name)]
        if name == "out":
            target = ref.at[pl.ds(j, 1)]
        elif name == "qkv":
            target = ref.at[j]
        else:
            target = ref.at[j, :, :, cut * half : (cut + 1) * half]
        if part == 0:
            return pltpu.make_async_copy(rows, target, loc.at[at])
        return remote(rows, target, dp_send.at[at], dp_recv.at[at], dp=flip(j, part))

    def give_early(at):
        cut = chunks[at][2]
        target = outs[2].at[j, :, :, cut * half : (cut + 1) * half]
        return pltpu.make_async_copy(early_cross.at[cut], target, loc.at[at])

    def collect_and_give(at):
        collect(at)
        if chunks[at][0] == "early":
            cross_early(at).start()
        else:
            give(at).start()

    def finish_early(at):
        cut = chunks[at][2]
        cross_early(at).wait_recv()

        def rows(index):
            value = early_cross[cut, index].astype(f32) + early[cut, index, z, y].astype(f32)
            early_cross[cut, index] = value.astype(low)

        each(early.shape[1], rows)
        give_early(at).start()

    heads = out_v.shape[1] // HD
    seq = middle_v.shape[0]
    wide_rows = heads * HD
    loads = [
        pltpu.make_async_copy(middle_in, middle_v, keep.at[0]),
        pltpu.make_async_copy(cotangent, late_v, keep.at[1]),
        pltpu.make_async_copy(normed_part.at[j], part_v.at[0], keep.at[2]),
        pltpu.make_async_copy(normed_part.at[flip(j, 2)], part_v.at[2], keep.at[3]),
        pltpu.make_async_copy(w_out, wout_v, keep.at[4]),
        pltpu.make_async_copy(w_qkv, wqkv_v, keep.at[5]),
        pltpu.make_async_copy(packed_in, packed_v, keep.at[6]),
        pltpu.make_async_copy(tables_in, tables_v, keep.at[7]),
    ]
    load_rows = pltpu.make_async_copy(rows_in, part_v, keep.at[8])
    load_attn = [
        pltpu.make_async_copy(
            attn_in.at[n], late_v.at[:, n * wide_rows : (n + 1) * wide_rows], keep.at[9 + n]
        )
        for n in range(4)
    ]
    load_residual = pltpu.make_async_copy(residual, late_v, keep.at[13])
    keep_input = pltpu.make_async_copy(late_v, input_grad, keep.at[14])

    def send_two(part):
        block = part_v.at[2] if part == 2 else normed_part.at[flip(j, part)]
        peer = flip(j, 1 if part == 3 else part)
        return remote(block, sum_v.at[part - 1], two_send.at[part], two_recv.at[part], dp=peer)

    def send_one(part):
        peer = flip(j, 1 if part == 3 else part)
        return remote(
            part_v.at[part], sum_v.at[part - 1], one_send.at[part], one_recv.at[part], dp=peer
        )

    def send_proj(part):
        there = proj_v.at[flip(j, 2) if part == 3 else j]
        peer = flip(j, 1 if part == 3 else part)
        return remote(there, there, proj_send.at[part], proj_recv.at[part], dp=peer)

    def over_rows(step):
        each(seq // 32, lambda index: step(pl.ds(pl.multiple_of(index * 32, 32), 32)))

    def add_two():
        loads[3].wait()
        send_two(3).wait_recv()

        def rows(here):
            value = part_v[2, here, :].astype(f32) + sum_v[2, here, :].astype(f32)
            part_v[2, here, :] = value.astype(low)

        over_rows(rows)
        send_two(2).start()

    def norm_back(values, grads, gain, gain_row):
        rate = lax.rsqrt(jnp.mean(values * values, -1, keepdims=True) + norm_eps)
        scaled = grads * gain
        mean = jnp.mean(values * scaled, -1, keepdims=True)
        gain_parts[gain_row : gain_row + 1, :] += jnp.sum(grads * values * rate, 0, keepdims=True)
        return rate * scaled - values * rate * rate * rate * mean

    def second_norm():
        for at in (0, 1, 2):
            loads[at].wait()
        send_two(1).wait_recv()
        send_two(2).wait_recv()
        gain_parts[...] = jnp.zeros_like(gain_parts)
        scale = scale_ref[0, 0]

        def rows(here):
            grads = part_v[0, here, :].astype(f32)
            for part in (1, 2):
                grads = grads + sum_v[part - 1, here, :].astype(f32)
            value_grad = norm_back(middle_v[here, :], grads, gains_ref[1:2, :], 1)
            middle_grad = late_v[here, :].astype(f32) + value_grad
            middle_v[here, :] = middle_grad
            proj_v[j, here, :] = (scale * middle_grad).astype(low)

        over_rows(rows)
        send_proj(1).start()
        send_proj(2).start()
        send_two(2).wait_send()
        load_rows.start()
        for copy in load_attn:
            copy.start()

    def hand_on():
        send_proj(2).wait_recv()
        send_proj(3).start()

    def out_back(part):
        if part == 0:
            for at in (4, 5, 6, 7):
                loads[at].wait()
        elif part != 2:
            send_proj(part).wait_recv()
        weights = wout_v[...].reshape(wide_rows, D)
        value = lax.dot_general(
            proj_v[flip(j, part)], weights, (((1,), (1,)), ((), ())), preferred_element_type=f32
        )
        out_v[...] = value.astype(low)

    def turn_back(values, n):
        return values * tables_v[n, 0] - pltpu.roll(values, HD // 2, 1) * tables_v[n, 1]

    def attend_back(part, head):
        n = flip(j, part)
        own = slice(head * HD, (head + 1) * HD)
        query = packed_v[n, :, own]
        key = packed_v[n, :, wide_rows : wide_rows + HD]
        value = packed_v[n, :, wide_rows + HD :]
        grad = out_v[:, own]
        scores = lax.dot_general(
            query, key, (((1,), (1,)), ((), ())), preferred_element_type=f32
        ) * HD ** (-0.5)
        row = lax.broadcasted_iota(jnp.int32, (seq, seq), 0)
        column = lax.broadcasted_iota(jnp.int32, (seq, seq), 1)
        scores = jnp.where(row >= column, scores, masked_value)
        weight = jnp.exp(scores - jnp.max(scores, -1, keepdims=True))
        probs = weight / jnp.sum(weight, -1, keepdims=True)
        prob_grads = lax.dot_general(
            grad, value, (((1,), (1,)), ((), ())), preferred_element_type=f32
        )
        row_dot = jnp.sum(prob_grads * probs, -1, keepdims=True)
        score_low = (probs * (prob_grads - row_dot)).astype(low)
        query_grad = jnp.dot(score_low, key, preferred_element_type=f32) * HD ** (-0.5)
        key_grad = lax.dot_general(
            score_low, query, (((0,), (0,)), ((), ())), preferred_element_type=f32
        ) * HD ** (-0.5)
        value_grad = lax.dot_general(
            probs.astype(low), grad, (((0,), (0,)), ((), ())), preferred_element_type=f32
        )
        if head == 0:
            kv_v[0] = key_grad
            kv_v[1] = value_grad
        else:
            kv_v[0] += key_grad
            kv_v[1] += value_grad
        packed_v[n, :, own] = turn_back(query_grad, n).astype(low)
        if head == heads - 1:
            packed_v[n, :, wide_rows : wide_rows + HD] = turn_back(kv_v[0], n).astype(low)
            packed_v[n, :, wide_rows + HD :] = kv_v[1].astype(low)

    def out_grad(cut):
        if cut == 0:
            for copy in load_attn:
                copy.wait()
        columns = slice(cut * D // 4, (cut + 1) * D // 4)
        rows = jnp.concatenate(
            [late_v[:, n * wide_rows : (n + 1) * wide_rows] for n in range(4)], 0
        )
        grads = proj_v[:, :, columns].reshape(4 * seq, D // 4)
        value = lax.dot_general(rows, grads, (((0,), (0,)), ((), ())), preferred_element_type=f32)
        shape = wout_v.shape[:-1] + (D // 4,)
        wout_v[:, :, :, :, columns] = value.astype(low).reshape(shape)

    def qkv_grad(cut):
        if cut == 0:
            load_rows.wait()
            load_residual.start()
        columns = slice(cut * D // 4, (cut + 1) * D // 4)
        rows = part_v[:, :, columns].reshape(4 * seq, D // 4)
        grads = packed_v[...].reshape(4 * seq, packed_v.shape[2])
        value = lax.dot_general(rows, grads, (((0,), (0,)), ((), ())), preferred_element_type=f32)
        wgrad_v[cut] = value.astype(low).reshape(wgrad_v.shape[1:])

    def rows_back(part):
        n = flip(j, part)
        if part == 2:
            send_one(3).wait_recv()
        for cut in range(4):
            columns = slice(cut * D // 4, (cut + 1) * D // 4)
            weights = wqkv_v[cut].reshape(D // 4, packed_v.shape[2])
            value = lax.dot_general(
                packed_v[n], weights, (((1,), (1,)), ((), ())), preferred_element_type=f32
            )
            if part == 2:
                value = value + sum_v[2, :, columns].astype(f32)
            part_v[part, :, columns] = value.astype(low)
        if part > 0:
            send_one(part).start()

    def first_norm():
        load_residual.wait()
        for part in (1, 2):
            send_one(part).wait_recv()

        def rows(here):
            grads = part_v[0, here, :].astype(f32)
            for part in (1, 2):
                grads = grads + sum_v[part - 1, here, :].astype(f32)
            value_grad = norm_back(late_v[here, :].astype(f32), grads, gains_ref[0:1, :], 0)
            late_v[here, :] = (middle_v[here, :] + value_grad).astype(low)

        over_rows(rows)
        keep_input.start()

    def sequence(part):
        return [functools.partial(out_back, part)] + [
            functools.partial(attend_back, part, head) for head in range(heads)
        ]

    work = {
        1: [second_norm] + sequence(0),
        2: sequence(1) + [hand_on],
        3: sequence(3) + sequence(2),
        4: [functools.partial(out_grad, cut) for cut in range(4)]
        + [functools.partial(qkv_grad, cut) for cut in range(4)],
        7: [functools.partial(rows_back, 3)],
        8: [functools.partial(rows_back, 2)],
        9: [functools.partial(rows_back, 1)],
        10: [functools.partial(rows_back, 0)],
        12: [first_norm],
    }

    late = list(range(2, count))
    send_two(3).start()
    send_two(1).start()
    for at in range(2):
        fetch(at).start()
    for copy in loads:
        copy.start()

    def begin(at):
        if fetches(at):
            fetch(at).start()
        cross(at).start()

    for at in late[:window]:
        begin(at)
    add_two()
    for at in range(2):
        fetch(at).wait()
        along(at, True)
    for step, at in enumerate(late):
        pieces = work.get(step, [])
        cut = (len(pieces) + 1) // 2
        cross(at).wait_send()
        following = late[step + window] if step + window < len(late) else None
        if following is not None and step != 4:
            begin(following)
        cross(at).wait_recv()
        if fetches(at):
            fetch(at).wait()
        along(at, True)
        for piece in pieces[:cut]:
            piece()
        if step < 2:
            collect_and_give(step)
        if step >= 1:
            collect_and_give(late[step - 1])
        for piece in pieces[cut:]:
            piece()
        if step == 4:
            begin(following)
        if step in (3, 4):
            finish_early(step - 3)
    collect_and_give(late[-1])
    for at in range(count):
        along(at, False)
        if chunks[at][0] == "early":
            cross_early(at).wait_send()
            give_early(at).wait()
        else:
            give(at).wait()
    for part in range(1, 4):
        if part != 2:
            send_two(part).wait_send()
        send_proj(part).wait_send()
        send_one(part).wait_send()
    keep_input.wait()


def scatter_call(line, ffn, normed_part, middle, cotangent, residual, w_out, w_qkv, packed, attn, rows, tables, scale, gains):
    low = jnp.bfloat16
    rm, ndp, _, piece, wq = w_qkv.shape
    wf, wo = ffn.shape[4], w_out.shape[3]
    seq = middle.shape[0]
    ffn = ffn.reshape(rm, ndp, line, 2, piece, wf)
    w_out = w_out.reshape(ndp, line, 2, piece, wo)
    w_qkv = w_qkv.reshape(rm, ndp, line, 2, piece, wq)

    def shape(*dims, kind=low):
        return jax.ShapeDtypeStruct(dims, kind)

    outs = (
        shape(ndp, rm, piece, wq),
        shape(ndp, piece, wo),
        shape(ndp, rm, piece, wf),
        shape(seq, D),
        shape(2, D, kind=jnp.float32),
    )

    def held(places):
        return [
            pltpu.VMEM((ndp, rm, places, piece, wq), low),
            pltpu.VMEM((ndp, 1, places, piece, wo), low),
            pltpu.VMEM((ndp - 1, rm, places, piece, wf), low),
        ]

    dma = pltpu.SemaphoreType.DMA
    whole = pl.BlockSpec(memory_space=pltpu.VMEM)
    count = 16
    return pl.pallas_call(
        functools.partial(scatter_kernel, line, wf // 2),
        out_shape=outs,
        in_specs=[ANY] * 11 + [pl.BlockSpec(memory_space=pltpu.SMEM), whole],
        out_specs=[ANY] * 4 + [whole],
        scratch_shapes=held(line)
        + held(line + 1)
        + [
            pltpu.VMEM((4, rm, line, piece, wf // 2), low),
            pltpu.VMEM((2, rm, line, 2, piece, wf // 2), low),
            pltpu.VMEM((2, rm, line + 1, 2, piece, wf // 2), low),
            pltpu.VMEM((2, rm, piece, wf // 2), low),
            pltpu.VMEM((seq, D), jnp.float32),
            pltpu.VMEM((seq, D), low),
            pltpu.VMEM((3, seq, D), low),
            pltpu.VMEM((ndp, seq, D), low),
            pltpu.VMEM((ndp, seq, D), low),
            pltpu.VMEM(w_out.shape, low),
            pltpu.VMEM(w_qkv.shape, low),
            pltpu.VMEM(w_qkv.shape, low),
            pltpu.VMEM(packed.shape, low),
            pltpu.VMEM(tables.shape, tables.dtype),
            pltpu.VMEM((seq, attn.shape[2]), low),
            pltpu.VMEM((2, seq, HD), jnp.float32),
        ]
        + [dma((count,))] * 3
        + [dma((count, line)), dma((count, line)), dma((count, line + 1))]
        + [dma((count,))] * 3
        + [dma((15,))]
        + [dma((4,))] * 6,
        compiler_params=pltpu.CompilerParams(
            collective_id=1, has_side_effects=True, vmem_limit_bytes=60 * 1024 * 1024
        ),
        name="scatter_grads",
    )(ffn, normed_part, middle, cotangent, residual, w_out, w_qkv, packed, attn, rows, tables, scale, gains)


def gains_kernel(line, part_ref, total_ref, dp_parts, wide_parts, dp_send, dp_recv, wide_send, wide_recv):
    j, w = lax.axis_index("dp"), lax.axis_index("wide")
    wide = 2 * line
    barrier = pltpu.get_barrier_semaphore()
    for part in range(1, 4):
        pl.semaphore_signal(barrier, device_id={"dp": flip(j, part)}, device_id_type=MESH)
    for far in range(1, wide):
        pl.semaphore_signal(barrier, device_id={"wide": (w + far) % wide}, device_id_type=MESH)
    pl.semaphore_wait(barrier, 3 + wide - 1)
    copies = [
        remote(part_ref, dp_parts.at[j], dp_send.at[part], dp_recv.at[part], dp=flip(j, part))
        for part in range(1, 4)
    ]
    for copy in copies:
        copy.start()
    dp_parts[j] = part_ref[...]
    for copy in copies:
        copy.wait()
    value = dp_parts[0]
    for rank in range(1, 4):
        value = value + dp_parts[rank]
    wide_parts[w] = value
    copies = [
        remote(
            wide_parts.at[w],
            wide_parts.at[w],
            wide_send.at[far],
            wide_recv.at[far],
            wide=(w + far) % wide,
        )
        for far in range(1, wide)
    ]
    for copy in copies:
        copy.start()
    for copy in copies:
        copy.wait()
    value = wide_parts[0]
    for rank in range(1, wide):
        value = value + wide_parts[rank]
    total_ref[...] = value


def gains_call(line, parts):
    dma = pltpu.SemaphoreType.DMA
    whole = pl.BlockSpec(memory_space=pltpu.VMEM)
    return pl.pallas_call(
        functools.partial(gains_kernel, line),
        out_shape=jax.ShapeDtypeStruct(parts.shape, jnp.float32),
        in_specs=[whole],
        out_specs=whole,
        scratch_shapes=[
            pltpu.VMEM((4, *parts.shape), jnp.float32),
            pltpu.VMEM((2 * line, *parts.shape), jnp.float32),
            dma((4,)),
            dma((4,)),
            dma((2 * line,)),
            dma((2 * line,)),
        ],
        compiler_params=pltpu.CompilerParams(collective_id=2, has_side_effects=True),
        name="sum_gains",
    )(parts)


def attention(tokens, ndp, heads, qkv_rows, tables):
    low = jnp.bfloat16
    seq_len = tokens // ndp
    cosine, sine = tables[:, 0].reshape(tokens, 1, HD), tables[:, 1].reshape(tokens, 1, HD)
    turned = qkv_rows[:, : (heads + 1) * HD].reshape(tokens, heads + 1, HD)
    turned = (turned * cosine + jnp.roll(turned, HD // 2, -1) * sine).astype(low)
    query_rows = turned[:, :heads].reshape(ndp, seq_len, heads, HD)
    key_rows = turned[:, heads].reshape(ndp, seq_len, HD)
    value_rows = qkv_rows[:, (heads + 1) * HD :].astype(low).reshape(ndp, seq_len, HD)
    probs_low = attention_probs(query_rows, key_rows).astype(low)
    out_low = jnp.einsum(
        "ngst,ntd->nsgd", probs_low, value_rows, preferred_element_type=jnp.float32
    ).astype(low)
    packed = jnp.concatenate(
        [turned.reshape(ndp, seq_len, (heads + 1) * HD), value_rows], -1
    )
    return packed, out_low.reshape(ndp, seq_len, heads * HD)


def attention_probs(query_rows, key_rows):
    seq_len = query_rows.shape[1]
    causal = jnp.arange(seq_len)[:, None] >= jnp.arange(seq_len)[None, :]
    scores = jnp.einsum(
        "nsgd,ntd->ngst", query_rows, key_rows, preferred_element_type=jnp.float32
    ) * HD ** (-0.5)
    scores = jnp.where(causal, scores, masked_value)
    row_top = jnp.max(scores, -1, keepdims=True)
    exp_scores = jnp.exp(scores - row_top)
    return exp_scores / jnp.sum(exp_scores, -1, keepdims=True)


def gather_weights(qkv_s, out_s, ffn_s, down_s, rows, low_rows, tables, residual, scale, gain):
    ndp, nwide = lax.axis_size("dp"), lax.axis_size("wide")
    if ndp == 4 and nwide == 8 and qkv_s.shape[2] % 16 == 0:
        return gather_call(
            nwide // 2, qkv_s, out_s, ffn_s, down_s, rows, low_rows, tables, residual, scale, gain
        )

    def spread(values):
        moved = lax.all_to_all(values, "dp", split_axis=0, concat_axis=0, tiled=True)
        return lax.all_gather(moved, "wide", axis=0)

    seq_len = rows.shape[0]
    tokens = ndp * seq_len
    heads = HEADS // ndp
    w_qkv = spread(qkv_s).transpose(2, 1, 0, 3, 4)
    w_out = spread(out_s).transpose(1, 0, 2, 3)
    w_ffn = spread(ffn_s).transpose(2, 1, 0, 3, 4)
    normed_one = lax.all_gather(rows, "dp", axis=0)
    all_tables = lax.all_gather(tables, "dp", axis=0)
    packed, out_low = attention(
        tokens,
        ndp,
        heads,
        dot(normed_one.reshape(tokens, D), w_qkv.reshape(D, -1)),
        all_tables,
    )
    part = dot(out_low.reshape(tokens, heads * HD), w_out.reshape(heads * HD, D))
    middle = residual.astype(jnp.float32) + scale * total(part)
    normed_two = (middle * norm_rate(middle) * gain).astype(jnp.bfloat16)
    return (
        w_qkv,
        w_out,
        w_ffn,
        lax.all_gather(down_s, "wide", axis=1),
        lax.all_gather(low_rows, "dp", axis=0),
        packed,
        out_low,
        middle,
        lax.all_gather(normed_two, "dp", axis=0),
        normed_one,
        all_tables,
    )


def scatter_grads(
    ffn, normed_part, middle, cotangent, residual, w_out, w_qkv, packed, attn, rows, tables, scale, gains
):
    ndp, nwide = lax.axis_size("dp"), lax.axis_size("wide")
    if ndp == 4 and nwide == 8 and ffn.shape[3] % 16 == 0:
        return scatter_call(
            nwide // 2, ffn, normed_part, middle, cotangent, residual,
            w_out, w_qkv, packed, attn, rows, tables, scale, gains,
        )
    low = jnp.bfloat16
    _, seq_len, width = packed.shape
    tokens = ndp * seq_len
    heads = HEADS // ndp
    wq = heads * HD
    score_scale = HD ** (-0.5)
    query_rows = packed[..., :wq].reshape(ndp, seq_len, heads, HD)
    key_rows = packed[..., wq : wq + HD]
    value_rows = packed[..., wq + HD :]
    normed_grad = total(normed_part.reshape(tokens, D))
    middle_local, gain_two = norm_backward(middle, norm_rate(middle), gains[1], normed_grad)
    middle_grad = cotangent.astype(jnp.float32) + middle_local
    proj_low = share((scale * middle_grad).astype(low))
    probs_float = attention_probs(query_rows, key_rows)
    attn_grad = dot_back(proj_low, w_out.reshape(wq, D)).astype(low)
    attn_grad = attn_grad.reshape(ndp, seq_len, heads, HD)
    prob_grads = jnp.einsum(
        "nsgd,ntd->ngst", attn_grad, value_rows, preferred_element_type=jnp.float32
    )
    row_dot = jnp.sum(prob_grads * probs_float, -1, keepdims=True)
    score_low = (probs_float * (prob_grads - row_dot)).astype(low)
    query_grad = (
        jnp.einsum("ngst,ntd->nsgd", score_low, key_rows, preferred_element_type=jnp.float32)
        * score_scale
    )
    key_grad = (
        jnp.einsum("ngst,nsgd->ntd", score_low, query_rows, preferred_element_type=jnp.float32)
        * score_scale
    )
    value_grad = jnp.einsum(
        "ngst,nsgd->ntd",
        probs_float.astype(low),
        attn_grad,
        preferred_element_type=jnp.float32,
    )
    turned = jnp.concatenate([query_grad.reshape(ndp, seq_len, wq), key_grad], -1)
    turned = turned.reshape(tokens, heads + 1, HD)
    cosine = tables[:, 0].reshape(tokens, 1, HD)
    sine = tables[:, 1].reshape(tokens, 1, HD)
    turned = (turned * cosine - jnp.roll(turned, HD // 2, -1) * sine).astype(low)
    qkv_low = jnp.concatenate(
        [turned.reshape(tokens, wq + HD), value_grad.reshape(tokens, HD).astype(low)], 1
    )
    normed_grad = total(dot_back(qkv_low, w_qkv.reshape(D, width)))
    source = residual.astype(jnp.float32)
    input_local, gain_one = norm_backward(source, norm_rate(source), gains[0], normed_grad)

    def collect(values):
        moved = lax.psum_scatter(values, "wide", scatter_dimension=0, tiled=False)
        return lax.all_to_all(moved, "dp", split_axis=0, concat_axis=0, tiled=True)

    grad_qkv = dot_grad(rows.reshape(tokens, D), qkv_low).astype(low).reshape(w_qkv.shape)
    grad_out = dot_grad(attn.reshape(tokens, wq), proj_low).astype(low).reshape(w_out.shape)
    return (
        collect(grad_qkv.transpose(2, 1, 0, 3, 4)),
        collect(grad_out.transpose(1, 0, 2, 3)),
        collect(ffn.transpose(2, 1, 0, 3, 4)),
        (middle_grad + input_local).astype(low),
        jnp.stack([gain_one, gain_two]),
    )


def sum_gains(parts):
    ndp, nwide = lax.axis_size("dp"), lax.axis_size("wide")
    if ndp == 4 and nwide == 8:
        return gains_call(nwide // 2, parts)
    return lax.psum(parts, ("dp", "wide"))


def unfold_rows(rows_ref, flat_ref, piece):
    count = rows_ref.shape[0]
    for first in range(0, count, 8):
        size = min(8, count - first)
        for row in range(piece):
            for group in range(B // 128):
                start = row * B + group * 128
                flat_ref[group, pl.ds(first * piece + row, size, stride=piece), :] = rows_ref[
                    first : first + size, start : start + 128
                ]


def block_places(rm, ndp, rf, part):
    places = []
    for i in range(rm):
        for c in range(ndp):
            places.append((i * ndp + c, 0, 0, (c, i), 0, B))
    for i in range(rm):
        for c in range(ndp):
            places.append((rm * rm + i, c * part, 0, (c, i), B, part))
            places.append((rm * rm + rm + i, c * part, 0, (c, i), B + part, part))
    first = rm * rm + 2 * rm
    for c in range(ndp):
        for i in range(rm):
            places.append((first + c * rm + i, 0, 1, (c,), i * B, B))
    first = first + rm * rm
    for i in range(rm):
        for b in range(rf):
            for c in range(ndp):
                for side in range(2):
                    block = first + side * rm * rf + i * rf + b
                    places.append((block, c * part, 2, (c, i), (side * rf + b) * part, part))
    first = first + 2 * rm * rf
    for b in range(rf):
        for i in range(rm):
            places.append((first + b * rm + i, 0, 3, (b,), i * B, B))
    return places


def pack_kernel(places, piece, rows_ref, *refs):
    pieces, flat_ref = refs[:4], refs[4]
    unfold_rows(rows_ref, flat_ref, piece)
    for block, column, array, lead, start, width in places:
        for offset in range(0, width, 128):
            value = flat_ref[(column + offset) // 128, block * piece : (block + 1) * piece, :]
            there = slice(start + offset, start + offset + 128)
            pieces[array][(*lead, slice(None), there)] = value.astype(jnp.bfloat16)


def slots_kernel(places, piece, slot_ref, *refs):
    pieces, send_ref, blocks_ref = refs[:4], refs[4], refs[5]
    for block, column, array, lead, start, width in places:
        value = pieces[array][(*lead, slice(None), slice(start, start + width))]
        blocks_ref[block, :, column : column + width] = value
    each_slot = send_ref.shape[1]

    def device(index, carry):
        for slot in range(each_slot):
            block = slot_ref[index * each_slot + slot]
            value = blocks_ref[jnp.maximum(block, 0)]
            send_ref[index, slot] = jnp.where(block >= 0, value, jnp.zeros_like(value))
        return carry

    lax.fori_loop(0, send_ref.shape[0], device, 0)


def precondition_kernel(scale_ref, grad_ref, left_ref, right_ref, step_ref):
    low, f32 = jnp.bfloat16, jnp.float32
    scale = scale_ref[pl.program_id(0)]
    grad = grad_ref[:, 0].reshape(B, B)
    value = jnp.dot(left_ref[0].astype(low), grad, preferred_element_type=f32)
    value = jnp.dot(value.astype(low), right_ref[0].astype(low), preferred_element_type=f32)
    rate = lax.rsqrt(jnp.mean(value * value, keepdims=True) + scale_eps)
    value = value * (weight_rate * scale * rate)
    step_ref[:, 0] = value.astype(low).reshape(step_ref.shape[0], step_ref.shape[2], B)


def update_kernel(piece, slot_ref, steps_ref, master_ref, out_ref, flat_ref):
    each_slot = steps_ref.shape[1]
    size = master_ref.shape[0]
    last = slot_ref.shape[0] - 1
    for index in range(size):
        slot = slot_ref[jnp.minimum(pl.program_id(0) * size + index, last)]
        value = steps_ref[slot // each_slot, slot % each_slot].astype(jnp.float32)
        for group in range(B // 128):
            flat_ref[group, index * piece : (index + 1) * piece, :] = value[
                :, group * 128 : (group + 1) * 128
            ]
    for row in range(piece):
        for group in range(B // 128):
            step = flat_ref[group, pl.ds(row, size, stride=piece), :]
            start = row * B + group * 128
            columns = slice(start, start + 128)
            out_ref[:, columns] = (1.0 - weight_decay) * master_ref[:, columns] - step


def vmem_call(kernel, outs, args, scratch=(), prefetch=0, name=None):
    whole = pl.BlockSpec(memory_space=pltpu.VMEM)
    small = pl.BlockSpec(memory_space=pltpu.SMEM)
    return pl.pallas_call(
        kernel,
        out_shape=outs,
        in_specs=[small] * prefetch + [whole] * (len(args) - prefetch),
        out_specs=jax.tree.map(lambda _: whole, outs),
        scratch_shapes=list(scratch),
        compiler_params=pltpu.CompilerParams(vmem_limit_bytes=48 * 1024 * 1024),
        name=name,
    )(*args)


def pack_call(rows, ndp):
    rm, rf, part, piece = D // B, FF // B, B // ndp, rows.shape[1] // B
    low = jnp.bfloat16
    outs = (
        jax.ShapeDtypeStruct((ndp, rm, piece, B + 2 * part), low),
        jax.ShapeDtypeStruct((ndp, piece, D), low),
        jax.ShapeDtypeStruct((ndp, rm, piece, 2 * rf * part), low),
        jax.ShapeDtypeStruct((rf, piece, D), low),
    )
    return vmem_call(
        functools.partial(pack_kernel, block_places(rm, ndp, rf, part), piece),
        outs,
        (rows,),
        [pltpu.VMEM((B // 128, NBLK * piece, 128), jnp.float32)],
        name="pack",
    )


def slots_call(slot_block, pieces, devices):
    ndp, rm, piece, _ = pieces[0].shape
    rf = pieces[3].shape[0]
    low = jnp.bfloat16
    outs = (
        jax.ShapeDtypeStruct((devices, slot_block.shape[0] // devices, piece, B), low),
        jax.ShapeDtypeStruct((NBLK, piece, B), low),
    )
    return vmem_call(
        functools.partial(slots_kernel, block_places(rm, ndp, rf, B // ndp), piece),
        outs,
        (slot_block, *pieces),
        prefetch=1,
        name="to_slots",
    )


def precondition_call(scale, owned, left, right):
    devices, slots, piece, _ = owned.shape
    block = pl.BlockSpec((devices, 1, piece, B), lambda n: (0, n, 0, 0))
    square = pl.BlockSpec((1, B, B), lambda n: (n, 0, 0))
    return pl.pallas_call(
        precondition_kernel,
        out_shape=jax.ShapeDtypeStruct(owned.shape, jnp.bfloat16),
        grid=(slots,),
        in_specs=[pl.BlockSpec(memory_space=pltpu.SMEM), block, square, square],
        out_specs=block,
        compiler_params=pltpu.CompilerParams(vmem_limit_bytes=48 * 1024 * 1024),
        name="precondition",
    )(scale, owned, left, right)


def update_call(block_slot, returned, master):
    count, width = master.shape
    size = 16
    rows = pl.BlockSpec((size, width), lambda step: (step, 0))
    return pl.pallas_call(
        functools.partial(update_kernel, width // B),
        out_shape=jax.ShapeDtypeStruct(master.shape, jnp.float32),
        grid=(pl.cdiv(count, size),),
        in_specs=[
            pl.BlockSpec(memory_space=pltpu.SMEM),
            pl.BlockSpec(memory_space=pltpu.VMEM),
            rows,
        ],
        out_specs=rows,
        scratch_shapes=[pltpu.VMEM((B // 128, size * width // B, 128), jnp.float32)],
        compiler_params=pltpu.CompilerParams(vmem_limit_bytes=48 * 1024 * 1024),
        name="update",
    )(block_slot, returned, master)


def pack(master_weights, ndp):
    low = jnp.bfloat16
    piece = master_weights.shape[1] // B
    if ndp == 4 and piece % 16 == 0:
        return pack_call(master_weights, ndp)
    rm, rf, part = D // B, FF // B, B // ndp
    first_key = rm * rm
    first_value = first_key + rm
    first_out = first_value + rm
    first_gate = first_out + rm * rm
    first_up = first_gate + rm * rf
    first_down = first_up + rm * rf
    mine = master_weights.astype(low).reshape(NBLK, piece, B)

    def cut_columns(first, blocks):
        own = mine[first : first + rm * blocks].reshape(rm, blocks, piece, ndp, part)
        return own.transpose(3, 0, 2, 1, 4).reshape(ndp, rm, piece, blocks * part)

    qkv_s = jnp.concatenate(
        [
            mine[:first_key].reshape(rm, ndp, piece, B).transpose(1, 0, 2, 3),
            cut_columns(first_key, 1),
            cut_columns(first_value, 1),
        ],
        -1,
    )
    out_s = (
        mine[first_out:first_gate].reshape(ndp, rm, piece, B).transpose(0, 2, 1, 3)
    ).reshape(ndp, piece, D)
    ffn_s = jnp.concatenate([cut_columns(first_gate, rf), cut_columns(first_up, rf)], -1)
    down_s = mine[first_down:].reshape(rf, rm, piece, B).transpose(0, 2, 1, 3)
    down_s = down_s.reshape(rf, piece, D)
    return qkv_s, out_s, ffn_s, down_s


def to_slots(slot_block, pieces, devices):
    ndp, rm, piece, _ = pieces[0].shape
    if ndp == 4 and piece % 16 == 0:
        return slots_call(slot_block, pieces, devices)
    grad_qkv, grad_out, grad_ffn, grad_down = pieces
    low = jnp.bfloat16
    rf = grad_down.shape[0]
    part = B // ndp
    wq = B

    def join_columns(cut, blocks):
        own = cut.reshape(ndp, rm, piece, blocks, part).transpose(1, 3, 2, 0, 4)
        return own.reshape(rm * blocks, piece, B)

    grad_rows = jnp.concatenate(
        [
            grad_qkv[..., :wq].transpose(1, 0, 2, 3).reshape(rm * ndp, piece, B),
            join_columns(grad_qkv[..., wq : wq + part], 1),
            join_columns(grad_qkv[..., wq + part :], 1),
            grad_out.reshape(ndp, piece, rm, B).transpose(0, 2, 1, 3).reshape(ndp * rm, piece, B),
            join_columns(grad_ffn[..., : rf * part], rf),
            join_columns(grad_ffn[..., rf * part :], rf),
            grad_down.reshape(rf, piece, rm, B).transpose(0, 2, 1, 3).reshape(rf * rm, piece, B),
        ],
        0,
    )
    send_rows = jnp.where(
        (slot_block >= 0)[:, None, None],
        grad_rows[jnp.maximum(slot_block, 0)],
        jnp.zeros((), low),
    )
    return send_rows.reshape(devices, -1, piece, B), grad_rows


def precondition(scale, owned, left, right):
    low = jnp.bfloat16
    devices, slots, piece, _ = owned.shape
    if piece % 16 == 0:
        return precondition_call(scale, owned, left, right)
    blocks = owned.transpose(1, 0, 2, 3).reshape(slots, B, B)
    value = jnp.einsum("nij,njk->nik", left.astype(low), blocks, preferred_element_type=jnp.float32)
    value = jnp.einsum(
        "nij,njk->nik", value.astype(low), right.astype(low), preferred_element_type=jnp.float32
    )
    rate = lax.rsqrt(jnp.mean(value * value, axis=(1, 2), keepdims=True) + scale_eps)
    steps = weight_rate * scale[:, None, None] * value * rate
    return steps.astype(low).reshape(slots, devices, piece, B).transpose(1, 0, 2, 3)


def update(block_slot, returned, master_weights):
    devices, slots, piece, _ = returned.shape
    if piece % 16 == 0:
        return update_call(block_slot, returned, master_weights)
    steps = returned.reshape(devices * slots, piece, B)[block_slot].astype(jnp.float32)
    return (1.0 - weight_decay) * master_weights - steps.reshape(NBLK, piece * B)


def local(
    inputs,
    cotangent,
    keep_mask,
    positions,
    master_weights,
    gains,
    gain_moments,
    block_slot,
    stat_left,
    stat_right,
    root_left,
    root_right,
):
    low = jnp.bfloat16
    ndp = lax.axis_size("dp")
    nwide = lax.axis_size("wide")
    rm = D // B
    rf = FF // B
    seq_len = inputs.shape[1]
    tokens = ndp * seq_len
    slot_dev = stat_left.shape[0]
    slots_all = slot_dev * ndp * nwide
    piece = master_weights.shape[1] // B
    part = B // ndp

    residual = inputs[0].astype(jnp.float32)
    branch_scale = keep_mask[0].astype(jnp.float32) / keep_rate()
    out_grad_f = cotangent[0].astype(jnp.float32)
    rate_one = norm_rate(residual)

    qkv_s, out_s, ffn_s, down_s = pack(master_weights, ndp)
    cosine_table, sine_table = rope_tables(positions[0])
    signs = jnp.where(jnp.arange(HD) < HD // 2, -1.0, 1.0)
    (
        w_qkv,
        w_out,
        w_ffn,
        w_down,
        down_low,
        packed,
        out_low,
        middle,
        normed_two,
        normed_one,
        all_tables,
    ) = gather_weights(
        qkv_s,
        out_s,
        ffn_s,
        down_s,
        (residual * rate_one * gains[0]).astype(low),
        (branch_scale * out_grad_f).astype(low),
        jnp.stack([cosine_table, sine_table * signs]),
        inputs[0],
        branch_scale.reshape(1, 1),
        gains[1:],
    )
    w_ffn = w_ffn.reshape(D, 2 * rf * part)
    w_down = w_down.reshape(rf * part, D)
    normed_two = normed_two.reshape(tokens, D)
    down_low = down_low.reshape(tokens, D)

    ffn_rows = dot(normed_two, w_ffn)
    gate_rows, up_rows = ffn_rows[:, : rf * part], ffn_rows[:, rf * part :]
    sigmoid_gate = jax.nn.sigmoid(gate_rows)
    hidden = (gate_rows * sigmoid_gate * up_rows).astype(low)
    hidden_grad = dot_back(down_low, w_down)
    gate_low = (
        hidden_grad * up_rows * sigmoid_gate * (1.0 + gate_rows * (1.0 - sigmoid_gate))
    ).astype(low)
    up_low = (hidden_grad * gate_rows * sigmoid_gate).astype(low)
    ffn_low = jnp.concatenate([gate_low, up_low], 1)
    down_part = dot_grad(hidden, down_low).astype(low).reshape(rf, nwide * piece, D)
    down_part, w_ffn, normed_two = lax.optimization_barrier((down_part, w_ffn, normed_two))
    grad_down = lax.psum_scatter(down_part, "wide", scatter_dimension=1, tiled=True)
    result = middle + branch_scale * total(dot(hidden, w_down))
    output = result.astype(low)[None]
    grad_qkv, grad_out, grad_ffn, input_grad, gain_parts = scatter_grads(
        dot_grad(normed_two, ffn_low).astype(low).reshape(rm, ndp, nwide, piece, 2 * rf * part),
        dot_back(ffn_low, w_ffn).astype(low).reshape(ndp, seq_len, D),
        middle,
        cotangent[0],
        inputs[0],
        w_out,
        w_qkv,
        packed,
        out_low,
        normed_one,
        all_tables,
        branch_scale.reshape(1, 1),
        gains,
    )
    input_grad = input_grad[None]
    gain_grads = sum_gains(gain_parts)
    new_gain_moments = stat_decay * gain_moments + (1.0 - stat_decay) * gain_grads * gain_grads
    new_gains = gains - gain_rate * gain_grads / (jnp.sqrt(new_gain_moments) + adam_eps)

    slot_block = jnp.full((slots_all,), -1, jnp.int32).at[block_slot].set(jnp.arange(NBLK))
    send_rows, grad_rows = to_slots(
        slot_block, (grad_qkv, grad_out, grad_ffn, grad_down), ndp * nwide
    )
    grad_local = grad_rows.reshape(NBLK, piece * B).astype(jnp.float32)
    owned = lax.all_to_all(send_rows, ("dp", "wide"), split_axis=0, concat_axis=0, tiled=True)
    own_blocks = lax.dynamic_slice_in_dim(
        slot_block, lax.axis_index(("dp", "wide")) * slot_dev, slot_dev
    )
    own_scale = jnp.where(own_blocks >= 0, block_scale(jnp.maximum(own_blocks, 0)), 0.0)
    steps_local = precondition(own_scale, owned, root_left, root_right)
    steps_local, gain_grads = lax.optimization_barrier((steps_local, gain_grads))
    returned = lax.all_to_all(steps_local, ("dp", "wide"), split_axis=0, concat_axis=0, tiled=True)
    blocks = owned.transpose(1, 0, 2, 3).reshape(slot_dev, B, B)
    new_left = stat_decay * stat_left + (1.0 - stat_decay) * jnp.einsum(
        "nij,nkj->nik", blocks, blocks, preferred_element_type=jnp.float32
    )
    new_right = stat_decay * stat_right + (1.0 - stat_decay) * jnp.einsum(
        "nji,njk->nik", blocks, blocks, preferred_element_type=jnp.float32
    )
    new_weights = update(block_slot, returned, master_weights)
    return (
        output,
        input_grad,
        grad_local,
        new_left,
        new_right,
        new_weights,
        gain_grads,
        new_gain_moments,
        new_gains,
    )


def solution(mesh):
    placed = (
        P(("dp", "wide"), None, None),
        P(("dp", "wide"), None, None),
        P(("dp", "wide")),
        P(("dp", "wide"), None),
        P(None, ("dp", "wide")),
        P(),
        P(),
        P(),
        P(("dp", "wide"), None, None),
        P(("dp", "wide"), None, None),
        P(("dp", "wide"), None, None),
        P(("dp", "wide"), None, None),
    )
    return jax.shard_map(
        local,
        mesh=mesh,
        in_specs=placed,
        out_specs=(
            P(("dp", "wide"), None, None),
            P(("dp", "wide"), None, None),
            P(None, ("dp", "wide")),
            P(("dp", "wide"), None, None),
            P(("dp", "wide"), None, None),
            P(None, ("dp", "wide")),
            P(),
            P(),
            P(),
        ),
        check_vma=False,
    )
```

```python
import functools

import jax
import jax.numpy as jnp
from jax import lax
from jax.experimental import pallas as pl
from jax.experimental.pallas import tpu as pltpu
from jax.sharding import PartitionSpec as P

D = 2048
HEADS = 16
HD = 128
KVH = 4
FF = 5632
B = 512
SEQ = 256
LAYER = 16
DEPTH = 24
STEP = 10
RAMP = 20
NBLK = 172


norm_eps = 1e-05
stat_decay = 0.95
weight_rate = 0.5
weight_decay = 0.001
gain_rate = 0.05
adam_eps = 1e-08
rope_base = 10000.0
scale_eps = 1e-06
masked_value = -1e30


def keep_rate():
    return 1.0 - 0.2 * (2.0 ** (LAYER / (DEPTH - 1)) - 1.0) * min(STEP / RAMP, 1.0)


def block_shapes():
    rows_model = D // B
    rows_kv = KVH * HD // B
    rows_ff = FF // B
    return [
        (rows_model, rows_model),
        (rows_model, rows_kv),
        (rows_model, rows_kv),
        (rows_model, rows_model),
        (rows_model, rows_ff),
        (rows_model, rows_ff),
        (rows_ff, rows_model),
    ]


def block_scale(block_index):
    bounds = []
    running = 0
    for row_blocks, col_blocks in block_shapes():
        running = running + row_blocks * col_blocks
        bounds.append(running)
    plain_scale = D ** (-0.5)
    out_scale = (SEQ / 8.0) ** 0.5 * D ** (-0.5)
    return jnp.where(
        block_index < bounds[2],
        plain_scale,
        jnp.where(
            block_index < bounds[3],
            out_scale,
            jnp.where(block_index < bounds[5], plain_scale, FF ** (-0.5)),
        ),
    ).astype(jnp.float32)


def rope_tables(position):
    half_dim = HD // 2
    freqs = rope_base ** (-(jnp.arange(half_dim).astype(jnp.float32) * 2.0 / HD))
    angles = position.astype(jnp.float32)[:, None] * freqs[None, :]
    cosine_table = jnp.concatenate([jnp.cos(angles), jnp.cos(angles)], -1)
    sine_table = jnp.concatenate([jnp.sin(angles), jnp.sin(angles)], -1)
    return (cosine_table, sine_table)


def rotate(values, cosine_table, sine_table):
    half_dim = HD // 2
    turned = jnp.concatenate([-values[..., half_dim:], values[..., :half_dim]], -1)
    return values * cosine_table[:, None, :] + turned * sine_table[:, None, :]


def norm_rate(values):
    return lax.rsqrt(jnp.mean(values * values, -1, keepdims=True) + norm_eps)


def norm_backward(values, rate, gain, grads):
    scaled = grads * gain
    value_grad = rate * scaled - values * rate * rate * rate * jnp.mean(
        values * scaled, -1, keepdims=True
    )
    gain_grad = jnp.sum(grads * values * rate, 0)
    return (value_grad, gain_grad)


def dot(left, right):
    return jnp.dot(left, right, preferred_element_type=jnp.float32)


def dot_back(grads, matrix):
    return lax.dot_general(
        grads, matrix, (((1,), (1,)), ((), ())), preferred_element_type=jnp.float32
    )


def dot_grad(rows, grads):
    return lax.dot_general(
        rows, grads, (((0,), (0,)), ((), ())), preferred_element_type=jnp.float32
    )


def share(values):
    return lax.all_gather(values, "dp", axis=0, tiled=True)


def total(values):
    return lax.psum_scatter(
        values.astype(jnp.bfloat16), "dp", scatter_dimension=0, tiled=True
    ).astype(jnp.float32)


MESH = pl.DeviceIdType.MESH
ANY = pl.BlockSpec(memory_space=pl.ANY)


def flip(index, part):
    chip, core = index // 2, index % 2
    return (chip + part // 2) % 2 * 2 + (core + part % 2) % 2


def remote(source, target, sent, landed, **device):
    return pltpu.make_async_remote_copy(
        src_ref=source,
        dst_ref=target,
        send_sem=sent,
        recv_sem=landed,
        device_id=device,
        device_id_type=MESH,
    )


def greet(line, z, y, j, w):
    barrier = pltpu.get_barrier_semaphore()
    for part in range(1, 4):
        pl.semaphore_signal(barrier, device_id={"dp": flip(j, part)}, device_id_type=MESH)
    pl.semaphore_signal(barrier, device_id={"wide": w + 1 - 2 * y}, device_id_type=MESH)

    @pl.when(z > 0)
    def _():
        pl.semaphore_signal(barrier, device_id={"wide": w - 2}, device_id_type=MESH)

    @pl.when(z < line - 1)
    def _():
        pl.semaphore_signal(barrier, device_id={"wide": w + 2}, device_id_type=MESH)

    ends = jnp.where(z > 0, 1, 0) + jnp.where(z < line - 1, 1, 0)
    pl.semaphore_wait(barrier, 4 + ends)


def each(count, step):
    def body(index, carry):
        step(index)
        return carry

    lax.fori_loop(0, count, body, 0)


def gather_kernel(line, blocks, half, *refs):
    sent_in, down_s, (residual_ref, scale_ref, gain_ref) = refs[:6], refs[6], refs[7:10]
    outs, (qkv_out, attn_out, middle_out, normed_out) = refs[10:15], refs[15:19]
    rows_out, tables_out = refs[19:21]
    rows_v, tables_v, wqkv_v, wout_v, qkv_v, attn_v, part_v, sum_v, normed_v = refs[21:30]
    loc, dp_send, dp_recv, up_sem, dn_sem, y_sem, recv, keep, sum_send, sum_recv, norm_send, norm_recv = refs[30:]
    qkv_s, out_s, ffn_s = sent_in[:3]
    qkv, out, ffn, down, low_out = outs
    row_to = (rows_v, low_out, tables_v)
    f32, low = jnp.float32, jnp.bfloat16
    j, w = lax.axis_index("dp"), lax.axis_index("wide")
    z, y = w // 2, w % 2
    other = w + 1 - 2 * y
    greet(line, z, y, j, w)

    def row_copy(part, place):
        there = row_to[place].at[flip(j, 2) if part == 3 else j]
        return remote(
            there if part == 3 else sent_in[3 + place],
            there,
            dp_send.at[3 + place, part],
            dp_recv.at[3 + place, part],
            dp=flip(j, 1 if part == 3 else part),
        )

    def hand_on(place):
        row_copy(2, place).wait_recv()
        row_copy(3, place).start()

    def weight_copy(part, place):
        peer = flip(j, part)
        target = (qkv.at[:, j, w], out.at[j, w], ffn.at[:, j, w])[place]
        return remote(
            sent_in[place].at[peer], target, dp_send.at[place, part], dp_recv.at[place, part], dp=peer
        )

    copies = [
        pltpu.make_async_copy(qkv_s.at[j], qkv.at[:, j, w], loc.at[0]),
        pltpu.make_async_copy(out_s.at[j], out.at[j, w], loc.at[1]),
        pltpu.make_async_copy(ffn_s.at[j], ffn.at[:, j, w], loc.at[2]),
    ] + [
        pltpu.make_async_copy(sent_in[3 + place], row_to[place].at[j], loc.at[3 + place])
        for place in range(3)
    ] + [pltpu.make_async_copy(down_s, down.at[:, w], loc.at[6])]
    for copy in copies:
        copy.start()
    for place in range(2):
        for part in range(1, 4):
            weight_copy(part, place).start()

    chunks = []
    for part in range(4):
        chunks += [("qkv", part, 0), ("out", part, 0)]
    for part in range(4):
        chunks += [("ffn", part, 0), ("ffn", part, 1)]
    chunks += [("down", slice(0, blocks // 2), 0), ("down", slice(blocks // 2, blocks), 0)]
    count = len(chunks)

    def crosses_first(at):
        name, part, _ = chunks[at]
        return name == "ffn" and part == 0

    def view(at, origin):
        name, part, side = chunks[at]
        if name == "qkv":
            return qkv.at[:, flip(j, part), origin]
        if name == "out":
            return out.at[flip(j, part), origin]
        if name == "down":
            return down.at[part, origin]
        return ffn.at[:, flip(j, part), origin, :, side * half : (side + 1) * half]

    def up(at, origin):
        there = view(at, origin)
        return remote(there, there, up_sem.at[at, origin], recv.at[at, origin], wide=w + 2)

    def dn(at, origin):
        there = view(at, origin)
        return remote(there, there, dn_sem.at[at, origin], recv.at[at, origin], wide=w - 2)

    def across(at, origin):
        there = view(at, origin)
        return remote(there, there, y_sem.at[at, origin], recv.at[at, origin], wide=other)

    def arrived(at, origin):
        across(at, origin).wait_recv()

    start = lambda copy: copy.start()
    finish = lambda copy: copy.wait_send()

    def both_ways(at, origin, act):
        @pl.when(z < line - 1)
        def _():
            act(up(at, origin))

        @pl.when(z > 0)
        def _():
            act(dn(at, origin))

    waited = []

    def own(at):
        name, part, side = chunks[at]
        place = ("qkv", "out", "ffn", "down").index(name)
        if place == 3:
            if part.start == 0:
                copies[6].wait()
        elif (place, part) not in waited:
            waited.append((place, part))
            if part == 0:
                copies[place].wait()
            else:
                weight_copy(part, place).wait_recv()
        across(at, w).start()
        both_ways(at, w, start)

    def turn(at):
        arrived(at, other)
        both_ways(at, other, start)

    def pass_on(at, far, act, waiting):
        first = crosses_first(at)
        for side in (0, 1) if first else (0,):
            column = y if side == 0 else 1 - y

            @pl.when(z >= far)
            def _():
                origin = (z - far) * 2 + column
                if waiting:
                    arrived(at, origin)

                @pl.when(z < line - 1)
                def _():
                    act(up(at, origin))

                if not first:
                    act(across(at, origin))

            @pl.when(z + far < line)
            def _():
                origin = (z + far) * 2 + column
                if waiting:
                    arrived(at, origin)

                @pl.when(z > 0)
                def _():
                    act(dn(at, origin))

                if not first:
                    act(across(at, origin))

    heads = attn_v.shape[2] // HD
    seq = rows_v.shape[1]
    turns = (3, 2, 1, 0)
    attn_chunks = [at for at in range(count) if chunks[at][0] in ("qkv", "out")]
    loads = [
        pltpu.make_async_copy(qkv, wqkv_v, keep.at[0]),
        pltpu.make_async_copy(out, wout_v, keep.at[1]),
    ]

    def weights_ready():
        for at in attn_chunks:
            for far in range(line):
                arrived(at, far * 2 + 1 - y)
        for load in loads:
            load.start()
        for part in (1, 3):
            row_copy(part, 0).wait_recv()
            row_copy(part, 2).wait_recv()
        copies[3].wait()
        copies[5].wait()
        for load in loads:
            load.wait()

    def project(part):
        n = flip(j, part)
        cosine, sine = tables_v[n, 0], tables_v[n, 1]
        weights = wqkv_v[...].reshape(D, wqkv_v.shape[4])
        value = jnp.dot(rows_v[n], weights, preferred_element_type=f32)
        for head in range(heads + 1):
            one = value[:, head * HD : (head + 1) * HD]
            turned = one * cosine + pltpu.roll(one, HD // 2, 1) * sine
            qkv_v[part, :, head * HD : (head + 1) * HD] = turned.astype(low)
        qkv_v[part, :, (heads + 1) * HD :] = value[:, (heads + 1) * HD :].astype(low)

    def attend(part, head):
        query = qkv_v[part, :, head * HD : (head + 1) * HD]
        key = qkv_v[part, :, heads * HD : (heads + 1) * HD]
        scores = lax.dot_general(
            query, key, (((1,), (1,)), ((), ())), preferred_element_type=f32
        ) * HD ** (-0.5)
        row = lax.broadcasted_iota(jnp.int32, (seq, seq), 0)
        column = lax.broadcasted_iota(jnp.int32, (seq, seq), 1)
        scores = jnp.where(row >= column, scores, masked_value)
        weight = jnp.exp(scores - jnp.max(scores, -1, keepdims=True))
        probs = (weight / jnp.sum(weight, -1, keepdims=True)).astype(low)
        value = jnp.dot(probs, qkv_v[part, :, (heads + 1) * HD :], preferred_element_type=f32)
        attn_v[part, :, head * HD : (head + 1) * HD] = value.astype(low)

    def send_sum(part):
        peer = flip(j, 1 if part == 3 else part)
        return remote(
            part_v.at[part], sum_v.at[part], sum_send.at[part], sum_recv.at[part], dp=peer
        )

    def finished(part):
        n = flip(j, part)
        return [
            pltpu.make_async_copy(qkv_v.at[part], qkv_out.at[n], keep.at[2 + part]),
            pltpu.make_async_copy(attn_v.at[part], attn_out.at[n], keep.at[6 + part]),
        ]

    def project_out(part):
        weights = wout_v[...].reshape(heads * HD, D)
        if part == 2:
            send_sum(3).wait_recv()
        for cut in range(4):
            columns = slice(cut * D // 4, (cut + 1) * D // 4)
            value = jnp.dot(attn_v[part], weights[:, columns], preferred_element_type=f32)
            if part == 2:
                value = value + sum_v[3, :, columns].astype(f32)
            part_v[part, :, columns] = value.astype(low)
        if part > 0:
            send_sum(part).start()
        for copy in finished(part):
            copy.start()

    def send_normed(part):
        there = normed_out.at[flip(j, 2) if part == 3 else j]
        return remote(
            there if part == 3 else normed_v,
            there,
            norm_send.at[part],
            norm_recv.at[part],
            dp=flip(j, 1 if part == 3 else part),
        )

    keep_normed = pltpu.make_async_copy(normed_v, normed_out.at[j], keep.at[10])
    keep_rows = pltpu.make_async_copy(rows_v, rows_out, keep.at[11])
    keep_tables = pltpu.make_async_copy(tables_v, tables_out, keep.at[12])

    def normalize():
        for part in (1, 2):
            send_sum(part).wait_recv()
        scale = scale_ref[0, 0]

        def rows(index):
            here = pl.ds(pl.multiple_of(index * 32, 32), 32)
            total_rows = part_v[0, here, :].astype(f32)
            for part in (1, 2):
                total_rows = total_rows + sum_v[part, here, :].astype(f32)
            middle = residual_ref[here, :].astype(f32) + scale * total_rows
            middle_out[here, :] = middle
            rate = lax.rsqrt(jnp.mean(middle * middle, -1, keepdims=True) + norm_eps)
            normed_v[here, :] = (middle * rate * gain_ref[...]).astype(low)

        each(seq // 32, rows)
        for part in (1, 2):
            send_normed(part).start()
        keep_normed.start()
        keep_rows.start()
        keep_tables.start()

    work = [weights_ready]
    for part in turns:
        work.append(functools.partial(project, part))
        for head in range(heads):
            work.append(functools.partial(attend, part, head))
        work.append(functools.partial(project_out, part))
    work.append(normalize)
    ready = attn_chunks[-1] + line

    def compute(pieces):
        for _ in range(pieces):
            if work:
                work.pop(0)()

    for step in range(count + line - 1):
        if step < count:
            own(step)
        for far in range(1, line):
            at = step - far
            if 0 <= at < count:
                if far == 1 and crosses_first(at):
                    turn(at)
                pass_on(at, far, start, True)
                if step >= ready:
                    compute(1)
        if step == 2:
            for part in range(1, 4):
                weight_copy(part, 2).start()
        if step == attn_chunks[-1] - 1:
            for part in (1, 2):
                row_copy(part, 0).start()
                row_copy(part, 2).start()
        if step == ready - 1:
            hand_on(0)
            hand_on(2)
        if step == ready:
            for part in (1, 2):
                row_copy(part, 1).start()
        if step >= ready:
            compute(1)
        if step == count:
            hand_on(1)
    compute(len(work))
    send_normed(2).wait_recv()
    send_normed(3).start()

    for at in range(count):
        if not crosses_first(at) and at not in attn_chunks:
            for far in range(line):
                arrived(at, far * 2 + 1 - y)
    copies[4].wait()
    for place in range(3):
        for part in range(1, 4):
            if place == 1 and part != 2:
                row_copy(part, place).wait()
            else:
                row_copy(part, place).wait_send()
            weight_copy(part, place).wait_send()
    for at in range(count):
        across(at, w).wait_send()
        both_ways(at, w, finish)
        if crosses_first(at):
            both_ways(at, other, finish)
        for far in range(1, line):
            pass_on(at, far, finish, False)
    for part in range(4):
        for copy in finished(part):
            copy.wait()
        if part > 0:
            send_sum(part).wait_send()
            send_normed(part).wait_send()
        if part in (1, 3):
            send_normed(part).wait_recv()
    keep_normed.wait()
    keep_rows.wait()
    keep_tables.wait()


def gather_call(line, qkv_s, out_s, ffn_s, down_s, rows, low_rows, tables, residual, scale, gain):
    low = jnp.bfloat16
    ndp, wide = qkv_s.shape[0], 2 * line
    rm, piece = qkv_s.shape[1], qkv_s.shape[2]
    seq, wq = rows.shape[0], D // ndp

    def shape(*dims, kind=low):
        return jax.ShapeDtypeStruct(dims, kind)

    outs = (
        shape(rm, ndp, wide, piece, qkv_s.shape[3]),
        shape(ndp, wide, piece, out_s.shape[2]),
        shape(rm, ndp, wide, piece, ffn_s.shape[3]),
        shape(down_s.shape[0], wide, piece, down_s.shape[2]),
        shape(ndp, seq, D),
        shape(ndp, seq, qkv_s.shape[3]),
        shape(ndp, seq, wq),
        shape(seq, D, kind=jnp.float32),
        shape(ndp, seq, D),
        shape(ndp, seq, D),
        shape(ndp, *tables.shape, kind=tables.dtype),
    )
    dma = pltpu.SemaphoreType.DMA
    whole = pl.BlockSpec(memory_space=pltpu.VMEM)
    args = (qkv_s, out_s, ffn_s, rows, low_rows, tables, down_s)
    count = 18
    return pl.pallas_call(
        functools.partial(gather_kernel, line, down_s.shape[0], ffn_s.shape[3] // 2),
        out_shape=outs,
        in_specs=[ANY] * len(args) + [whole, pl.BlockSpec(memory_space=pltpu.SMEM), whole],
        out_specs=[ANY] * 7 + [whole] + [ANY] * 3,
        scratch_shapes=[
            pltpu.VMEM((ndp, seq, D), low),
            pltpu.VMEM((ndp, *tables.shape), tables.dtype),
            pltpu.VMEM(outs[0].shape, low),
            pltpu.VMEM(outs[1].shape, low),
            pltpu.VMEM((ndp, seq, qkv_s.shape[3]), low),
            pltpu.VMEM((ndp, seq, wq), low),
            pltpu.VMEM((ndp, seq, D), low),
            pltpu.VMEM((ndp, seq, D), low),
            pltpu.VMEM((seq, D), low),
            dma((7,)),
            dma((6, 4)),
            dma((6, 4)),
        ]
        + [dma((count, wide))] * 4
        + [dma((13,)), dma((4,)), dma((4,)), dma((4,)), dma((4,))],
        compiler_params=pltpu.CompilerParams(
            collective_id=0, has_side_effects=True, vmem_limit_bytes=56 * 1024 * 1024
        ),
        name="gather_weights",
    )(*args, residual, scale, gain)


def scatter_kernel(line, half, *refs):
    (grad_ffn, normed_part, middle_in, cotangent, residual, w_out, w_qkv) = refs[:7]
    packed_in, attn_in, rows_in, tables_in, scale_ref, gains_ref = refs[7:13]
    outs, (input_grad, gain_parts) = refs[13:16], refs[16:18]
    crossed, lined, mine_ffn = refs[18:21], refs[21:24], refs[24]
    early, early_line, early_cross = refs[25:28]
    middle_v, late_v, sum_v, part_v, proj_v, wout_v, wqkv_v, wgrad_v, packed_v, tables_v, out_v, kv_v = refs[28:40]
    y_send, y_recv, load, up_sem, dn_sem, recv, dp_send, dp_recv, loc = refs[40:49]
    keep, two_send, two_recv, proj_send, proj_recv, one_send, one_recv = refs[49:]
    j, w = lax.axis_index("dp"), lax.axis_index("wide")
    z, y = w // 2, w % 2
    other = w + 1 - 2 * y
    greet(line, z, y, j, w)
    f32, low = jnp.float32, jnp.bfloat16
    window = 2

    chunks = [("early", 0, 0), ("early", 0, 1)]
    for part in range(1, 4):
        chunks += [("ffn", part, 0), ("ffn", part, 1)]
    for part in range(4):
        chunks += [("qkv", part, 0)]
    for part in range(4):
        chunks += [("out", part, 0)]
    count = len(chunks)
    names = ("qkv", "out", "ffn")

    def source(at, side):
        name, part, cut = chunks[at]
        if name == "qkv":
            return wgrad_v.at[:, flip(j, part), :, side]
        if name == "out":
            return wout_v.at[pl.ds(flip(j, part), 1), :, side]
        return grad_ffn.at[:, flip(j, part), :, side, :, cut * half : (cut + 1) * half]

    def held(refs, at):
        name, part, cut = chunks[at]
        ref = refs[names.index(name)]
        if name == "ffn":
            return ref.at[part - 1, :, :, :, cut * half : (cut + 1) * half]
        return ref.at[part]

    def own_rows(at):
        name, part, cut = chunks[at]
        if name == "ffn":
            return mine_ffn.at[(2 * part + cut) % (window + 2)]
        return source(at, y)

    def cross(at):
        return remote(
            source(at, 1 - y), held(crossed, at), y_send.at[at], y_recv.at[at], wide=other
        )

    def fetch(at):
        cut = chunks[at][2]
        if chunks[at][0] == "early":
            there = grad_ffn.at[:, j, :, :, :, cut * half : (cut + 1) * half]
            return pltpu.make_async_copy(there, early.at[cut], load.at[at])
        return pltpu.make_async_copy(source(at, y), own_rows(at), load.at[at])

    def fetches(at):
        return chunks[at][0] in ("early", "ffn")

    def cross_early(at):
        cut = chunks[at][2]
        return remote(
            early.at[cut, :, z, 1 - y], early_cross.at[cut], y_send.at[at], y_recv.at[at], wide=other
        )

    def moving(at, dest):
        if chunks[at][0] == "early":
            return early.at[chunks[at][2], :, dest]
        return held(crossed, at).at[:, dest]

    def landing(at, put):
        if chunks[at][0] == "early":
            return early_line.at[chunks[at][2], :, put]
        return held(lined, at).at[:, put]

    def up(at, dest, last):
        put = line if last else dest
        return remote(
            moving(at, dest), landing(at, put), up_sem.at[at, dest], recv.at[at, put], wide=w + 2
        )

    def dn(at, dest):
        return remote(
            moving(at, dest), landing(at, dest), dn_sem.at[at, dest], recv.at[at, dest], wide=w - 2
        )

    def arrived(at, put):
        there = landing(at, put)
        remote(there, there, dn_sem.at[at, 0], recv.at[at, put], wide=other).wait_recv()

    def add(at, dest, puts):
        name, part, cut = chunks[at]
        if name == "early":
            if not puts:
                return

            def rows(index):
                for side in range(2):
                    value = early[cut, index, dest, side].astype(f32)
                    for put in puts:
                        value = value + early_line[cut, index, put, side].astype(f32)
                    early[cut, index, dest, side] = value.astype(low)

            each(early.shape[1], rows)
            return
        here, own, line_in = held(crossed, at), own_rows(at), held(lined, at)

        def rows(index):
            value = here[index, dest].astype(f32) + own[index, dest].astype(f32)
            for put in puts:
                value = value + line_in[index, put].astype(f32)
            here[index, dest] = value.astype(low)

        each(here.shape[0], rows)

    def along(at, act):
        for far in range(line - 1, 0, -1):

            @pl.when(z >= far)
            def _():
                dest = z - far
                if act:

                    @pl.when(z < line - 1)
                    def _():
                        arrived(at, dest)
                        add(at, dest, (dest,))

                    @pl.when(z == line - 1)
                    def _():
                        add(at, dest, ())

                    dn(at, dest).start()
                else:
                    dn(at, dest).wait_send()

            @pl.when(z + far < line)
            def _():
                dest = z + far
                if act:

                    @pl.when(z > 0)
                    def _():
                        arrived(at, dest)
                        add(at, dest, (dest,))

                    @pl.when(z == 0)
                    def _():
                        add(at, dest, ())

                    up(at, dest, far == 1).start()
                else:
                    up(at, dest, far == 1).wait_send()

    def collect(at):
        @pl.when(z == 0)
        def _():
            arrived(at, z)
            add(at, z, (z,))

        @pl.when(z == line - 1)
        def _():
            arrived(at, line)
            add(at, z, (line,))

        @pl.when((z > 0) & (z < line - 1))
        def _():
            arrived(at, z)
            arrived(at, line)
            add(at, z, (z, line))

    def give(at):
        name, part, cut = chunks[at]
        rows = held(crossed, at).at[:, z]
        ref = outs[names.index(name)]
        if name == "out":
            target = ref.at[pl.ds(j, 1)]
        elif name == "qkv":
            target = ref.at[j]
        else:
            target = ref.at[j, :, :, cut * half : (cut + 1) * half]
        if part == 0:
            return pltpu.make_async_copy(rows, target, loc.at[at])
        return remote(rows, target, dp_send.at[at], dp_recv.at[at], dp=flip(j, part))

    def give_early(at):
        cut = chunks[at][2]
        target = outs[2].at[j, :, :, cut * half : (cut + 1) * half]
        return pltpu.make_async_copy(early_cross.at[cut], target, loc.at[at])

    def collect_and_give(at):
        collect(at)
        if chunks[at][0] == "early":
            cross_early(at).start()
        else:
            give(at).start()

    def finish_early(at):
        cut = chunks[at][2]
        cross_early(at).wait_recv()

        def rows(index):
            value = early_cross[cut, index].astype(f32) + early[cut, index, z, y].astype(f32)
            early_cross[cut, index] = value.astype(low)

        each(early.shape[1], rows)
        give_early(at).start()

    heads = out_v.shape[1] // HD
    seq = middle_v.shape[0]
    wide_rows = heads * HD
    loads = [
        pltpu.make_async_copy(middle_in, middle_v, keep.at[0]),
        pltpu.make_async_copy(cotangent, late_v, keep.at[1]),
        pltpu.make_async_copy(normed_part.at[j], part_v.at[0], keep.at[2]),
        pltpu.make_async_copy(normed_part.at[flip(j, 2)], part_v.at[2], keep.at[3]),
        pltpu.make_async_copy(w_out, wout_v, keep.at[4]),
        pltpu.make_async_copy(w_qkv, wqkv_v, keep.at[5]),
        pltpu.make_async_copy(packed_in, packed_v, keep.at[6]),
        pltpu.make_async_copy(tables_in, tables_v, keep.at[7]),
    ]
    load_rows = pltpu.make_async_copy(rows_in, part_v, keep.at[8])
    load_attn = [
        pltpu.make_async_copy(
            attn_in.at[n], late_v.at[:, n * wide_rows : (n + 1) * wide_rows], keep.at[9 + n]
        )
        for n in range(4)
    ]
    load_residual = pltpu.make_async_copy(residual, late_v, keep.at[13])
    keep_input = pltpu.make_async_copy(late_v, input_grad, keep.at[14])

    def send_two(part):
        block = part_v.at[2] if part == 2 else normed_part.at[flip(j, part)]
        peer = flip(j, 1 if part == 3 else part)
        return remote(block, sum_v.at[part - 1], two_send.at[part], two_recv.at[part], dp=peer)

    def send_one(part):
        peer = flip(j, 1 if part == 3 else part)
        return remote(
            part_v.at[part], sum_v.at[part - 1], one_send.at[part], one_recv.at[part], dp=peer
        )

    def send_proj(part):
        there = proj_v.at[flip(j, 2) if part == 3 else j]
        peer = flip(j, 1 if part == 3 else part)
        return remote(there, there, proj_send.at[part], proj_recv.at[part], dp=peer)

    def over_rows(step):
        each(seq // 32, lambda index: step(pl.ds(pl.multiple_of(index * 32, 32), 32)))

    def add_two():
        loads[3].wait()
        send_two(3).wait_recv()

        def rows(here):
            value = part_v[2, here, :].astype(f32) + sum_v[2, here, :].astype(f32)
            part_v[2, here, :] = value.astype(low)

        over_rows(rows)
        send_two(2).start()

    def norm_back(values, grads, gain, gain_row):
        rate = lax.rsqrt(jnp.mean(values * values, -1, keepdims=True) + norm_eps)
        scaled = grads * gain
        mean = jnp.mean(values * scaled, -1, keepdims=True)
        gain_parts[gain_row : gain_row + 1, :] += jnp.sum(grads * values * rate, 0, keepdims=True)
        return rate * scaled - values * rate * rate * rate * mean

    def second_norm():
        for at in (0, 1, 2):
            loads[at].wait()
        send_two(1).wait_recv()
        send_two(2).wait_recv()
        gain_parts[...] = jnp.zeros_like(gain_parts)
        scale = scale_ref[0, 0]

        def rows(here):
            grads = part_v[0, here, :].astype(f32)
            for part in (1, 2):
                grads = grads + sum_v[part - 1, here, :].astype(f32)
            value_grad = norm_back(middle_v[here, :], grads, gains_ref[1:2, :], 1)
            middle_grad = late_v[here, :].astype(f32) + value_grad
            middle_v[here, :] = middle_grad
            proj_v[j, here, :] = (scale * middle_grad).astype(low)

        over_rows(rows)
        send_proj(1).start()
        send_proj(2).start()
        send_two(2).wait_send()
        load_rows.start()
        for copy in load_attn:
            copy.start()

    def hand_on():
        send_proj(2).wait_recv()
        send_proj(3).start()

    def out_back(part):
        if part == 0:
            for at in (4, 5, 6, 7):
                loads[at].wait()
        elif part != 2:
            send_proj(part).wait_recv()
        weights = wout_v[...].reshape(wide_rows, D)
        value = lax.dot_general(
            proj_v[flip(j, part)], weights, (((1,), (1,)), ((), ())), preferred_element_type=f32
        )
        out_v[...] = value.astype(low)

    def turn_back(values, n):
        return values * tables_v[n, 0] - pltpu.roll(values, HD // 2, 1) * tables_v[n, 1]

    def attend_back(part, head):
        n = flip(j, part)
        own = slice(head * HD, (head + 1) * HD)
        query = packed_v[n, :, own]
        key = packed_v[n, :, wide_rows : wide_rows + HD]
        value = packed_v[n, :, wide_rows + HD :]
        grad = out_v[:, own]
        scores = lax.dot_general(
            query, key, (((1,), (1,)), ((), ())), preferred_element_type=f32
        ) * HD ** (-0.5)
        row = lax.broadcasted_iota(jnp.int32, (seq, seq), 0)
        column = lax.broadcasted_iota(jnp.int32, (seq, seq), 1)
        scores = jnp.where(row >= column, scores, masked_value)
        weight = jnp.exp(scores - jnp.max(scores, -1, keepdims=True))
        probs = weight / jnp.sum(weight, -1, keepdims=True)
        prob_grads = lax.dot_general(
            grad, value, (((1,), (1,)), ((), ())), preferred_element_type=f32
        )
        row_dot = jnp.sum(prob_grads * probs, -1, keepdims=True)
        score_low = (probs * (prob_grads - row_dot)).astype(low)
        query_grad = jnp.dot(score_low, key, preferred_element_type=f32) * HD ** (-0.5)
        key_grad = lax.dot_general(
            score_low, query, (((0,), (0,)), ((), ())), preferred_element_type=f32
        ) * HD ** (-0.5)
        value_grad = lax.dot_general(
            probs.astype(low), grad, (((0,), (0,)), ((), ())), preferred_element_type=f32
        )
        if head == 0:
            kv_v[0] = key_grad
            kv_v[1] = value_grad
        else:
            kv_v[0] += key_grad
            kv_v[1] += value_grad
        packed_v[n, :, own] = turn_back(query_grad, n).astype(low)
        if head == heads - 1:
            packed_v[n, :, wide_rows : wide_rows + HD] = turn_back(kv_v[0], n).astype(low)
            packed_v[n, :, wide_rows + HD :] = kv_v[1].astype(low)

    def out_grad(cut):
        if cut == 0:
            for copy in load_attn:
                copy.wait()
        columns = slice(cut * D // 4, (cut + 1) * D // 4)
        rows = jnp.concatenate(
            [late_v[:, n * wide_rows : (n + 1) * wide_rows] for n in range(4)], 0
        )
        grads = proj_v[:, :, columns].reshape(4 * seq, D // 4)
        value = lax.dot_general(rows, grads, (((0,), (0,)), ((), ())), preferred_element_type=f32)
        shape = wout_v.shape[:-1] + (D // 4,)
        wout_v[:, :, :, :, columns] = value.astype(low).reshape(shape)

    def qkv_grad(cut):
        if cut == 0:
            load_rows.wait()
            load_residual.start()
        columns = slice(cut * D // 4, (cut + 1) * D // 4)
        rows = part_v[:, :, columns].reshape(4 * seq, D // 4)
        grads = packed_v[...].reshape(4 * seq, packed_v.shape[2])
        value = lax.dot_general(rows, grads, (((0,), (0,)), ((), ())), preferred_element_type=f32)
        wgrad_v[cut] = value.astype(low).reshape(wgrad_v.shape[1:])

    def rows_back(part):
        n = flip(j, part)
        if part == 2:
            send_one(3).wait_recv()
        for cut in range(4):
            columns = slice(cut * D // 4, (cut + 1) * D // 4)
            weights = wqkv_v[cut].reshape(D // 4, packed_v.shape[2])
            value = lax.dot_general(
                packed_v[n], weights, (((1,), (1,)), ((), ())), preferred_element_type=f32
            )
            if part == 2:
                value = value + sum_v[2, :, columns].astype(f32)
            part_v[part, :, columns] = value.astype(low)
        if part > 0:
            send_one(part).start()

    def first_norm():
        load_residual.wait()
        for part in (1, 2):
            send_one(part).wait_recv()

        def rows(here):
            grads = part_v[0, here, :].astype(f32)
            for part in (1, 2):
                grads = grads + sum_v[part - 1, here, :].astype(f32)
            value_grad = norm_back(late_v[here, :].astype(f32), grads, gains_ref[0:1, :], 0)
            late_v[here, :] = (middle_v[here, :] + value_grad).astype(low)

        over_rows(rows)
        keep_input.start()

    def sequence(part):
        return [functools.partial(out_back, part)] + [
            functools.partial(attend_back, part, head) for head in range(heads)
        ]

    work = {
        1: [second_norm] + sequence(0),
        2: sequence(1) + [hand_on],
        3: sequence(3) + sequence(2),
        4: [functools.partial(out_grad, cut) for cut in range(4)]
        + [functools.partial(qkv_grad, cut) for cut in range(4)],
        7: [functools.partial(rows_back, 3)],
        8: [functools.partial(rows_back, 2)],
        9: [functools.partial(rows_back, 1)],
        10: [functools.partial(rows_back, 0)],
        12: [first_norm],
    }

    late = list(range(2, count))
    send_two(3).start()
    send_two(1).start()
    for at in range(2):
        fetch(at).start()
    for copy in loads:
        copy.start()

    def begin(at):
        if fetches(at):
            fetch(at).start()
        cross(at).start()

    for at in late[:window]:
        begin(at)
    add_two()
    for at in range(2):
        fetch(at).wait()
        along(at, True)
    for step, at in enumerate(late):
        pieces = work.get(step, [])
        cut = (len(pieces) + 1) // 2
        cross(at).wait_send()
        following = late[step + window] if step + window < len(late) else None
        if following is not None and step != 4:
            begin(following)
        cross(at).wait_recv()
        if fetches(at):
            fetch(at).wait()
        along(at, True)
        for piece in pieces[:cut]:
            piece()
        if step < 2:
            collect_and_give(step)
        if step >= 1:
            collect_and_give(late[step - 1])
        for piece in pieces[cut:]:
            piece()
        if step == 4:
            begin(following)
        if step in (3, 4):
            finish_early(step - 3)
    collect_and_give(late[-1])
    for at in range(count):
        along(at, False)
        if chunks[at][0] == "early":
            cross_early(at).wait_send()
            give_early(at).wait()
        else:
            give(at).wait()
    for part in range(1, 4):
        if part != 2:
            send_two(part).wait_send()
        send_proj(part).wait_send()
        send_one(part).wait_send()
    keep_input.wait()


def scatter_call(line, ffn, normed_part, middle, cotangent, residual, w_out, w_qkv, packed, attn, rows, tables, scale, gains):
    low = jnp.bfloat16
    rm, ndp, _, piece, wq = w_qkv.shape
    wf, wo = ffn.shape[4], w_out.shape[3]
    seq = middle.shape[0]
    ffn = ffn.reshape(rm, ndp, line, 2, piece, wf)
    w_out = w_out.reshape(ndp, line, 2, piece, wo)
    w_qkv = w_qkv.reshape(rm, ndp, line, 2, piece, wq)

    def shape(*dims, kind=low):
        return jax.ShapeDtypeStruct(dims, kind)

    outs = (
        shape(ndp, rm, piece, wq),
        shape(ndp, piece, wo),
        shape(ndp, rm, piece, wf),
        shape(seq, D),
        shape(2, D, kind=jnp.float32),
    )

    def held(places):
        return [
            pltpu.VMEM((ndp, rm, places, piece, wq), low),
            pltpu.VMEM((ndp, 1, places, piece, wo), low),
            pltpu.VMEM((ndp - 1, rm, places, piece, wf), low),
        ]

    dma = pltpu.SemaphoreType.DMA
    whole = pl.BlockSpec(memory_space=pltpu.VMEM)
    count = 16
    return pl.pallas_call(
        functools.partial(scatter_kernel, line, wf // 2),
        out_shape=outs,
        in_specs=[ANY] * 11 + [pl.BlockSpec(memory_space=pltpu.SMEM), whole],
        out_specs=[ANY] * 4 + [whole],
        scratch_shapes=held(line)
        + held(line + 1)
        + [
            pltpu.VMEM((4, rm, line, piece, wf // 2), low),
            pltpu.VMEM((2, rm, line, 2, piece, wf // 2), low),
            pltpu.VMEM((2, rm, line + 1, 2, piece, wf // 2), low),
            pltpu.VMEM((2, rm, piece, wf // 2), low),
            pltpu.VMEM((seq, D), jnp.float32),
            pltpu.VMEM((seq, D), low),
            pltpu.VMEM((3, seq, D), low),
            pltpu.VMEM((ndp, seq, D), low),
            pltpu.VMEM((ndp, seq, D), low),
            pltpu.VMEM(w_out.shape, low),
            pltpu.VMEM(w_qkv.shape, low),
            pltpu.VMEM(w_qkv.shape, low),
            pltpu.VMEM(packed.shape, low),
            pltpu.VMEM(tables.shape, tables.dtype),
            pltpu.VMEM((seq, attn.shape[2]), low),
            pltpu.VMEM((2, seq, HD), jnp.float32),
        ]
        + [dma((count,))] * 3
        + [dma((count, line)), dma((count, line)), dma((count, line + 1))]
        + [dma((count,))] * 3
        + [dma((15,))]
        + [dma((4,))] * 6,
        compiler_params=pltpu.CompilerParams(
            collective_id=1, has_side_effects=True, vmem_limit_bytes=60 * 1024 * 1024
        ),
        name="scatter_grads",
    )(ffn, normed_part, middle, cotangent, residual, w_out, w_qkv, packed, attn, rows, tables, scale, gains)


def gains_kernel(line, part_ref, total_ref, dp_parts, wide_parts, dp_send, dp_recv, wide_send, wide_recv):
    j, w = lax.axis_index("dp"), lax.axis_index("wide")
    wide = 2 * line
    barrier = pltpu.get_barrier_semaphore()
    for part in range(1, 4):
        pl.semaphore_signal(barrier, device_id={"dp": flip(j, part)}, device_id_type=MESH)
    for far in range(1, wide):
        pl.semaphore_signal(barrier, device_id={"wide": (w + far) % wide}, device_id_type=MESH)
    pl.semaphore_wait(barrier, 3 + wide - 1)
    copies = [
        remote(part_ref, dp_parts.at[j], dp_send.at[part], dp_recv.at[part], dp=flip(j, part))
        for part in range(1, 4)
    ]
    for copy in copies:
        copy.start()
    dp_parts[j] = part_ref[...]
    for copy in copies:
        copy.wait()
    value = dp_parts[0]
    for rank in range(1, 4):
        value = value + dp_parts[rank]
    wide_parts[w] = value
    copies = [
        remote(
            wide_parts.at[w],
            wide_parts.at[w],
            wide_send.at[far],
            wide_recv.at[far],
            wide=(w + far) % wide,
        )
        for far in range(1, wide)
    ]
    for copy in copies:
        copy.start()
    for copy in copies:
        copy.wait()
    value = wide_parts[0]
    for rank in range(1, wide):
        value = value + wide_parts[rank]
    total_ref[...] = value


def gains_call(line, parts):
    dma = pltpu.SemaphoreType.DMA
    whole = pl.BlockSpec(memory_space=pltpu.VMEM)
    return pl.pallas_call(
        functools.partial(gains_kernel, line),
        out_shape=jax.ShapeDtypeStruct(parts.shape, jnp.float32),
        in_specs=[whole],
        out_specs=whole,
        scratch_shapes=[
            pltpu.VMEM((4, *parts.shape), jnp.float32),
            pltpu.VMEM((2 * line, *parts.shape), jnp.float32),
            dma((4,)),
            dma((4,)),
            dma((2 * line,)),
            dma((2 * line,)),
        ],
        compiler_params=pltpu.CompilerParams(collective_id=2, has_side_effects=True),
        name="sum_gains",
    )(parts)


def attention(tokens, ndp, heads, qkv_rows, tables):
    low = jnp.bfloat16
    seq_len = tokens // ndp
    cosine, sine = tables[:, 0].reshape(tokens, 1, HD), tables[:, 1].reshape(tokens, 1, HD)
    turned = qkv_rows[:, : (heads + 1) * HD].reshape(tokens, heads + 1, HD)
    turned = (turned * cosine + jnp.roll(turned, HD // 2, -1) * sine).astype(low)
    query_rows = turned[:, :heads].reshape(ndp, seq_len, heads, HD)
    key_rows = turned[:, heads].reshape(ndp, seq_len, HD)
    value_rows = qkv_rows[:, (heads + 1) * HD :].astype(low).reshape(ndp, seq_len, HD)
    probs_low = attention_probs(query_rows, key_rows).astype(low)
    out_low = jnp.einsum(
        "ngst,ntd->nsgd", probs_low, value_rows, preferred_element_type=jnp.float32
    ).astype(low)
    packed = jnp.concatenate(
        [turned.reshape(ndp, seq_len, (heads + 1) * HD), value_rows], -1
    )
    return packed, out_low.reshape(ndp, seq_len, heads * HD)


def attention_probs(query_rows, key_rows):
    seq_len = query_rows.shape[1]
    causal = jnp.arange(seq_len)[:, None] >= jnp.arange(seq_len)[None, :]
    scores = jnp.einsum(
        "nsgd,ntd->ngst", query_rows, key_rows, preferred_element_type=jnp.float32
    ) * HD ** (-0.5)
    scores = jnp.where(causal, scores, masked_value)
    row_top = jnp.max(scores, -1, keepdims=True)
    exp_scores = jnp.exp(scores - row_top)
    return exp_scores / jnp.sum(exp_scores, -1, keepdims=True)


def gather_weights(qkv_s, out_s, ffn_s, down_s, rows, low_rows, tables, residual, scale, gain):
    ndp, nwide = lax.axis_size("dp"), lax.axis_size("wide")
    if ndp == 4 and nwide == 8 and qkv_s.shape[2] % 16 == 0:
        return gather_call(
            nwide // 2, qkv_s, out_s, ffn_s, down_s, rows, low_rows, tables, residual, scale, gain
        )

    def spread(values):
        moved = lax.all_to_all(values, "dp", split_axis=0, concat_axis=0, tiled=True)
        return lax.all_gather(moved, "wide", axis=0)

    seq_len = rows.shape[0]
    tokens = ndp * seq_len
    heads = HEADS // ndp
    w_qkv = spread(qkv_s).transpose(2, 1, 0, 3, 4)
    w_out = spread(out_s).transpose(1, 0, 2, 3)
    w_ffn = spread(ffn_s).transpose(2, 1, 0, 3, 4)
    normed_one = lax.all_gather(rows, "dp", axis=0)
    all_tables = lax.all_gather(tables, "dp", axis=0)
    packed, out_low = attention(
        tokens,
        ndp,
        heads,
        dot(normed_one.reshape(tokens, D), w_qkv.reshape(D, -1)),
        all_tables,
    )
    part = dot(out_low.reshape(tokens, heads * HD), w_out.reshape(heads * HD, D))
    middle = residual.astype(jnp.float32) + scale * total(part)
    normed_two = (middle * norm_rate(middle) * gain).astype(jnp.bfloat16)
    return (
        w_qkv,
        w_out,
        w_ffn,
        lax.all_gather(down_s, "wide", axis=1),
        lax.all_gather(low_rows, "dp", axis=0),
        packed,
        out_low,
        middle,
        lax.all_gather(normed_two, "dp", axis=0),
        normed_one,
        all_tables,
    )


def scatter_grads(
    ffn, normed_part, middle, cotangent, residual, w_out, w_qkv, packed, attn, rows, tables, scale, gains
):
    ndp, nwide = lax.axis_size("dp"), lax.axis_size("wide")
    if ndp == 4 and nwide == 8 and ffn.shape[3] % 16 == 0:
        return scatter_call(
            nwide // 2, ffn, normed_part, middle, cotangent, residual,
            w_out, w_qkv, packed, attn, rows, tables, scale, gains,
        )
    low = jnp.bfloat16
    _, seq_len, width = packed.shape
    tokens = ndp * seq_len
    heads = HEADS // ndp
    wq = heads * HD
    score_scale = HD ** (-0.5)
    query_rows = packed[..., :wq].reshape(ndp, seq_len, heads, HD)
    key_rows = packed[..., wq : wq + HD]
    value_rows = packed[..., wq + HD :]
    normed_grad = total(normed_part.reshape(tokens, D))
    middle_local, gain_two = norm_backward(middle, norm_rate(middle), gains[1], normed_grad)
    middle_grad = cotangent.astype(jnp.float32) + middle_local
    proj_low = share((scale * middle_grad).astype(low))
    probs_float = attention_probs(query_rows, key_rows)
    attn_grad = dot_back(proj_low, w_out.reshape(wq, D)).astype(low)
    attn_grad = attn_grad.reshape(ndp, seq_len, heads, HD)
    prob_grads = jnp.einsum(
        "nsgd,ntd->ngst", attn_grad, value_rows, preferred_element_type=jnp.float32
    )
    row_dot = jnp.sum(prob_grads * probs_float, -1, keepdims=True)
    score_low = (probs_float * (prob_grads - row_dot)).astype(low)
    query_grad = (
        jnp.einsum("ngst,ntd->nsgd", score_low, key_rows, preferred_element_type=jnp.float32)
        * score_scale
    )
    key_grad = (
        jnp.einsum("ngst,nsgd->ntd", score_low, query_rows, preferred_element_type=jnp.float32)
        * score_scale
    )
    value_grad = jnp.einsum(
        "ngst,nsgd->ntd",
        probs_float.astype(low),
        attn_grad,
        preferred_element_type=jnp.float32,
    )
    turned = jnp.concatenate([query_grad.reshape(ndp, seq_len, wq), key_grad], -1)
    turned = turned.reshape(tokens, heads + 1, HD)
    cosine = tables[:, 0].reshape(tokens, 1, HD)
    sine = tables[:, 1].reshape(tokens, 1, HD)
    turned = (turned * cosine - jnp.roll(turned, HD // 2, -1) * sine).astype(low)
    qkv_low = jnp.concatenate(
        [turned.reshape(tokens, wq + HD), value_grad.reshape(tokens, HD).astype(low)], 1
    )
    normed_grad = total(dot_back(qkv_low, w_qkv.reshape(D, width)))
    source = residual.astype(jnp.float32)
    input_local, gain_one = norm_backward(source, norm_rate(source), gains[0], normed_grad)

    def collect(values):
        moved = lax.psum_scatter(values, "wide", scatter_dimension=0, tiled=False)
        return lax.all_to_all(moved, "dp", split_axis=0, concat_axis=0, tiled=True)

    grad_qkv = dot_grad(rows.reshape(tokens, D), qkv_low).astype(low).reshape(w_qkv.shape)
    grad_out = dot_grad(attn.reshape(tokens, wq), proj_low).astype(low).reshape(w_out.shape)
    return (
        collect(grad_qkv.transpose(2, 1, 0, 3, 4)),
        collect(grad_out.transpose(1, 0, 2, 3)),
        collect(ffn.transpose(2, 1, 0, 3, 4)),
        (middle_grad + input_local).astype(low),
        jnp.stack([gain_one, gain_two]),
    )


def sum_gains(parts):
    ndp, nwide = lax.axis_size("dp"), lax.axis_size("wide")
    if ndp == 4 and nwide == 8:
        return gains_call(nwide // 2, parts)
    return lax.psum(parts, ("dp", "wide"))


def unfold_rows(rows_ref, flat_ref, piece):
    count = rows_ref.shape[0]
    for first in range(0, count, 8):
        size = min(8, count - first)
        for row in range(piece):
            for group in range(B // 128):
                start = row * B + group * 128
                flat_ref[group, pl.ds(first * piece + row, size, stride=piece), :] = rows_ref[
                    first : first + size, start : start + 128
                ]


def block_places(rm, ndp, rf, part):
    places = []
    for i in range(rm):
        for c in range(ndp):
            places.append((i * ndp + c, 0, 0, (c, i), 0, B))
    for i in range(rm):
        for c in range(ndp):
            places.append((rm * rm + i, c * part, 0, (c, i), B, part))
            places.append((rm * rm + rm + i, c * part, 0, (c, i), B + part, part))
    first = rm * rm + 2 * rm
    for c in range(ndp):
        for i in range(rm):
            places.append((first + c * rm + i, 0, 1, (c,), i * B, B))
    first = first + rm * rm
    for i in range(rm):
        for b in range(rf):
            for c in range(ndp):
                for side in range(2):
                    block = first + side * rm * rf + i * rf + b
                    places.append((block, c * part, 2, (c, i), (side * rf + b) * part, part))
    first = first + 2 * rm * rf
    for b in range(rf):
        for i in range(rm):
            places.append((first + b * rm + i, 0, 3, (b,), i * B, B))
    return places


def pack_kernel(places, piece, rows_ref, *refs):
    pieces, flat_ref = refs[:4], refs[4]
    unfold_rows(rows_ref, flat_ref, piece)
    for block, column, array, lead, start, width in places:
        for offset in range(0, width, 128):
            value = flat_ref[(column + offset) // 128, block * piece : (block + 1) * piece, :]
            there = slice(start + offset, start + offset + 128)
            pieces[array][(*lead, slice(None), there)] = value.astype(jnp.bfloat16)


def slots_kernel(places, piece, slot_ref, *refs):
    pieces, send_ref, blocks_ref = refs[:4], refs[4], refs[5]
    for block, column, array, lead, start, width in places:
        value = pieces[array][(*lead, slice(None), slice(start, start + width))]
        blocks_ref[block, :, column : column + width] = value
    each_slot = send_ref.shape[1]

    def device(index, carry):
        for slot in range(each_slot):
            block = slot_ref[index * each_slot + slot]
            value = blocks_ref[jnp.maximum(block, 0)]
            send_ref[index, slot] = jnp.where(block >= 0, value, jnp.zeros_like(value))
        return carry

    lax.fori_loop(0, send_ref.shape[0], device, 0)


def precondition_kernel(scale_ref, grad_ref, left_ref, right_ref, step_ref):
    low, f32 = jnp.bfloat16, jnp.float32
    scale = scale_ref[pl.program_id(0)]
    grad = grad_ref[:, 0].reshape(B, B)
    value = jnp.dot(left_ref[0].astype(low), grad, preferred_element_type=f32)
    value = jnp.dot(value.astype(low), right_ref[0].astype(low), preferred_element_type=f32)
    rate = lax.rsqrt(jnp.mean(value * value, keepdims=True) + scale_eps)
    value = value * (weight_rate * scale * rate)
    step_ref[:, 0] = value.astype(low).reshape(step_ref.shape[0], step_ref.shape[2], B)


def update_kernel(piece, slot_ref, steps_ref, master_ref, out_ref, flat_ref):
    each_slot = steps_ref.shape[1]
    size = master_ref.shape[0]
    last = slot_ref.shape[0] - 1
    for index in range(size):
        slot = slot_ref[jnp.minimum(pl.program_id(0) * size + index, last)]
        value = steps_ref[slot // each_slot, slot % each_slot].astype(jnp.float32)
        for group in range(B // 128):
            flat_ref[group, index * piece : (index + 1) * piece, :] = value[
                :, group * 128 : (group + 1) * 128
            ]
    for row in range(piece):
        for group in range(B // 128):
            step = flat_ref[group, pl.ds(row, size, stride=piece), :]
            start = row * B + group * 128
            columns = slice(start, start + 128)
            out_ref[:, columns] = (1.0 - weight_decay) * master_ref[:, columns] - step


def vmem_call(kernel, outs, args, scratch=(), prefetch=0, name=None):
    def whole(array):
        return pl.BlockSpec(array.shape, lambda step: (0,) * len(array.shape))

    small = pl.BlockSpec(memory_space=pltpu.SMEM)
    return pl.pallas_call(
        kernel,
        out_shape=[pltpu.HBM(out.shape, out.dtype) for out in outs],
        grid=(1,),
        in_specs=[small] * prefetch + [whole(arg) for arg in args[prefetch:]],
        out_specs=[whole(out) for out in outs],
        scratch_shapes=list(scratch),
        compiler_params=pltpu.CompilerParams(vmem_limit_bytes=60 * 1024 * 1024),
        name=name,
    )(*args)


def pack_call(rows, ndp):
    rm, rf, part, piece = D // B, FF // B, B // ndp, rows.shape[1] // B
    low = jnp.bfloat16
    outs = (
        jax.ShapeDtypeStruct((ndp, rm, piece, B + 2 * part), low),
        jax.ShapeDtypeStruct((ndp, piece, D), low),
        jax.ShapeDtypeStruct((ndp, rm, piece, 2 * rf * part), low),
        jax.ShapeDtypeStruct((rf, piece, D), low),
    )
    return vmem_call(
        functools.partial(pack_kernel, block_places(rm, ndp, rf, part), piece),
        outs,
        (rows,),
        [pltpu.VMEM((B // 128, NBLK * piece, 128), jnp.float32)],
        name="pack",
    )


def slots_call(slot_block, pieces, devices):
    ndp, rm, piece, _ = pieces[0].shape
    rf = pieces[3].shape[0]
    low = jnp.bfloat16
    outs = (
        jax.ShapeDtypeStruct((devices, slot_block.shape[0] // devices, piece, B), low),
        jax.ShapeDtypeStruct((NBLK, piece, B), low),
    )
    return vmem_call(
        functools.partial(slots_kernel, block_places(rm, ndp, rf, B // ndp), piece),
        outs,
        (slot_block, *pieces),
        prefetch=1,
        name="to_slots",
    )


def precondition_call(scale, owned, left, right):
    devices, slots, piece, _ = owned.shape
    block = pl.BlockSpec((devices, 1, piece, B), lambda n: (0, n, 0, 0))
    square = pl.BlockSpec((1, B, B), lambda n: (n, 0, 0))
    return pl.pallas_call(
        precondition_kernel,
        out_shape=pltpu.HBM(owned.shape, jnp.bfloat16),
        grid=(slots,),
        in_specs=[pl.BlockSpec(memory_space=pltpu.SMEM), block, square, square],
        out_specs=block,
        compiler_params=pltpu.CompilerParams(vmem_limit_bytes=48 * 1024 * 1024),
        name="precondition",
    )(scale, owned, left, right)


def update_call(block_slot, returned, master):
    count, width = master.shape
    size = 16
    rows = pl.BlockSpec((size, width), lambda step: (step, 0))
    return pl.pallas_call(
        functools.partial(update_kernel, width // B),
        out_shape=jax.ShapeDtypeStruct(master.shape, jnp.float32),
        grid=(pl.cdiv(count, size),),
        in_specs=[
            pl.BlockSpec(memory_space=pltpu.SMEM),
            pl.BlockSpec(memory_space=pltpu.VMEM),
            rows,
        ],
        out_specs=rows,
        scratch_shapes=[pltpu.VMEM((B // 128, size * width // B, 128), jnp.float32)],
        compiler_params=pltpu.CompilerParams(vmem_limit_bytes=48 * 1024 * 1024),
        name="update",
    )(block_slot, returned, master)


def pack(master_weights, ndp):
    low = jnp.bfloat16
    piece = master_weights.shape[1] // B
    if ndp == 4 and piece % 16 == 0:
        return pack_call(master_weights, ndp)
    rm, rf, part = D // B, FF // B, B // ndp
    first_key = rm * rm
    first_value = first_key + rm
    first_out = first_value + rm
    first_gate = first_out + rm * rm
    first_up = first_gate + rm * rf
    first_down = first_up + rm * rf
    mine = master_weights.astype(low).reshape(NBLK, piece, B)

    def cut_columns(first, blocks):
        own = mine[first : first + rm * blocks].reshape(rm, blocks, piece, ndp, part)
        return own.transpose(3, 0, 2, 1, 4).reshape(ndp, rm, piece, blocks * part)

    qkv_s = jnp.concatenate(
        [
            mine[:first_key].reshape(rm, ndp, piece, B).transpose(1, 0, 2, 3),
            cut_columns(first_key, 1),
            cut_columns(first_value, 1),
        ],
        -1,
    )
    out_s = (
        mine[first_out:first_gate].reshape(ndp, rm, piece, B).transpose(0, 2, 1, 3)
    ).reshape(ndp, piece, D)
    ffn_s = jnp.concatenate([cut_columns(first_gate, rf), cut_columns(first_up, rf)], -1)
    down_s = mine[first_down:].reshape(rf, rm, piece, B).transpose(0, 2, 1, 3)
    down_s = down_s.reshape(rf, piece, D)
    return qkv_s, out_s, ffn_s, down_s


def to_slots(slot_block, pieces, devices):
    ndp, rm, piece, _ = pieces[0].shape
    if ndp == 4 and piece % 16 == 0:
        return slots_call(slot_block, pieces, devices)
    grad_qkv, grad_out, grad_ffn, grad_down = pieces
    low = jnp.bfloat16
    rf = grad_down.shape[0]
    part = B // ndp
    wq = B

    def join_columns(cut, blocks):
        own = cut.reshape(ndp, rm, piece, blocks, part).transpose(1, 3, 2, 0, 4)
        return own.reshape(rm * blocks, piece, B)

    grad_rows = jnp.concatenate(
        [
            grad_qkv[..., :wq].transpose(1, 0, 2, 3).reshape(rm * ndp, piece, B),
            join_columns(grad_qkv[..., wq : wq + part], 1),
            join_columns(grad_qkv[..., wq + part :], 1),
            grad_out.reshape(ndp, piece, rm, B).transpose(0, 2, 1, 3).reshape(ndp * rm, piece, B),
            join_columns(grad_ffn[..., : rf * part], rf),
            join_columns(grad_ffn[..., rf * part :], rf),
            grad_down.reshape(rf, piece, rm, B).transpose(0, 2, 1, 3).reshape(rf * rm, piece, B),
        ],
        0,
    )
    send_rows = jnp.where(
        (slot_block >= 0)[:, None, None],
        grad_rows[jnp.maximum(slot_block, 0)],
        jnp.zeros((), low),
    )
    return send_rows.reshape(devices, -1, piece, B), grad_rows


def precondition(scale, owned, left, right):
    low = jnp.bfloat16
    devices, slots, piece, _ = owned.shape
    if piece % 16 == 0:
        return precondition_call(scale, owned, left, right)
    blocks = owned.transpose(1, 0, 2, 3).reshape(slots, B, B)
    value = jnp.einsum("nij,njk->nik", left.astype(low), blocks, preferred_element_type=jnp.float32)
    value = jnp.einsum(
        "nij,njk->nik", value.astype(low), right.astype(low), preferred_element_type=jnp.float32
    )
    rate = lax.rsqrt(jnp.mean(value * value, axis=(1, 2), keepdims=True) + scale_eps)
    steps = weight_rate * scale[:, None, None] * value * rate
    return steps.astype(low).reshape(slots, devices, piece, B).transpose(1, 0, 2, 3)


def update(block_slot, returned, master_weights):
    devices, slots, piece, _ = returned.shape
    if piece % 16 == 0:
        return update_call(block_slot, returned, master_weights)
    steps = returned.reshape(devices * slots, piece, B)[block_slot].astype(jnp.float32)
    return (1.0 - weight_decay) * master_weights - steps.reshape(NBLK, piece * B)


def local(
    inputs,
    cotangent,
    keep_mask,
    positions,
    master_weights,
    gains,
    gain_moments,
    block_slot,
    stat_left,
    stat_right,
    root_left,
    root_right,
):
    low = jnp.bfloat16
    ndp = lax.axis_size("dp")
    nwide = lax.axis_size("wide")
    rm = D // B
    rf = FF // B
    seq_len = inputs.shape[1]
    tokens = ndp * seq_len
    slot_dev = stat_left.shape[0]
    slots_all = slot_dev * ndp * nwide
    piece = master_weights.shape[1] // B
    part = B // ndp

    residual = inputs[0].astype(jnp.float32)
    branch_scale = keep_mask[0].astype(jnp.float32) / keep_rate()
    out_grad_f = cotangent[0].astype(jnp.float32)
    rate_one = norm_rate(residual)

    qkv_s, out_s, ffn_s, down_s = pack(master_weights, ndp)
    cosine_table, sine_table = rope_tables(positions[0])
    signs = jnp.where(jnp.arange(HD) < HD // 2, -1.0, 1.0)
    (
        w_qkv,
        w_out,
        w_ffn,
        w_down,
        down_low,
        packed,
        out_low,
        middle,
        normed_two,
        normed_one,
        all_tables,
    ) = gather_weights(
        qkv_s,
        out_s,
        ffn_s,
        down_s,
        (residual * rate_one * gains[0]).astype(low),
        (branch_scale * out_grad_f).astype(low),
        jnp.stack([cosine_table, sine_table * signs]),
        inputs[0],
        branch_scale.reshape(1, 1),
        gains[1:],
    )
    w_ffn = w_ffn.reshape(D, 2 * rf * part)
    w_down = w_down.reshape(rf * part, D)
    normed_two = normed_two.reshape(tokens, D)
    down_low = down_low.reshape(tokens, D)

    ffn_rows = dot(normed_two, w_ffn)
    gate_rows, up_rows = ffn_rows[:, : rf * part], ffn_rows[:, rf * part :]
    sigmoid_gate = jax.nn.sigmoid(gate_rows)
    hidden = (gate_rows * sigmoid_gate * up_rows).astype(low)
    down_part = dot_grad(hidden, down_low).astype(low).reshape(rf, nwide * piece, D)
    down_part, w_down_back = lax.optimization_barrier((down_part, w_down))
    grad_down = lax.psum_scatter(down_part, "wide", scatter_dimension=1, tiled=True)
    hidden_grad = dot_back(down_low, w_down_back)
    gate_low = (
        hidden_grad * up_rows * sigmoid_gate * (1.0 + gate_rows * (1.0 - sigmoid_gate))
    ).astype(low)
    up_low = (hidden_grad * gate_rows * sigmoid_gate).astype(low)
    ffn_low = jnp.concatenate([gate_low, up_low], 1)
    result = middle + branch_scale * total(dot(hidden, w_down))
    output = result.astype(low)[None]
    grad_qkv, grad_out, grad_ffn, input_grad, gain_parts = scatter_grads(
        dot_grad(normed_two, ffn_low).astype(low).reshape(rm, ndp, nwide, piece, 2 * rf * part),
        dot_back(ffn_low, w_ffn).astype(low).reshape(ndp, seq_len, D),
        middle,
        cotangent[0],
        inputs[0],
        w_out,
        w_qkv,
        packed,
        out_low,
        normed_one,
        all_tables,
        branch_scale.reshape(1, 1),
        gains,
    )
    input_grad = input_grad[None]
    gain_grads = sum_gains(gain_parts)
    new_gain_moments = stat_decay * gain_moments + (1.0 - stat_decay) * gain_grads * gain_grads
    new_gains = gains - gain_rate * gain_grads / (jnp.sqrt(new_gain_moments) + adam_eps)

    slot_block = jnp.full((slots_all,), -1, jnp.int32).at[block_slot].set(jnp.arange(NBLK))
    send_rows, grad_rows = to_slots(
        slot_block, (grad_qkv, grad_out, grad_ffn, grad_down), ndp * nwide
    )
    grad_local = grad_rows.reshape(NBLK, piece * B).astype(jnp.float32)
    owned = lax.all_to_all(send_rows, ("dp", "wide"), split_axis=0, concat_axis=0, tiled=True)
    own_blocks = lax.dynamic_slice_in_dim(
        slot_block, lax.axis_index(("dp", "wide")) * slot_dev, slot_dev
    )
    own_scale = jnp.where(own_blocks >= 0, block_scale(jnp.maximum(own_blocks, 0)), 0.0)
    steps_local = precondition(own_scale, owned, root_left, root_right)
    steps_local, gain_grads = lax.optimization_barrier((steps_local, gain_grads))
    returned = lax.all_to_all(steps_local, ("dp", "wide"), split_axis=0, concat_axis=0, tiled=True)
    blocks = owned.transpose(1, 0, 2, 3).reshape(slot_dev, B, B)
    new_left = stat_decay * stat_left + (1.0 - stat_decay) * jnp.einsum(
        "nij,nkj->nik", blocks, blocks, preferred_element_type=jnp.float32
    )
    new_right = stat_decay * stat_right + (1.0 - stat_decay) * jnp.einsum(
        "nji,njk->nik", blocks, blocks, preferred_element_type=jnp.float32
    )
    new_weights = update(block_slot, returned, master_weights)
    return (
        output,
        input_grad,
        grad_local,
        new_left,
        new_right,
        new_weights,
        gain_grads,
        new_gain_moments,
        new_gains,
    )


def solution(mesh):
    placed = (
        P(("dp", "wide"), None, None),
        P(("dp", "wide"), None, None),
        P(("dp", "wide")),
        P(("dp", "wide"), None),
        P(None, ("dp", "wide")),
        P(),
        P(),
        P(),
        P(("dp", "wide"), None, None),
        P(("dp", "wide"), None, None),
        P(("dp", "wide"), None, None),
        P(("dp", "wide"), None, None),
    )
    return jax.shard_map(
        local,
        mesh=mesh,
        in_specs=placed,
        out_specs=(
            P(("dp", "wide"), None, None),
            P(("dp", "wide"), None, None),
            P(None, ("dp", "wide")),
            P(("dp", "wide"), None, None),
            P(("dp", "wide"), None, None),
            P(None, ("dp", "wide")),
            P(),
            P(),
            P(),
        ),
        check_vma=False,
    )
```
